32 devices in a mesh: section: 2 (over y), dp: 16 (over z, x, core).
Axes of the slice: x: 2, y: 2, z: 4, core: 2. Of those that a mesh axis runs over, the one named last changes fastest.
Arguments:
- token_rows: bfloat16 [2, 8192, 512], P('section', 'dp'), may hold values from -6 to 6
- lengths: int32 [16, 2, 8], P('dp'), may hold values from 1 to 100, 512 in all within a row
- self_qkv: bfloat16 [2, 512, 1536], P('section'), may hold values from -0.25 to 0.25
- self_out: bfloat16 [2, 512, 512], P('section'), may hold values from -1 to 1
- ffn_in: bfloat16 [2, 512, 2048], P('section'), may hold values from -0.25 to 0.25
- ffn_in_bias: bfloat16 [2, 2048], P('section'), may hold values from -3 to 3
- ffn_out: bfloat16 [2, 2048, 512], P('section'), may hold values from -0.125 to 0.125
- ffn_out_bias: bfloat16 [2, 512], P('section'), may hold values from -3 to 3
- norm_gain: bfloat16 [2, 2, 512], P('section'), may hold values from 0.25 to 1.75
- norm_bias: bfloat16 [2, 2, 512], P('section'), may hold values from -3 to 3
- cross_weights: bfloat16 [2, 512, 1024], P('section')
- cross_gain: bfloat16 [512], replicated, may hold values from 0.25 to 1.75
- cross_bias: bfloat16 [512], replicated, may hold values from -3 to 3
- output_grad: bfloat16 [8192, 512], P('dp'), may hold values from -6 to 6
Outputs:
- layer_rows: bfloat16 [2, 8192, 512], P('section', 'dp')
- rows_grad: float32 [2, 8192, 512], P('section', 'dp')
- self_qkv_grad: float32 [2, 512, 1536], P('section')
- self_out_grad: float32 [2, 512, 512], P('section')
- ffn_in_grad: float32 [2, 512, 2048], P('section')
- ffn_in_bias_grad: float32 [2, 2048], P('section')
- ffn_out_grad: float32 [2, 2048, 512], P('section')
- ffn_out_bias_grad: float32 [2, 512], P('section')
- norm_gain_grad: float32 [2, 2, 512], P('section')
- norm_bias_grad: float32 [2, 2, 512], P('section')
- cross_weights_grad: float32 [2, 512, 1024], P('section')
- cross_gain_grad: float32 [512], replicated
- cross_bias_grad: float32 [512], replicated
The draws below stay inside these ranges and needn't reach their ends.
Inputs may be any that keep to these rules, and one draw needn't show every extreme that they name: Each packed row has 8 source and 8 target sentences; source sentence j and target sentence j form a pair; each side's lengths sum to 512 and the longest is 100.
All inputs are finite; a program needn't handle non-finite values.
Results may differ from the reference program's by a relative error of at most 0.02.
Values may be sent and summed in bfloat16 or wider, within the bound.
No kernel may reach another device: no remote copies, remote signals or barrier semaphores. Data moves between devices by JAX's collectives and lax.ppermute only.
A program may use at most 192 MiB of HBM per device.

```python
import math
import jax
import jax.numpy as jnp
import numpy as np
from jax import lax

D = 512
HEADS = 8
FF = 2048
HEAD_DIM = 64
ROW_LEN = 512
SENT_MAX = 100
SENTS = 8
REPEATS = 2
ROWS = 16
TOKENS = 8192


def draw_cross_weights(key, part):
    key = jax.random.fold_in(key, 11)
    sample = jax.random.truncated_normal(key, -4.0, 4.0, (2, D, 2 * D), jnp.float32)
    halves = jnp.arange(2)[:, None, None]
    columns = jnp.arange(2 * D)[None, None, :]
    widened = (halves == 1) & (columns >= D)
    scales = jnp.where(widened, (D // 16) ** (-0.5), D ** (-0.5))
    return (sample * scales).astype(jnp.bfloat16)


def shard_levels(rng, dims, pieces, smallest, high):
    factor_of = 1.0
    for dim, shards_of in pieces:
        heights = jax.random.uniform(jax.random.fold_in(jax.random.fold_in(rng, 6), dim), (shards_of,), jnp.float32, smallest / len(pieces), high / len(pieces))
        factor_of = factor_of * jnp.repeat(jnp.exp(heights), dims[dim] // shards_of).reshape((-1,) + (1,) * (len(dims) - 1 - dim))
    return factor_of


def length_profile(amount, total, bound, skew):
    weights = [(1 << 20) // math.isqrt(standing ** skew) + 1 for standing in range(2, amount + 1)]
    rest, given = total - bound - (amount - 1), [1] * (amount - 1)
    while rest > 0:
        free = [i for i in range(amount - 1) if given[i] < bound]
        mass, budget = sum([weights[i] for i in free]), rest
        for i in free:
            extra = min(bound - given[i], max(1, budget * weights[i] // mass), rest)
            given[i] = given[i] + extra
            rest = rest - extra
    return np.array([bound] + given)


def ragged(rng, count, total, bound, slope):
    if count == 2:
        one = jax.random.randint(rng, (), max(1, total - bound), min(bound, total - 1) + 1)
        return jnp.stack([one, total - one])
    sizes = jnp.asarray(length_profile(count, total, bound, slope), jnp.int32)
    couples = (count - 1) // 2
    source_of, taker = sizes[1:1 + 2 * couples:2], sizes[2:2 + 2 * couples:2]
    room = jnp.minimum(source_of - 1, bound - taker)
    shifted = jax.random.randint(jax.random.fold_in(rng, 1), (couples,), 0, 1 << 20) % (room + 1)
    sizes = sizes.at[1:1 + 2 * couples:2].set(source_of - shifted).at[2:2 + 2 * couples:2].set(taker + shifted)
    return sizes[jax.random.permutation(jax.random.fold_in(rng, 2), count)]


def scatter_about(stream_key, shape, scale, bound, cuts=(), kind=jnp.bfloat16):
    result = jax.random.normal(stream_key, shape, jnp.float32) * scale
    if len(cuts) > 0:
        result = shard_levels(stream_key, shape, cuts, -0.22, 0.18) * result
    return jnp.clip(result, min=-bound, max=bound).astype(kind)


def setup_inputs(seed: int = 0) -> dict:
    keys = jax.random.split(jax.random.key(seed), 15)
    token_rows = scatter_about(keys[0], (2, TOKENS, D), 1.0, 6.0, ((0, 2), (1, 16)))
    lengths = jax.vmap(lambda own: ragged(own, SENTS, ROW_LEN, SENT_MAX, 2))(jax.random.split(keys[1], ROWS * 2)).reshape((ROWS, 2, SENTS)).astype(jnp.int32)
    self_qkv = scatter_about(keys[2], (2, D, 3 * D), D ** -0.5, 0.25, ((0, 2),))
    self_out = scatter_about(keys[3], (2, D, D), (D // 16) ** -0.5, 1.0, ((0, 2),))
    ffn_in = scatter_about(keys[4], (2, D, FF), D ** -0.5, 0.25, ((0, 2),))
    ffn_in_bias = scatter_about(keys[5], (2, FF), 0.5, 3.0, ((0, 2),))
    ffn_out = scatter_about(keys[6], (2, FF, D), FF ** -0.5, 0.125, ((0, 2),))
    ffn_out_bias = scatter_about(keys[7], (2, D), 0.5, 3.0, ((0, 2),))
    norm_gain = jnp.clip(1.0 + 0.15 * jax.random.normal(keys[8], (2, 2, D), jnp.float32), 0.25, 1.75).astype(jnp.bfloat16)
    norm_bias = scatter_about(keys[9], (2, 2, D), 0.5, 3.0, ((0, 2),))
    cross_weights = draw_cross_weights(jax.random.fold_in(keys[14], 71), 0)
    cross_gain = jnp.clip(1.0 + 0.15 * jax.random.normal(keys[11], (D,), jnp.float32), 0.25, 1.75).astype(jnp.bfloat16)
    cross_bias = scatter_about(keys[12], (D,), 0.5, 3.0)
    output_grad = scatter_about(keys[13], (TOKENS, D), 1.0, 6.0, ((0, 16),))
    return {"token_rows": token_rows, "lengths": lengths, "self_qkv": self_qkv, "self_out": self_out, "ffn_in": ffn_in, "ffn_in_bias": ffn_in_bias, "ffn_out": ffn_out, "ffn_out_bias": ffn_out_bias, "norm_gain": norm_gain, "norm_bias": norm_bias, "cross_weights": cross_weights, "cross_gain": cross_gain, "cross_bias": cross_bias, "output_grad": output_grad}


EPSILON = 1e-05
MASKED = -1000000000.0
HIGHEST = lax.Precision.HIGHEST

@jax.custom_vjp
def low(v):
    return lax.optimization_barrier(v.astype(jnp.bfloat16)).astype(jnp.float32)

@jax.custom_vjp
def low_back(v):
    return v

def low_keep(v):
    return (low(v), None)

def low_pass(kept, grad):
    return (grad,)

def back_keep(v):
    return (v, None)

def back_low(kept, grad):
    return (low(grad),)
low.defvjp(low_keep, low_pass)
low_back.defvjp(back_keep, back_low)

def product(former, latter):
    return jnp.dot(former, latter, precision=HIGHEST)

def layer_norm(values, norm_gain, norm_offset):
    centre = values - lax.optimization_barrier(jnp.mean(values, axis=-1, keepdims=True))
    spread = lax.optimization_barrier(jnp.mean(centre * centre, axis=-1, keepdims=True))
    return centre * lax.rsqrt(spread + EPSILON) * norm_gain + norm_offset

def segment_ids(length_row):
    bounds = jnp.cumsum(length_row).astype(jnp.int32)
    places = jnp.arange(ROW_LEN, dtype=jnp.int32)
    return lax.optimization_barrier(jnp.sum((places[:, None] >= bounds[None, :]).astype(jnp.int32), axis=1)).astype(jnp.int32)

def attention(queries, key_rows, values, allowed):
    scaling = HEAD_DIM ** (-0.5)
    query_heads = queries.reshape(queries.shape[0], HEADS, HEAD_DIM)
    key_heads = key_rows.reshape(key_rows.shape[0], HEADS, HEAD_DIM)
    value_heads = values.reshape(values.shape[0], HEADS, HEAD_DIM)
    scores = low_back(scaling * jnp.einsum('qhd,khd->hqk', query_heads, key_heads, precision=HIGHEST))
    scores = jnp.where(allowed[None], scores, MASKED)
    attn_probs = low(jax.nn.softmax(scores, axis=-1))
    attended = jnp.einsum('hqk,khd->qhd', attn_probs, value_heads, precision=HIGHEST)
    return attended.reshape(queries.shape[0], D)

def self_part(state, w_qkv, w_attn, allowed):
    projected = low(low_back(product(low(state), w_qkv)))
    attended = low(low_back(attention(projected[:, :D], projected[:, D:2 * D], projected[:, 2 * D:], allowed)))
    return low_back(product(attended, w_attn))

def feed_forward(hidden, w_in, b_in, w_out, b_out):
    pre_gelu = low_back(product(low(hidden), w_in) + b_in)
    activated = low(jax.nn.gelu(pre_gelu))
    return low_back(product(activated, w_out) + b_out)

def encoder_layer(state, params, allowed):
    w_qkv, w_attn, w_in, b_in, w_out, b_out, gain_rows, offsets = params
    hidden = layer_norm(state + self_part(state, w_qkv, w_attn, allowed), gain_rows[0], offsets[0])
    return layer_norm(hidden + feed_forward(hidden, w_in, b_in, w_out, b_out), gain_rows[1], offsets[1])

def decoder_layer(state, memory_kv, params, cross_w, cross_gain_f, cross_bias_f, self_mask, cross_mask):
    w_qkv, w_attn, w_in, b_in, w_out, b_out, gain_rows, offsets = params
    hidden = layer_norm(state + self_part(state, w_qkv, w_attn, self_mask), gain_rows[0], offsets[0])
    cross_queries = low(low_back(product(low(hidden), cross_w[:, :D])))
    cross_attended = low(low_back(attention(cross_queries, memory_kv[:, :D], memory_kv[:, D:], cross_mask)))
    joined = layer_norm(hidden + low_back(product(cross_attended, cross_w[:, D:])), cross_gain_f, cross_bias_f)
    return layer_norm(joined + feed_forward(joined, w_in, b_in, w_out, b_out), gain_rows[1], offsets[1])

def row_pass(enc_params, dec_params, enc_cross, dec_cross, cross_gain_f, cross_bias_f, source, target, length_pair):
    source_ids = segment_ids(length_pair[0])
    target_ids = segment_ids(length_pair[1])
    places = jnp.arange(ROW_LEN, dtype=jnp.int32)
    enc_mask = source_ids[:, None] == source_ids[None, :]
    dec_mask = (target_ids[:, None] == target_ids[None, :]) & (places[:, None] >= places[None, :])
    cross_mask = target_ids[:, None] == source_ids[None, :]
    state = source
    for repeat in range(REPEATS):
        state = encoder_layer(state, enc_params, enc_mask)
    memory_kv = low(low_back(product(low(state), enc_cross)))
    output = target
    for repeat in range(REPEATS):
        output = decoder_layer(output, memory_kv, dec_params, dec_cross, cross_gain_f, cross_bias_f, dec_mask, cross_mask)
    return (state, output)

def forward(rows, stacked, cross_gain_f, cross_bias_f, lengths):
    enc_params = tuple((weight[0] for weight in stacked[:8]))
    dec_params = tuple((weight[1] for weight in stacked[:8]))
    source = rows[0].reshape(ROWS, ROW_LEN, D)
    target = rows[1].reshape(ROWS, ROW_LEN, D)

    def one_row(packed_row):
        return row_pass(enc_params, dec_params, stacked[8][0], stacked[8][1], cross_gain_f, cross_bias_f, packed_row[0], packed_row[1], packed_row[2])
    memory, decoded = lax.map(jax.checkpoint(one_row), (source, target, lengths))
    return (memory.reshape(TOKENS, D), decoded.reshape(TOKENS, D))

def reference(token_rows, lengths, self_qkv, self_out, ffn_in, ffn_in_bias, ffn_out, ffn_out_bias, norm_gain, norm_bias, cross_weights, cross_gain, cross_bias, output_grad):
    stacked = tuple((weight.astype(jnp.float32) for weight in (self_qkv, self_out, ffn_in, ffn_in_bias, ffn_out, ffn_out_bias, norm_gain, norm_bias, cross_weights)))

    def run(rows, stacked_f, gain_f, offset_f):
        return forward(rows, stacked_f, gain_f, offset_f, lengths)
    (memory, decoded), pull_back = jax.vjp(run, token_rows.astype(jnp.float32), stacked, cross_gain.astype(jnp.float32), cross_bias.astype(jnp.float32))
    rows_grad, weight_grads, gain_grad, offset_grad = pull_back((jnp.zeros_like(memory), output_grad.astype(jnp.float32)))
    layer_rows = jnp.stack([memory, decoded]).astype(jnp.bfloat16)
    return (layer_rows, rows_grad, weight_grads[0], weight_grads[1], weight_grads[2], weight_grads[3], weight_grads[4], weight_grads[5], weight_grads[6], weight_grads[7], weight_grads[8], gain_grad, offset_grad)
```

```python
import types

import jax
import jax.numpy as jnp
from jax import lax
from jax.experimental import pallas as pl
from jax.experimental.pallas import tpu as pltpu
from jax.sharding import PartitionSpec as P

BF, F32 = jnp.bfloat16, jnp.float32
D, FF, HEAD_DIM, SENTS, REPEATS = 512, 2048, 64, 8, 2
T = 512
WIN = 128
EPSILON = 1e-05
MASKED = -1e9
SCALE = HEAD_DIM**-0.5
LOG2E = 1.4426950408889634
K0 = 0.7978845608028654
K1 = K0 * 0.044715
UNROLL = 4
VMEM_LIMIT = 60 * 2**20


def nn(a, b):
    return lax.dot_general(a, b, (((1,), (0,)), ((), ())), preferred_element_type=F32)


def nt(a, b):
    return lax.dot_general(a, b, (((1,), (1,)), ((), ())), preferred_element_type=F32)


def tn(a, b):
    return lax.dot_general(a, b, (((0,), (0,)), ((), ())), preferred_element_type=F32)


def iota(axis):
    return lax.broadcasted_iota(jnp.int32, (WIN, WIN), axis)


def halves():
    lane = lax.broadcasted_iota(jnp.int32, (1, WIN), 1)
    even = jnp.where(lane < HEAD_DIM, 1.0, 0.0).astype(BF)
    odd = jnp.where(lane < HEAD_DIM, 0.0, 1.0).astype(BF)
    return even, odd


def wide(ref, rows):
    part = ref[rows, :]
    return jnp.concatenate([part] * (D // WIN), 1)


def chunks(size=256):
    return [slice(i, i + size) for i in range(0, T, size)]


def prepare(lens, starts):
    for side in range(2):
        total = jnp.int32(0)
        for j in range(SENTS):
            starts[side, j] = total
            total = total + lens[0, side, j]


def window(lens, starts, side, s):
    first = starts[side, s]
    base = pl.multiple_of(jnp.minimum((first // 16) * 16, T - WIN), 16)
    return base, first - base, first - base + lens[0, side, s]


def sentences(body):
    @pl.loop(0, SENTS // UNROLL)
    def _(j):
        for t in range(UNROLL):
            body(j * UNROLL + t)


def attend(q, qc, k, kc, v, vc, out, probs, lens, starts, qside, kside, lim):
    even, odd = halves()
    row, col = iota(0), iota(1)

    def body(s):
        wq, lo, hi = window(lens, starts, qside, s)
        wk, klo, khi = (wq, lo, hi) if kside is qside else window(lens, starts, kside, s)
        valid = (row >= klo) & (row < khi)
        if lim is not None:
            valid = valid & (row - col <= lim)
        mine = (row >= lo) & (row < hi)
        for g in range(4):
            qs = q[pl.ds(wq, WIN), qc + g * WIN : qc + (g + 1) * WIN]
            ks = k[pl.ds(wk, WIN), kc + g * WIN : kc + (g + 1) * WIN]
            vs = v[pl.ds(wk, WIN), vc + g * WIN : vc + (g + 1) * WIN]
            scores = nt(ks, jnp.concatenate([qs * even, qs * odd], 0))
            parts = []
            for h in range(2):
                x = jnp.where(valid, scores[:, h * WIN : (h + 1) * WIN] * (SCALE * LOG2E), MASKED)
                p = jnp.exp2(x - jnp.max(x, 0, keepdims=True))
                parts.append((p * (1.0 / jnp.sum(p, 0, keepdims=True))).astype(BF))
            probs[s, :, g * 2 * WIN : (g + 1) * 2 * WIN] = jnp.concatenate(parts, 1)
            turned = jnp.concatenate([parts[0].T, parts[1].T], 1)
            r = nn(turned, jnp.concatenate([vs * even, vs * odd], 0))
            place = (pl.ds(wq, WIN), slice(g * WIN, (g + 1) * WIN))
            out[place] = jnp.where(mine, r, out[place].astype(F32)).astype(BF)

    sentences(body)


def attend_backward(q, qc, k, kc, v, vc, probs, grad, dq, dkv, lens, starts, qside, kside):
    even, odd = halves()
    row = iota(0)

    def body(s):
        wq, lo, hi = window(lens, starts, qside, s)
        wk, klo, khi = (wq, lo, hi) if kside is qside else window(lens, starts, kside, s)
        mine = (row >= lo) & (row < hi)
        theirs = (row >= klo) & (row < khi)
        keep = jnp.where(mine, 1.0, 0.0).astype(BF)
        keep_even, keep_odd = keep * even, keep * odd
        for g in range(4):
            qs = q[pl.ds(wq, WIN), qc + g * WIN : qc + (g + 1) * WIN]
            ks = k[pl.ds(wk, WIN), kc + g * WIN : kc + (g + 1) * WIN]
            vs = v[pl.ds(wk, WIN), vc + g * WIN : vc + (g + 1) * WIN]
            go = grad[pl.ds(wq, WIN), g * WIN : (g + 1) * WIN]
            both_g = jnp.concatenate([go * keep_even, go * keep_odd], 0)
            both_q = jnp.concatenate([qs * even, qs * odd], 0)
            p_low = probs[s, :, g * 2 * WIN : (g + 1) * 2 * WIN]
            p = p_low.astype(F32)
            dp = nt(vs, both_g)
            ds = (p * (dp - jnp.sum(p * dp, 0, keepdims=True))).astype(BF)
            dv = nn(p_low, both_g)
            dk = nn(ds, both_q) * SCALE
            turned = jnp.concatenate([ds[:, :WIN].T, ds[:, WIN:].T], 1)
            dqs = nn(turned, jnp.concatenate([ks * even, ks * odd], 0)) * SCALE
            ref, c = dq
            place = (pl.ds(wq, WIN), slice(c + g * WIN, c + (g + 1) * WIN))
            ref[place] = jnp.where(mine, dqs, ref[place].astype(F32)).astype(BF)
            ref, c_k, c_v, adds = dkv
            for c, value in ((c_k, dk), (c_v, dv)):
                place = (pl.ds(wk, WIN), slice(c + g * WIN, c + (g + 1) * WIN))
                if adds:
                    ref[place] += value
                else:
                    ref[place] = jnp.where(theirs, value, ref[place].astype(F32)).astype(BF)

    sentences(body)


def normed(v):
    centre = v - jnp.mean(v, -1, keepdims=True)
    rstd = lax.rsqrt(jnp.mean(centre * centre, -1, keepdims=True) + EPSILON)
    return centre * rstd, rstd


def norm_out(v, rows, xh, rs, gain, bias, wide_ref, low_ref):
    xhat, rstd = normed(v)
    xh[rows, :] = xhat.astype(BF)
    rs[rows, :] = jnp.broadcast_to(rstd, (v.shape[0], WIN))
    h = xhat * gain + bias
    wide_ref[rows, :] = h
    low_ref[rows, :] = h.astype(BF)


def norm_backward(dst, xh, rs, gain, low, vec, gain_row, bias_row):
    for rows in chunks():
        dy = dst[rows, :]
        xhat = xh[rows, :].astype(F32)
        rstd = wide(rs, rows)
        prod = dy * xhat
        vec[gain_row : gain_row + 1, :] += jnp.sum(prod, 0, keepdims=True)
        vec[bias_row : bias_row + 1, :] += jnp.sum(dy, 0, keepdims=True)
        scaled = dy * gain
        m1 = jnp.mean(scaled, -1, keepdims=True)
        m2 = jnp.mean(prod * gain, -1, keepdims=True)
        ds = rstd * (scaled - m1 - xhat * m2)
        dst[rows, :] = ds
        low[rows, :] = ds.astype(BF)


def self_forward(x, low, w_qkv, w_out, qkv, att, probs, xh, rs, gain, bias, h, h_low, lens, starts, side, lim):
    for c in range(3):
        cols = slice(c * D, (c + 1) * D)
        qkv[:, cols] = nn(low[...], w_qkv[:, cols]).astype(BF)
    attend(qkv, 0, qkv, D, qkv, 2 * D, att, probs, lens, starts, side, side, lim)
    for rows in chunks():
        norm_out(x[rows, :] + nn(att[rows, :], w_out[...]), rows, xh, rs, gain, bias, h, h_low)


def self_tail(dst, da, w_out, tmp, qkv, probs, dqkv, w_qkv, lens, starts, side):
    tmp[...] = nt(da[...], w_out[...]).astype(BF)
    attend_backward(
        qkv, 0, qkv, D, qkv, 2 * D, probs, tmp, (dqkv, 0), (dqkv, D, 2 * D, False), lens, starts, side, side
    )
    for rows in chunks():
        dst[rows, :] += nt(dqkv[rows, :], w_qkv[...])


def self_backward(dst, xh, rs, gain, vec, da, w_out, tmp, qkv, probs, dqkv, w_qkv, lens, starts, side):
    norm_backward(dst, xh, rs, gain, da, vec, 5, 7)
    self_tail(dst, da, w_out, tmp, qkv, probs, dqkv, w_qkv, lens, starts, side)


def ffn_forward(h, h_low, w_in, b_in, w_out, b_out, z, gd, xh, rs, gain, bias, out, out_low):
    for c in range(4):
        cols = slice(c * D, (c + 1) * D)
        u = nn(h_low[...], w_in[:, cols]) + b_in[:, cols].astype(F32)
        square = u * u
        half = 0.5 + 0.5 * jnp.tanh(u * (K0 + K1 * square))
        act = u * half
        z[:, cols] = act.astype(BF)
        gd[:, cols] = (half + act * (1.0 - half) * (2.0 * K0 + 6.0 * K1 * square)).astype(BF)
    for rows in chunks():
        v = h[rows, :] + (nn(z[rows, :], w_out[...]) + b_out[...].astype(F32))
        norm_out(v, rows, xh, rs, gain, bias, out, out_low)


def ffn_backward(dst, xh, rs, gain, vec, dz, gdu, w_in, w_out):
    norm_backward(dst, xh, rs, gain, dz, vec, 6, 8)
    vec[4:5, :] += jnp.sum(dz[...].astype(F32), 0, keepdims=True)
    for c in range(4):
        cols = slice(c * D, (c + 1) * D)
        du = (nt(dz[...], w_out[cols, :]) * gdu[:, cols].astype(F32)).astype(BF)
        gdu[:, cols] = du
        vec[c : c + 1, :] += jnp.sum(du.astype(F32), 0, keepdims=True)
    for rows in chunks():
        dst[rows, :] += nt(gdu[rows, :], w_in[...])


def rows_of(ref):
    return ref[...].reshape(2 * T, ref.shape[-1])


class Copies:
    def __init__(self, sems):
        self.sems, self.used = sems, 0

    def slots(self, count=1):
        first = self.used
        self.used += count
        return first

    def make(self, src, dst, slot=None):
        slot = self.slots() if slot is None else slot
        return pltpu.make_async_copy(src, dst, self.sems.at[slot])

    def table(self, **pairs):
        return types.SimpleNamespace(**{n: self.make(a, b) for n, (a, b) in pairs.items()})


def every(table):
    return list(vars(table).values())


HERE, VMEM, SMEM = pl.ANY, pltpu.VMEM, pltpu.SMEM


def phase(body, ins, outs, scratch, flops, n_sems=64):
    in_names, out_names, names = list(ins), list(outs), list(scratch)

    def kernel(*refs):
        labels = in_names + out_names + ["v_" + n for n in names]
        r = types.SimpleNamespace(**dict(zip(labels, refs)))
        r.starts, r.sems = refs[-2:]
        body(r)

    moved = sum(a.size * a.dtype.itemsize for a, _ in ins.values())
    results = pl.pallas_call(
        kernel,
        name=body.__name__,
        in_specs=[pl.BlockSpec(memory_space=s) for _, s in ins.values()],
        out_specs=[pl.BlockSpec(memory_space=HERE)] * len(outs),
        out_shape=[jax.ShapeDtypeStruct(s, d) for s, d in outs.values()],
        scratch_shapes=[VMEM(s, d) for s, d in scratch.values()]
        + [SMEM((2, SENTS), jnp.int32), pltpu.SemaphoreType.DMA((n_sems,))],
        compiler_params=pltpu.CompilerParams(vmem_limit_bytes=VMEM_LIMIT),
        cost_estimate=pl.CostEstimate(flops=flops, bytes_accessed=moved, transcendentals=0),
    )(*[a for a, _ in ins.values()])
    return types.SimpleNamespace(**dict(zip(out_names, results)))


ROW, BOTH, FFN = ((T, D), BF), ((2, T, D), BF), ((2, T, FF), BF)
ROW32, TRIPLE = ((T, D), F32), ((T, 3 * D), BF)
RSTD, RSTDS = ((T, WIN), F32), ((2, T, WIN), F32)
PROBS, VEC, MEMKV = ((SENTS, WIN, 2 * T), BF), ((16, D), F32), ((T + 16, 2 * D), BF)
W_IN, W_OUT, W_QKV, W_CROSS, W_SQUARE = ((D, FF), BF), ((FF, D), BF), ((D, 3 * D), BF), ((D, 2 * D), BF), ((D, D), BF)


def twice(kind):
    return ((2,) + kind[0], kind[1])


def at_hand(w):
    return types.SimpleNamespace(**{n: (a, SMEM if n == "lens" else VMEM if a.ndim < 3 or a.shape[1] < 8 else HERE) for n, a in vars(w).items()})


def is_encoder():
    return lax.axis_index("section") == 0


def gains(r):
    return [r.gain[0, j : j + 1, :].astype(F32) for j in range(2)]


def biases(r):
    return [r.bias[0, j : j + 1, :].astype(F32) for j in range(2)]


def first(r):
    enc = is_encoder()
    dec = jnp.logical_not(enc)
    cp = Copies(r.sems)
    load = cp.table(
        x=(r.tok.at[0], r.v_low.at[0]),
        qkv=(r.w_qkv.at[0], r.v_wqkv),
        so=(r.w_so.at[0], r.v_wso),
        fin=(r.w_fin.at[0], r.v_fin),
        fout=(r.w_fout.at[0], r.v_fout),
        cq=(r.w_cross.at[0, :, :D], r.v_cross),
    )
    load.x.start()
    load.qkv.start()
    load.so.start()

    @pl.when(enc)
    def _():
        load.fin.start()
        load.fout.start()

    @pl.when(dec)
    def _():
        load.cq.start()

    prepare(r.lens, r.starts)
    lim = jnp.where(enc, 4 * T, 0)
    r.v_att[...] = jnp.zeros(r.v_att.shape, BF)
    load.x.wait()
    r.v_x[...] = r.v_low[0].astype(F32)
    gain, bias = gains(r), biases(r)
    self_slots, ffn_slots = cp.slots(12), cp.slots(8)

    def self_copies(i):
        pairs = (
            (r.v_qkv, r.qkv), (r.v_probs, r.probs), (r.v_att, r.att), (r.v_xh1, r.xh1), (r.v_rs1, r.rs1),
            (r.v_hlow, r.hlow),
        )
        return [cp.make(a.at[i], b.at[i], self_slots + 2 * n + i) for n, (a, b) in enumerate(pairs)]

    def ffn_copies(i):
        pairs = ((r.v_z, r.z), (r.v_gd, r.gd), (r.v_xh2, r.xh2), (r.v_rs2, r.rs2))
        return [cp.make(a.at[i], b.at[i], ffn_slots + 2 * n + i) for n, (a, b) in enumerate(pairs)]

    @pl.loop(0, REPEATS)
    def _(i):
        @pl.when(i == 0)
        def _():
            load.qkv.wait()
            load.so.wait()

        @pl.when(jnp.logical_or(enc, i == 0))
        def _():
            self_forward(
                r.v_x, r.v_low.at[i], r.v_wqkv, r.v_wso, r.v_qkv.at[i], r.v_att.at[i], r.v_probs.at[i],
                r.v_xh1.at[i], r.v_rs1.at[i], gain[0], bias[0], r.v_h, r.v_hlow.at[i], r.lens, r.starts,
                lax.axis_index("section"), lim,
            )
            for c in self_copies(i):
                c.start()

        @pl.when(jnp.logical_and(enc, i == 0))
        def _():
            load.fin.wait()
            load.fout.wait()

        @pl.when(enc)
        def _():
            ffn_forward(
                r.v_h, r.v_hlow.at[i], r.v_fin, r.b_in, r.v_fout, r.b_out, r.v_z.at[i], r.v_gd.at[i],
                r.v_xh2.at[i], r.v_rs2.at[i], gain[1], bias[1], r.v_x, r.v_low.at[i + 1],
            )
            for c in ffn_copies(i):
                c.start()

    dec_out = cp.table(h=(r.v_h, r.h), cq=(r.v_cq, r.cq))
    enc_out = cp.table(x1=(r.v_low.at[1], r.x1low), mem=(r.v_low.at[2], r.mem))

    @pl.when(dec)
    def _():
        load.cq.wait()
        r.v_cq[...] = nn(r.v_hlow[0], r.v_cross[...]).astype(BF)
        for c in every(dec_out):
            c.start()
        for c in self_copies(0) + every(dec_out):
            c.wait()

    @pl.when(enc)
    def _():
        for c in every(enc_out):
            c.start()
        for i in range(REPEATS):
            for c in self_copies(i) + ffn_copies(i):
                c.wait()
        for c in every(enc_out):
            c.wait()


def first_phase(w):
    saved = dict(
        qkv=twice(TRIPLE), probs=twice(PROBS), att=BOTH, xh1=BOTH, rs1=RSTDS, hlow=BOTH, z=FFN, gd=FFN, xh2=BOTH,
        rs2=RSTDS, h=ROW32, cq=ROW,
    )
    scratch = dict(saved, low=((3, T, D), BF), wqkv=W_QKV, wso=W_SQUARE, fin=W_IN, fout=W_OUT, cross=W_SQUARE, x=ROW32)
    ins = dict(
        lens=w.lens, tok=w.tok, w_qkv=w.w_qkv, w_so=w.w_so, w_fin=w.w_fin, w_fout=w.w_fout, w_cross=w.w_cross,
        b_in=w.b_in, b_out=w.b_out, gain=w.gain, bias=w.bias,
    )
    return phase(first, ins, dict(saved, x1low=ROW, mem=ROW), scratch, 16 * 10**9)


def middle(r):
    @pl.when(jnp.logical_not(is_encoder()))
    def _():
        cp = Copies(r.sems)
        load = cp.table(
            cq=(r.cq, r.v_cq.at[0]),
            h=(r.h, r.v_h),
            cross=(r.w_cross.at[0], r.v_cross),
            fin=(r.w_fin.at[0], r.v_fin),
            fout=(r.w_fout.at[0], r.v_fout),
            qkv=(r.w_qkv.at[0], r.v_wqkv),
            so=(r.w_so.at[0], r.v_wso),
            og=(r.og, r.v_og),
        )
        for c in every(load):
            c.start()
        prepare(r.lens, r.starts)
        gain, bias = gains(r), biases(r)
        cgain, cbias = r.cgain[...].astype(F32), r.cbias[...].astype(F32)
        for ref in (r.v_vec, r.v_gkv, r.v_catt, r.v_att1, r.v_dcq, r.v_dqkv1):
            ref[...] = jnp.zeros(ref.shape, ref.dtype)
        for c in range(2):
            cols = slice(c * D, (c + 1) * D)
            r.v_mkv[:, cols] = nn(r.mem[...], r.w_c0[0, :, cols]).astype(BF)
        load.cq.wait()
        load.h.wait()
        load.cross.wait()
        saved = (
            (r.v_h1low1, r.h1low1), (r.v_x1low, r.x1low), (r.v_att1, r.att1), (r.v_h2low, r.h2low),
            (r.v_catt, r.catt), (r.v_z, r.z), (r.v_declow, r.decoded),
        )
        early = [cp.make(a, b) for a, b in saved]

        @pl.loop(0, REPEATS)
        def _(i):
            @pl.when(i == 1)
            def _():
                load.qkv.wait()
                load.so.wait()
                self_forward(
                    r.v_x, r.v_x1low, r.v_wqkv, r.v_wso, r.v_qkv1, r.v_att1, r.v_probs1, r.v_xh1, r.v_rs1,
                    gain[0], bias[0], r.v_h, r.v_h1low1, r.lens, r.starts, 1, 0,
                )
                r.v_cq[1] = nn(r.v_h1low1[...], r.v_cross[:, :D]).astype(BF)

            attend(
                r.v_cq.at[i], 0, r.v_mkv, 0, r.v_mkv, D, r.v_catt.at[i], r.v_probsc.at[i], r.lens, r.starts, 1, 0,
                None,
            )
            for rows in chunks():
                v = r.v_h[rows, :] + nn(r.v_catt.at[i][rows, :], r.v_cross[:, D:])
                norm_out(v, rows, r.v_xhc.at[i], r.v_rsc.at[i], cgain, cbias, r.v_h2, r.v_h2low.at[i])

            @pl.when(i == 0)
            def _():
                load.fin.wait()
                load.fout.wait()

            ffn_forward(
                r.v_h2, r.v_h2low.at[i], r.v_fin, r.b_in, r.v_fout, r.b_out, r.v_z.at[i], r.v_gdu.at[i],
                r.v_xh2.at[i], r.v_rs2.at[i], gain[1], bias[1], r.v_x, r.v_declow,
            )

            @pl.when(i == 0)
            def _():
                r.v_x1low[...] = r.v_declow[...]

        for c in early:
            c.start()
        load.og.wait()
        r.v_x[...] = r.v_og[...].astype(F32)

        @pl.loop(0, REPEATS)
        def _(j):
            i = 1 - j
            ffn_backward(
                r.v_x, r.v_xh2.at[i], r.v_rs2.at[i], gain[1], r.v_vec, r.v_dz.at[i], r.v_gdu.at[i], r.v_fin, r.v_fout
            )
            norm_backward(r.v_x, r.v_xhc.at[i], r.v_rsc.at[i], cgain, r.v_dc.at[i], r.v_vec, 9, 10)
            r.v_tmp[...] = nt(r.v_dc[i], r.v_cross[:, D:]).astype(BF)
            attend_backward(
                r.v_cq.at[i], 0, r.v_mkv, 0, r.v_mkv, D, r.v_probsc.at[i], r.v_tmp, (r.v_dcq.at[i], 0),
                (r.v_gkv, 0, D, True), r.lens, r.starts, 1, 0,
            )

            @pl.when(i == 1)
            def _():
                for rows in chunks():
                    r.v_x[rows, :] += nt(r.v_dcq.at[i][rows, :], r.v_cross[:, :D])
                self_backward(
                    r.v_x, r.v_xh1, r.v_rs1, gain[0], r.v_vec, r.v_da1, r.v_wso, r.v_tmp, r.v_qkv1, r.v_probs1,
                    r.v_dqkv1, r.v_wqkv, r.lens, r.starts, 1,
                )

        r.v_gkvlow[:T, :] = r.v_gkv[...].astype(BF)
        r.v_gkvlow[T:, :] = jnp.concatenate(
            [jnp.concatenate([r.v_vec[9:10, :], r.v_vec[10:11, :]], 1), jnp.zeros((15, 2 * D), F32)], 0
        ).astype(BF)
        r.v_gmem[...] = nt(r.v_gkvlow[:T, :], r.w_c0[0]).astype(BF)
        saved = (
            (r.v_gmem, r.gmem), (r.v_gkvlow, r.gkv), (r.v_gdu, r.du), (r.v_dz, r.dz), (r.v_dc, r.dc),
            (r.v_dcq, r.dcq), (r.v_da1, r.da1), (r.v_dqkv1, r.dqkv1), (r.v_x, r.dh), (r.v_vec, r.vec),
        )
        late = [cp.make(a, b) for a, b in saved]
        for c in late:
            c.start()
        for c in early + late:
            c.wait()


def middle_phase(w, one, mem, w_c0):
    outs = dict(
        gmem=ROW, gkv=MEMKV, decoded=ROW, z=FFN, du=FFN, h2low=BOTH, catt=BOTH, h1low1=ROW, dz=BOTH, dc=BOTH, dcq=BOTH,
        att1=ROW, x1low=ROW, da1=ROW, dqkv1=TRIPLE, dh=ROW32, vec=VEC,
    )
    scratch = dict(
        cq=BOTH, h=ROW32, cross=W_CROSS, fin=W_IN, fout=W_OUT, wqkv=W_QKV, wso=W_SQUARE, og=ROW, vec=VEC,
        gkv=((T, 2 * D), F32), catt=BOTH, att1=ROW, dcq=BOTH, dqkv1=TRIPLE, mkv=((T, 2 * D), BF), h1low1=ROW,
        x1low=ROW, h2low=BOTH, z=FFN, declow=ROW, x=ROW32, qkv1=TRIPLE, probs1=PROBS, xh1=ROW, rs1=RSTD,
        probsc=twice(PROBS), xhc=BOTH, rsc=RSTDS, h2=ROW32, gdu=FFN, xh2=BOTH, rs2=RSTDS, dz=BOTH, dc=BOTH, tmp=ROW,
        da1=ROW, gkvlow=MEMKV, gmem=ROW,
    )
    ins = dict(
        lens=w.lens, mem=(mem, VMEM), w_c0=(w_c0, VMEM), cq=(one.cq, HERE), h=(one.h, HERE), og=(w.og[0], HERE),
        w_qkv=w.w_qkv, w_so=w.w_so, w_fin=w.w_fin, w_fout=w.w_fout, w_cross=w.w_cross, b_in=w.b_in, b_out=w.b_out,
        gain=w.gain, bias=w.bias, cgain=w.cgain, cbias=w.cbias,
    )
    return phase(middle, ins, outs, scratch, 30 * 10**9)


PIECES = 16
X_FIRST, Z_FIRST = (0, 1, 2, 3), (0, 2, 3, 1)
ROWS_A = ROWS_B = 512
ROWS_C, ROWS_Q = 32 * 12 + 16, 32 * 12


def place_of(piece, order):
    relative = piece ^ (lax.axis_index("dp") % PIECES)
    place = jnp.int32(0)
    for n, bit in enumerate(order):
        place = place + ((relative >> bit) & 1) * (1 << (3 - n))
    return place


def piece_at(place, order):
    relative = 0
    for n, bit in enumerate(order):
        relative += ((place >> (3 - n)) & 1) << bit
    return relative ^ (lax.axis_index("dp") % PIECES)


def put(dst, order, block, first_row, first_col, high):
    height, width = block.shape
    for j in range(0, height, high):
        place = place_of((first_row + j) // high, order)
        for c in range(0, width, WIN):
            at = ((first_col + c) // WIN) * high
            dst[place, at : at + high, :] = block[j : j + high, c : c + WIN].astype(BF)


def split_out(cp, ref, keep, send):
    made = [cp.make(ref.at[:8], keep), cp.make(ref.at[8:], send)]
    for c in made:
        c.start()
    return made


def third(r):
    enc = is_encoder()
    cp = Copies(r.sems)
    load = cp.table(
        xh2=(r.xh2, r.v_xh2),
        rs2=(r.rs2, r.v_rs2),
        fout=(r.w_fout.at[0], r.v_fout),
        gd=(r.gd, r.v_gdu),
        fin=(r.w_fin.at[0], r.v_fin),
        xh1=(r.xh1.at[1], r.v_xh1),
        rs1=(r.rs1.at[1], r.v_rs1),
        so=(r.w_so.at[0], r.v_wso),
        qkv=(r.qkv.at[1], r.v_qkv1),
        probs=(r.probs.at[1], r.v_probs1),
        wqkv=(r.w_qkv.at[0], r.v_wqkv),
        z=(r.z, r.v_z),
        hlow=(r.hlow, r.v_hlow),
    )
    saved = ((r.v_x, r.dh), (r.v_da1, r.da1), (r.v_dqkv1, r.dqkv1), (r.v_vec, r.vec))
    out = [cp.make(a, b) for a, b in saved]

    @pl.when(enc)
    def _():
        for c in every(load):
            c.start()
        prepare(r.lens, r.starts)
        gain = gains(r)
        r.v_vec[...] = jnp.zeros(r.v_vec.shape, F32)
        r.v_dqkv1[...] = jnp.zeros(r.v_dqkv1.shape, BF)
        r.v_x[...] = r.gmem[...].astype(F32)
        for c in (load.xh2, load.rs2, load.fout, load.gd, load.fin):
            c.wait()

        @pl.loop(0, REPEATS)
        def _(j):
            i = 1 - j
            ffn_backward(
                r.v_x, r.v_xh2.at[i], r.v_rs2.at[i], gain[1], r.v_vec, r.v_dz.at[i], r.v_gdu.at[i], r.v_fin, r.v_fout
            )

            @pl.when(i == 1)
            def _():
                for c in (load.xh1, load.rs1, load.so, load.qkv, load.probs, load.wqkv):
                    c.wait()
                self_backward(
                    r.v_x, r.v_xh1, r.v_rs1, gain[0], r.v_vec, r.v_da1, r.v_wso, r.v_tmp, r.v_qkv1, r.v_probs1,
                    r.v_dqkv1, r.v_wqkv, r.lens, r.starts, 0,
                )

        for c in out:
            c.start()
        load.z.wait()
        load.hlow.wait()

    dec_load = cp.table(z=(r.z_d, r.v_z), du=(r.du_d, r.v_gdu), h=(r.h2low_d, r.v_hlow), dz=(r.dz_d, r.v_dz))

    @pl.when(jnp.logical_not(enc))
    def _():
        for c in every(dec_load):
            c.start()
        for c in every(dec_load):
            c.wait()

    hidden, grad_out = rows_of(r.v_hlow), rows_of(r.v_dz)
    for c in range(4):
        cols = slice(c * D, (c + 1) * D)
        put(r.v_a, X_FIRST, tn(hidden, r.v_gdu[:, :, cols].reshape(2 * T, D)), 0, c * D, 32)
    sends = split_out(cp, r.v_a, r.a_keep, r.a_send)
    for c in range(4):
        cols = slice(c * D, (c + 1) * D)
        put(r.v_b, Z_FIRST, tn(r.v_z[:, :, cols].reshape(2 * T, D), grad_out), c * D, 0, 128)
    sends += split_out(cp, r.v_b, r.b_keep, r.b_send)
    for c in sends:
        c.wait()

    @pl.when(enc)
    def _():
        for c in out:
            c.wait()


def third_phase(w, one, two, gmem):
    half_a, half_b = ((8, ROWS_A, WIN), BF), ((8, ROWS_B, WIN), BF)
    outs = dict(dh=ROW32, da1=ROW, dqkv1=TRIPLE, vec=VEC, a_keep=half_a, a_send=half_a, b_keep=half_b, b_send=half_b)
    scratch = dict(
        xh2=BOTH, rs2=RSTDS, fout=W_OUT, gdu=FFN, fin=W_IN, xh1=ROW, rs1=RSTD, wso=W_SQUARE, qkv1=TRIPLE, probs1=PROBS,
        wqkv=W_QKV, z=FFN, hlow=BOTH, x=ROW32, da1=ROW, dqkv1=TRIPLE, vec=VEC, dz=BOTH, tmp=ROW,
        a=((PIECES, ROWS_A, WIN), BF), b=((PIECES, ROWS_B, WIN), BF),
    )
    ins = dict(lens=w.lens, gmem=(gmem, VMEM), w_qkv=w.w_qkv, w_so=w.w_so, w_fin=w.w_fin, w_fout=w.w_fout, gain=w.gain)
    more = dict(
        xh2=one.xh2, rs2=one.rs2, gd=one.gd, xh1=one.xh1, rs1=one.rs1, qkv=one.qkv, probs=one.probs, z=one.z,
        hlow=one.hlow, z_d=two.z, du_d=two.du, h2low_d=two.h2low, dz_d=two.dz,
    )
    ins.update({n: (a, HERE) for n, a in more.items()})
    return phase(third, ins, outs, scratch, 25 * 10**9)


def fourth(r):
    enc = is_encoder()
    dec = jnp.logical_not(enc)
    cp = Copies(r.sems)
    first_slot = cp.slots(6)

    def own(encoder):
        pairs = (
            (r.dh_e if encoder else r.dh_d, r.v_x),
            (r.vec_e if encoder else r.vec_d, r.v_vec),
            (r.da1_e if encoder else r.da1_d, r.v_da.at[1]),
            (r.att.at[1] if encoder else r.att1_d, r.v_att.at[1]),
        )
        return [cp.make(a, b, first_slot + n) for n, (a, b) in enumerate(pairs)]

    load = cp.table(
        xh1=(r.xh1.at[0], r.v_xh1),
        rs1=(r.rs1.at[0], r.v_rs1),
        att=(r.att.at[0], r.v_att.at[0]),
    )
    enc_cross = cp.table(mem=(r.mem, r.v_one.at[0]))
    dec_cross = cp.table(
        cross=(r.w_cross.at[0, :, :D], r.v_cross),
        h0=(r.hlow.at[0], r.v_one.at[0]),
        h1=(r.h1low1, r.v_one.at[1]),
        att=(r.catt, r.v_two),
        dc=(r.dc, r.v_dc),
        dcq=(r.dcq, r.v_dcq),
        layer=(r.decoded, r.v_layer),
    )
    gain = gains(r)

    @pl.when(enc)
    def _():
        for c in own(True) + every(enc_cross):
            c.start()

    @pl.when(dec)
    def _():
        for c in own(False) + every(dec_cross):
            c.start()

    for c in every(load):
        c.start()
    for c in own(True) + every(load):
        c.wait()

    @pl.when(dec)
    def _():
        dec_cross.cross.wait()
        dec_cross.dcq.wait()
        for rows in chunks():
            r.v_x[rows, :] += nt(r.v_dcq.at[0][rows, :], r.v_cross[...])

    norm_backward(r.v_x, r.v_xh1, r.v_rs1, gain[0], r.v_da.at[0], r.v_vec, 5, 7)
    out = cp.table(x=(r.v_x, r.ds), da=(r.v_da.at[0], r.da0))
    for c in every(out):
        c.start()
    layer_slot = cp.slots()
    enc_layer = cp.make(r.v_one.at[0], r.layer.at[0], layer_slot)
    dec_layer = cp.make(r.v_layer, r.layer.at[0], layer_slot)
    put(r.v_c, Z_FIRST, tn(rows_of(r.v_att), rows_of(r.v_da)), 0, 0, 32)

    @pl.when(enc)
    def _():
        enc_cross.mem.wait()
        enc_layer.start()
        for c in range(2):
            cols = slice(c * D, (c + 1) * D)
            put(r.v_c, Z_FIRST, tn(r.v_one[0], r.gkv[:T, cols]), 0, D + c * D, 32)
        tail = r.gkv[T:, :].astype(F32)
        r.v_vec[9:10, :] = tail[0:1, :D]
        r.v_vec[10:11, :] = tail[0:1, D:]

    @pl.when(dec)
    def _():
        dec_cross.layer.wait()
        dec_layer.start()
        for c in (dec_cross.h0, dec_cross.h1, dec_cross.att, dec_cross.dc):
            c.wait()
        put(r.v_c, Z_FIRST, tn(rows_of(r.v_one), rows_of(r.v_dcq)), 0, D, 32)
        put(r.v_c, Z_FIRST, tn(rows_of(r.v_two), rows_of(r.v_dc)), 0, 2 * D, 32)

    for p in range(PIECES):
        line = r.v_vec[p : p + 1, :]
        tile = [line[:, j * WIN : (j + 1) * WIN] for j in range(4)] + [jnp.zeros((12, WIN), F32)]
        r.v_c[place_of(p, Z_FIRST), ROWS_C - 16 :, :] = jnp.concatenate(tile, 0).astype(BF)
    for c in split_out(cp, r.v_c, r.c_keep, r.c_send) + every(out) + [enc_layer]:
        c.wait()


def fourth_phase(w, one, two, three, gkv):
    half_c = ((8, ROWS_C, WIN), BF)
    outs = dict(layer=((1, T, D), BF), ds=ROW32, da0=ROW, c_keep=half_c, c_send=half_c)
    scratch = dict(
        xh1=ROW, rs1=RSTD, att=BOTH, x=ROW32, vec=VEC, da=BOTH, one=BOTH, two=BOTH, dc=BOTH, dcq=BOTH, cross=W_SQUARE,
        layer=ROW, c=((PIECES, ROWS_C, WIN), BF),
    )
    ins = dict(gkv=(gkv, VMEM), gain=w.gain, w_cross=w.w_cross)
    more = dict(
        xh1=one.xh1, rs1=one.rs1, att=one.att, mem=one.mem, hlow=one.hlow, dh_e=three.dh, vec_e=three.vec,
        da1_e=three.da1, dh_d=two.dh, vec_d=two.vec, da1_d=two.da1, att1_d=two.att1, h1low1=two.h1low1, catt=two.catt,
        dc=two.dc, dcq=two.dcq, decoded=two.decoded,
    )
    ins.update({n: (a, HERE) for n, a in more.items()})
    return phase(fourth, ins, outs, scratch, 4 * 10**9)


def fifth(r):
    enc = is_encoder()
    cp = Copies(r.sems)
    first_slot = cp.slots(2)

    def own(encoder):
        pairs = (
            (r.dqkv1_e if encoder else r.dqkv1_d, r.v_dqkv.at[1]),
            (r.x1low_e if encoder else r.x1low_d, r.v_low.at[1]),
        )
        return [cp.make(a, b, first_slot + n) for n, (a, b) in enumerate(pairs)]

    load = cp.table(
        da=(r.da0, r.v_da),
        so=(r.w_so.at[0], r.v_wso),
        qkv=(r.qkv.at[0], r.v_qkv),
        probs=(r.probs.at[0], r.v_probs),
        x=(r.ds, r.v_x),
        wqkv=(r.w_qkv.at[0], r.v_wqkv),
        low=(r.tok.at[0], r.v_low.at[0]),
    )
    for c in every(load):
        c.start()

    @pl.when(enc)
    def _():
        for c in own(True):
            c.start()

    @pl.when(jnp.logical_not(enc))
    def _():
        for c in own(False):
            c.start()

    prepare(r.lens, r.starts)
    r.v_dqkv[0] = jnp.zeros(r.v_dqkv.shape[1:], BF)
    for c in every(load) + own(True):
        c.wait()
    self_tail(
        r.v_x, r.v_da, r.v_wso, r.v_tmp, r.v_qkv, r.v_probs, r.v_dqkv.at[0], r.v_wqkv, r.lens, r.starts,
        lax.axis_index("section"),
    )
    made = [cp.make(r.v_x, r.rows.at[0])]
    made[0].start()
    inputs, grads = rows_of(r.v_low), rows_of(r.v_dqkv)
    for c in range(3):
        cols = slice(c * D, (c + 1) * D)
        put(r.v_q, X_FIRST, tn(inputs, grads[:, cols]), 0, c * D, 32)
    for c in made + split_out(cp, r.v_q, r.q_keep, r.q_send):
        c.wait()


def fifth_phase(w, one, two, three, four, before):
    half_q = ((8, ROWS_Q, WIN), BF)
    outs = dict(rows=((1, T, D), F32), q_keep=half_q, q_send=half_q)
    scratch = dict(
        wso=W_SQUARE, qkv=TRIPLE, probs=PROBS, wqkv=W_QKV, low=BOTH, x=ROW32, da=ROW, dqkv=twice(TRIPLE), tmp=ROW,
        q=((PIECES, ROWS_Q, WIN), BF),
    )
    ins = dict(lens=w.lens, tok=w.tok, w_qkv=w.w_qkv, w_so=w.w_so)
    more = dict(
        qkv=one.qkv, probs=one.probs, x1low_e=one.x1low, x1low_d=two.x1low, dqkv1_e=three.dqkv1, dqkv1_d=two.dqkv1,
        ds=four.ds, da0=four.da0,
    )
    ins.update({n: (a, HERE) for n, a in more.items()})
    ins.update({"before%d" % n: (a, VMEM) for n, a in enumerate(before)})
    return phase(fifth, ins, outs, scratch, 8 * 10**9)


def across(value, bit):
    pairs = [(i, i ^ (1 << bit)) for i in range(lax.axis_size("dp"))]
    return lax.ppermute(value, "dp", pairs)


def added(a, b):
    return (a.astype(F32) + b.astype(F32)).astype(BF)


def halve(keep, send, bit):
    got = across(send, bit)
    half = keep.shape[0] // 2
    if half == 0:
        return added(keep, got), None
    return added(keep[:half], got[:half]), added(keep[half:], got[half:])


def scatter_rest(keep, send, order):
    for bit in order[1:]:
        keep, send = halve(keep, send, bit)
    bit = len(order)
    while (1 << bit) < lax.axis_size("dp"):
        keep = added(keep, across(keep, bit))
        bit += 1
    return keep


def gather(piece, order):
    for bit in reversed(order[1:]):
        piece = jnp.concatenate([piece, across(piece, bit)], 0)
    return piece, across(piece, order[0])


def unpack(kernel, ins, scratch, outs):
    return pl.pallas_call(
        kernel,
        name=kernel.__name__,
        in_specs=[pl.BlockSpec(memory_space=VMEM)] * len(ins),
        out_specs=[pl.BlockSpec(memory_space=HERE if big else VMEM) for _, big in outs],
        out_shape=[jax.ShapeDtypeStruct(s, F32) for s, _ in outs],
        scratch_shapes=[VMEM(s, F32) for s in scratch] + [pltpu.SemaphoreType.DMA((len(scratch), PIECES))],
        compiler_params=pltpu.CompilerParams(vmem_limit_bytes=VMEM_LIMIT),
        cost_estimate=pl.CostEstimate(flops=4 * 10**9, bytes_accessed=12 * 10**6, transcendentals=0),
    )(*ins)


def pieces_out(halves, order, high, first, wide, out, whole, sems):
    made = []
    for place in range(PIECES):
        ref, at = halves[place // 8], place % 8
        rows = pl.ds(pl.multiple_of(piece_at(place, order) * high, high), high)
        for c in range(wide // WIN):
            start = first + c * high
            whole[rows, c * WIN : (c + 1) * WIN] = ref[at, start : start + high, :].astype(F32)
        made.append(pltpu.make_async_copy(whole.at[rows, :], out.at[0, rows, :], sems.at[place]))
        made[-1].start()
    return made


def unpack_in(a0, a1, fin, v_fin, sems):
    for c in pieces_out((a0, a1), X_FIRST, 32, 0, FF, fin, v_fin, sems.at[0]):
        c.wait()


def unpack_out(b0, b1, fout, v_fout, sems):
    for c in pieces_out((b0, b1), Z_FIRST, 128, 0, D, fout, v_fout, sems.at[0]):
        c.wait()


def unpack_qkv(q0, q1, qkv, v_qkv, sems):
    for c in pieces_out((q0, q1), X_FIRST, 32, 0, 3 * D, qkv, v_qkv, sems.at[0]):
        c.wait()


def unpack_rest(c0, c1, so, cross, b_in, b_out, gain, bias, cgain, cbias, v_so, v_cross, sems):
    made = pieces_out((c0, c1), Z_FIRST, 32, 0, D, so, v_so, sems.at[0])
    made += pieces_out((c0, c1), Z_FIRST, 32, 4 * 32, 2 * D, cross, v_cross, sems.at[1])

    def line(p):
        place = place_of(p, Z_FIRST)
        at = place % 8
        tail = jnp.where(place < 8, c0[at, ROWS_C - 16 :, :].astype(F32), c1[at, ROWS_C - 16 :, :].astype(F32))
        return jnp.concatenate([tail[j : j + 1, :] for j in range(4)], 1)

    for n in range(4):
        b_in[:, n * D : (n + 1) * D] = line(n)
    b_out[...] = line(4)
    for n in range(2):
        gain[0, n : n + 1, :] = line(5 + n)
        bias[0, n : n + 1, :] = line(7 + n)
    cgain[...] = line(9)
    cbias[...] = line(10)
    for c in made:
        c.wait()


def body(
    token_rows, lengths, self_qkv, self_out, ffn_in, ffn_in_bias, ffn_out, ffn_out_bias, norm_gain, norm_bias,
    cross_weights, cross_gain, cross_bias, output_grad,
):
    to_decoder, to_encoder = [(0, 1)], [(1, 0)]
    w = at_hand(
        types.SimpleNamespace(
            tok=token_rows, lens=lengths, w_qkv=self_qkv, w_so=self_out, w_fin=ffn_in, b_in=ffn_in_bias, w_fout=ffn_out,
            b_out=ffn_out_bias, gain=norm_gain, bias=norm_bias, w_cross=cross_weights, cgain=cross_gain.reshape(1, D),
            cbias=cross_bias.reshape(1, D), og=output_grad,
        )
    )
    w_c0 = lax.ppermute(cross_weights, "section", to_decoder)
    one = first_phase(w)
    mem = lax.ppermute(one.mem, "section", to_decoder)
    two = middle_phase(w, one, mem, w_c0)
    gmem = lax.ppermute(two.gmem, "section", to_encoder)
    gkv = lax.ppermute(two.gkv, "section", to_encoder)
    three = third_phase(w, one, two, gmem)
    four = fourth_phase(w, one, two, three, gkv)
    a, a_send = halve(three.a_keep, three.a_send, 0)
    b, b_send = halve(three.b_keep, three.b_send, 0)
    five = fifth_phase(w, one, two, three, four, (a_send, b_send))
    c, c_send = halve(four.c_keep, four.c_send, 0)
    q, q_send = halve(five.q_keep, five.q_send, 0)
    a = scatter_rest(a, a_send, X_FIRST)
    b = scatter_rest(b, b_send, Z_FIRST)
    c = scatter_rest(c, c_send, Z_FIRST)
    q = scatter_rest(q, q_send, X_FIRST)
    (g_fin,) = unpack(unpack_in, gather(a, X_FIRST), [(D, FF)], [((1, D, FF), True)])
    (g_fout,) = unpack(unpack_out, gather(b, Z_FIRST), [(FF, D)], [((1, FF, D), True)])
    (g_qkv,) = unpack(unpack_qkv, gather(q, X_FIRST), [(D, 3 * D)], [((1, D, 3 * D), True)])
    small = [(1, FF), (1, D), (1, 2, D), (1, 2, D), (1, D), (1, D)]
    g_so, g_cross, g_bin, g_bout, g_gain, g_bias, g_cgain, g_cbias = unpack(
        unpack_rest,
        gather(c, Z_FIRST),
        [(D, D), (D, 2 * D)],
        [((1, D, D), True), ((1, D, 2 * D), True)] + [(shape, False) for shape in small],
    )
    return (
        four.layer, five.rows, g_qkv, g_so, g_fin, g_bin, g_fout, g_bout, g_gain, g_bias, g_cross, g_cgain.reshape(D),
        g_cbias.reshape(D),
    )


def solution(mesh):
    by_section = P("section")
    in_specs = (
        P("section", "dp"), P("dp"), by_section, by_section, by_section, by_section, by_section, by_section, by_section,
        by_section, by_section, P(), P(), P("dp"),
    )
    out_specs = (P("section", "dp"), P("section", "dp")) + (by_section,) * 9 + (P(), P())
    return jax.shard_map(body, mesh=mesh, in_specs=in_specs, out_specs=out_specs, check_vma=False)
```

```python
import types

import jax
import jax.numpy as jnp
from jax import lax
from jax.experimental import pallas as pl
from jax.experimental.pallas import tpu as pltpu
from jax.sharding import PartitionSpec as P

BF, F32 = jnp.bfloat16, jnp.float32
D, FF, HEAD_DIM, SENTS, REPEATS = 512, 2048, 64, 8, 2
T = 512
WIN = 128
EPSILON = 1e-05
MASKED = -1e9
SCALE = HEAD_DIM**-0.5
LOG2E = 1.4426950408889634
K0 = 0.7978845608028654
K1 = K0 * 0.044715
UNROLL_FORWARD, UNROLL_BACKWARD = 8, 4
VMEM_LIMIT = 60 * 2**20


def nn(a, b):
    return lax.dot_general(a, b, (((1,), (0,)), ((), ())), preferred_element_type=F32)


def nt(a, b):
    return lax.dot_general(a, b, (((1,), (1,)), ((), ())), preferred_element_type=F32)


def tn(a, b):
    return lax.dot_general(a, b, (((0,), (0,)), ((), ())), preferred_element_type=F32)


def iota(axis):
    return lax.broadcasted_iota(jnp.int32, (WIN, WIN), axis)


def halves():
    lane = lax.broadcasted_iota(jnp.int32, (1, WIN), 1)
    even = jnp.where(lane < HEAD_DIM, 1.0, 0.0).astype(BF)
    odd = jnp.where(lane < HEAD_DIM, 0.0, 1.0).astype(BF)
    return even, odd


def wide(ref, rows):
    part = ref[rows, :]
    return jnp.concatenate([part] * (D // WIN), 1)


def chunks(size=256):
    return [slice(i, i + size) for i in range(0, T, size)]


def prepare(lens, starts):
    for side in range(2):
        total = jnp.int32(0)
        for j in range(SENTS):
            starts[side, j] = total
            total = total + lens[0, side, j]


def window(lens, starts, side, s):
    first = starts[side, s]
    base = pl.multiple_of(jnp.minimum((first // 16) * 16, T - WIN), 16)
    return base, first - base, first - base + lens[0, side, s]


def sentences(body, unroll):
    @pl.loop(0, SENTS // unroll)
    def _(j):
        for t in range(unroll):
            body(j * unroll + t)


def attend(q, qc, k, kc, v, vc, out, probs, lens, starts, qside, kside, lim):
    even, odd = halves()
    row, col = iota(0), iota(1)
    line = lax.broadcasted_iota(jnp.int32, (1, WIN), 1)

    def body(s):
        wq, lo, hi = window(lens, starts, qside, s)
        wk, klo, khi = (wq, lo, hi) if kside is qside else window(lens, starts, kside, s)
        valid = (row >= klo) & (row < khi)
        if lim is not None:
            valid = valid & (row - col <= lim)
        mine = (line >= lo) & (line < hi)

        def score(g):
            qs = q[pl.ds(wq, WIN), qc + g * WIN : qc + (g + 1) * WIN]
            ks = k[pl.ds(wk, WIN), kc + g * WIN : kc + (g + 1) * WIN]
            return nt(ks, jnp.concatenate([qs * even, qs * odd], 0))

        def soften(g, scores):
            parts = []
            for h in range(2):
                x = jnp.where(valid, scores[:, h * WIN : (h + 1) * WIN] * (SCALE * LOG2E), MASKED)
                p = jnp.exp2(x - jnp.max(x, 0, keepdims=True))
                inverse = jnp.where(mine, 1.0 / jnp.sum(p, 0, keepdims=True), 0.0)
                parts.append((p * inverse).astype(BF))
            probs[s, :, g * 2 * WIN : (g + 1) * 2 * WIN] = jnp.concatenate(parts, 1)
            return jnp.concatenate(parts, 1)

        def finish(g, turned):
            vs = v[pl.ds(wk, WIN), vc + g * WIN : vc + (g + 1) * WIN]
            place = (pl.ds(wq, WIN), slice(g * WIN, (g + 1) * WIN))
            both = tn(turned, vs)
            out[place] += jnp.where(col < HEAD_DIM, both[:WIN], both[WIN:]).astype(BF)

        for g in range(4):
            finish(g, soften(g, score(g)))

    sentences(body, UNROLL_FORWARD)


def attend_backward(q, qc, k, kc, v, vc, probs, grad, dq, dkv, lens, starts, qside, kside):
    even, odd = halves()
    even_s, odd_s = even * SCALE, odd * SCALE

    def body(s):
        wq, _, _ = window(lens, starts, qside, s)
        wk, _, _ = (wq, 0, 0) if kside is qside else window(lens, starts, kside, s)

        def cut(ref, at, c, g):
            return ref[pl.ds(at, WIN), c + g * WIN : c + (g + 1) * WIN]

        def first_part(g):
            go = cut(grad, wq, 0, g)
            both_g = jnp.concatenate([go * even, go * odd], 0)
            return both_g, nt(cut(v, wk, vc, g), both_g)

        def second_part(g, dp):
            p_low = probs[s, :, g * 2 * WIN : (g + 1) * 2 * WIN]
            p = p_low.astype(F32)
            return p_low, (p * (dp - jnp.sum(p * dp, 0, keepdims=True))).astype(BF)

        def third_part(g, both_g, p_low, ds):
            qs, ks = cut(q, wq, qc, g), cut(k, wk, kc, g)
            dv = nn(p_low, both_g)
            dk = nn(ds, jnp.concatenate([qs * even_s, qs * odd_s], 0))
            turned = jnp.concatenate([ds[:, :WIN].T, ds[:, WIN:].T], 1)
            dqs = nn(turned, jnp.concatenate([ks * even_s, ks * odd_s], 0))
            ref, c = dq
            ref[pl.ds(wq, WIN), c + g * WIN : c + (g + 1) * WIN] += dqs.astype(ref.dtype)
            ref, c_k, c_v = dkv
            for c, value in ((c_k, dk), (c_v, dv)):
                ref[pl.ds(wk, WIN), c + g * WIN : c + (g + 1) * WIN] += value.astype(ref.dtype)

        start = [first_part(g) for g in range(4)]
        middle_part = [second_part(g, start[g][1]) for g in range(4)]
        for g in range(4):
            third_part(g, start[g][0], *middle_part[g])

    sentences(body, UNROLL_BACKWARD)


def normed(v):
    centre = v - jnp.mean(v, -1, keepdims=True)
    rstd = lax.rsqrt(jnp.mean(centre * centre, -1, keepdims=True) + EPSILON)
    return centre * rstd, rstd


def norm_out(v, rows, xh, rs, gain, bias, wide_ref, low_ref):
    xhat, rstd = normed(v)
    xh[rows, :] = xhat.astype(BF)
    rs[rows, :] = jnp.broadcast_to(rstd, (v.shape[0], WIN))
    h = xhat * gain + bias
    wide_ref[rows, :] = h
    low_ref[rows, :] = h.astype(BF)


def norm_backward(dst, xh, rs, gain, low, vec, gain_row, bias_row):
    for rows in chunks():
        dy = dst[rows, :]
        xhat = xh[rows, :].astype(F32)
        rstd = wide(rs, rows)
        prod = dy * xhat
        vec[gain_row : gain_row + 1, :] += jnp.sum(prod, 0, keepdims=True)
        vec[bias_row : bias_row + 1, :] += jnp.sum(dy, 0, keepdims=True)
        scaled = dy * gain
        m1 = jnp.mean(scaled, -1, keepdims=True)
        m2 = jnp.mean(prod * gain, -1, keepdims=True)
        ds = rstd * (scaled - m1 - xhat * m2)
        dst[rows, :] = ds
        low[rows, :] = ds.astype(BF)


def self_forward(x, low, w_qkv, w_out, qkv, att, probs, xh, rs, gain, bias, h, h_low, lens, starts, side, lim):
    for c in range(3):
        cols = slice(c * D, (c + 1) * D)
        qkv[:, cols] = nn(low[...], w_qkv[:, cols]).astype(BF)
    attend(qkv, 0, qkv, D, qkv, 2 * D, att, probs, lens, starts, side, side, lim)
    for rows in chunks():
        norm_out(x[rows, :] + nn(att[rows, :], w_out[...]), rows, xh, rs, gain, bias, h, h_low)


def self_tail(dst, da, w_out, tmp, qkv, probs, dqkv, w_qkv, lens, starts, side):
    tmp[...] = nt(da[...], w_out[...]).astype(BF)
    attend_backward(
        qkv, 0, qkv, D, qkv, 2 * D, probs, tmp, (dqkv, 0), (dqkv, D, 2 * D), lens, starts, side, side
    )
    for rows in chunks():
        dst[rows, :] += nt(dqkv[rows, :], w_qkv[...])


def self_backward(dst, xh, rs, gain, vec, da, w_out, tmp, qkv, probs, dqkv, w_qkv, lens, starts, side):
    norm_backward(dst, xh, rs, gain, da, vec, 5, 7)
    self_tail(dst, da, w_out, tmp, qkv, probs, dqkv, w_qkv, lens, starts, side)


def ffn_forward(h, h_low, w_in, b_in, w_out, b_out, z, gd, xh, rs, gain, bias, out, out_low):
    for c in range(4):
        cols = slice(c * D, (c + 1) * D)
        u = nn(h_low[...], w_in[:, cols]) + b_in[:, cols].astype(F32)
        square = u * u
        half = 0.5 + 0.5 * jnp.tanh(u * (K0 + K1 * square))
        act = u * half
        z[:, cols] = act.astype(BF)
        gd[:, cols] = (half + act * (1.0 - half) * (2.0 * K0 + 6.0 * K1 * square)).astype(BF)
    for rows in chunks():
        v = h[rows, :] + (nn(z[rows, :], w_out[...]) + b_out[...].astype(F32))
        norm_out(v, rows, xh, rs, gain, bias, out, out_low)


def ffn_backward(dst, xh, rs, gain, vec, dz, gdu, w_in, w_out):
    norm_backward(dst, xh, rs, gain, dz, vec, 6, 8)
    vec[4:5, :] += jnp.sum(dz[...].astype(F32), 0, keepdims=True)
    for c in range(4):
        cols = slice(c * D, (c + 1) * D)
        du = (nt(dz[...], w_out[cols, :]) * gdu[:, cols].astype(F32)).astype(BF)
        gdu[:, cols] = du
        vec[c : c + 1, :] += jnp.sum(du.astype(F32), 0, keepdims=True)
    for rows in chunks():
        dst[rows, :] += nt(gdu[rows, :], w_in[...])


def rows_of(ref):
    return ref[...].reshape(2 * T, ref.shape[-1])


class Copies:
    def __init__(self, sems):
        self.sems, self.used = sems, 0

    def slots(self, count=1):
        first = self.used
        self.used += count
        return first

    def make(self, src, dst, slot=None):
        slot = self.slots() if slot is None else slot
        return pltpu.make_async_copy(src, dst, self.sems.at[slot])

    def table(self, **pairs):
        return types.SimpleNamespace(**{n: self.make(a, b) for n, (a, b) in pairs.items()})


def every(table):
    return list(vars(table).values())


HERE, VMEM, SMEM = pl.ANY, pltpu.VMEM, pltpu.SMEM


def phase(body, ins, outs, scratch, flops, n_sems=64):
    in_names, out_names, names = list(ins), list(outs), list(scratch)

    def kernel(*refs):
        labels = in_names + out_names + ["v_" + n for n in names]
        r = types.SimpleNamespace(**dict(zip(labels, refs)))
        r.starts, r.sems = refs[-2:]
        body(r)

    moved = sum(a.size * a.dtype.itemsize for a, _ in ins.values())
    results = pl.pallas_call(
        kernel,
        name=body.__name__,
        in_specs=[pl.BlockSpec(memory_space=s) for _, s in ins.values()],
        out_specs=[pl.BlockSpec(memory_space=HERE)] * len(outs),
        out_shape=[jax.ShapeDtypeStruct(s, d) for s, d in outs.values()],
        scratch_shapes=[VMEM(s, d) for s, d in scratch.values()]
        + [SMEM((2, SENTS), jnp.int32), pltpu.SemaphoreType.DMA((n_sems,))],
        compiler_params=pltpu.CompilerParams(vmem_limit_bytes=VMEM_LIMIT),
        cost_estimate=pl.CostEstimate(flops=flops, bytes_accessed=moved, transcendentals=0),
    )(*[a for a, _ in ins.values()])
    return types.SimpleNamespace(**dict(zip(out_names, results)))


ROW, BOTH, FFN = ((T, D), BF), ((2, T, D), BF), ((2, T, FF), BF)
ROW32, TRIPLE = ((T, D), F32), ((T, 3 * D), BF)
RSTD, RSTDS = ((T, WIN), F32), ((2, T, WIN), F32)
PROBS, VEC, MEMKV = ((SENTS, WIN, 2 * T), BF), ((16, D), F32), ((T + 16, 2 * D), BF)
W_IN, W_OUT, W_QKV, W_CROSS, W_SQUARE = ((D, FF), BF), ((FF, D), BF), ((D, 3 * D), BF), ((D, 2 * D), BF), ((D, D), BF)


def twice(kind):
    return ((2,) + kind[0], kind[1])


def at_hand(w):
    return types.SimpleNamespace(**{n: (a, SMEM if n == "lens" else VMEM if a.ndim < 3 or a.shape[1] < 8 else HERE) for n, a in vars(w).items()})


def is_encoder():
    return lax.axis_index("section") == 0


def gains(r):
    return [r.gain[0, j : j + 1, :].astype(F32) for j in range(2)]


def biases(r):
    return [r.bias[0, j : j + 1, :].astype(F32) for j in range(2)]


def first(r):
    enc = is_encoder()
    dec = jnp.logical_not(enc)
    cp = Copies(r.sems)
    load = cp.table(
        x=(r.tok.at[0], r.v_low.at[0]),
        qkv=(r.w_qkv.at[0], r.v_wqkv),
        so=(r.w_so.at[0], r.v_wso),
        fin=(r.w_fin.at[0], r.v_fin),
        fout=(r.w_fout.at[0], r.v_fout),
        cq=(r.w_cross.at[0, :, :D], r.v_cross),
    )
    load.x.start()
    load.qkv.start()
    load.so.start()

    @pl.when(enc)
    def _():
        load.fin.start()
        load.fout.start()

    @pl.when(dec)
    def _():
        load.cq.start()

    prepare(r.lens, r.starts)
    lim = jnp.where(enc, 4 * T, 0)
    r.v_att[...] = jnp.zeros(r.v_att.shape, BF)
    load.x.wait()
    r.v_x[...] = r.v_low[0].astype(F32)
    gain, bias = gains(r), biases(r)
    self_slots, ffn_slots = cp.slots(12), cp.slots(8)

    def self_copies(i):
        pairs = (
            (r.v_qkv, r.qkv), (r.v_probs, r.probs), (r.v_att, r.att), (r.v_xh1, r.xh1), (r.v_rs1, r.rs1),
            (r.v_hlow, r.hlow),
        )
        return [cp.make(a.at[i], b.at[i], self_slots + 2 * n + i) for n, (a, b) in enumerate(pairs)]

    def ffn_copies(i):
        pairs = ((r.v_z, r.z), (r.v_gd, r.gd), (r.v_xh2, r.xh2), (r.v_rs2, r.rs2))
        return [cp.make(a.at[i], b.at[i], ffn_slots + 2 * n + i) for n, (a, b) in enumerate(pairs)]

    @pl.loop(0, REPEATS)
    def _(i):
        @pl.when(i == 0)
        def _():
            load.qkv.wait()
            load.so.wait()

        @pl.when(jnp.logical_or(enc, i == 0))
        def _():
            self_forward(
                r.v_x, r.v_low.at[i], r.v_wqkv, r.v_wso, r.v_qkv.at[i], r.v_att.at[i], r.v_probs.at[i],
                r.v_xh1.at[i], r.v_rs1.at[i], gain[0], bias[0], r.v_h, r.v_hlow.at[i], r.lens, r.starts,
                lax.axis_index("section"), lim,
            )
            for c in self_copies(i):
                c.start()

        @pl.when(jnp.logical_and(enc, i == 0))
        def _():
            load.fin.wait()
            load.fout.wait()

        @pl.when(enc)
        def _():
            ffn_forward(
                r.v_h, r.v_hlow.at[i], r.v_fin, r.b_in, r.v_fout, r.b_out, r.v_z.at[i], r.v_gd.at[i],
                r.v_xh2.at[i], r.v_rs2.at[i], gain[1], bias[1], r.v_x, r.v_low.at[i + 1],
            )
            for c in ffn_copies(i):
                c.start()

    dec_out = cp.table(h=(r.v_h, r.h), cq=(r.v_cq, r.cq))
    enc_out = cp.table(x1=(r.v_low.at[1], r.x1low), mem=(r.v_low.at[2], r.mem))

    @pl.when(dec)
    def _():
        load.cq.wait()
        r.v_cq[...] = nn(r.v_hlow[0], r.v_cross[...]).astype(BF)
        for c in every(dec_out):
            c.start()
        for c in self_copies(0) + every(dec_out):
            c.wait()

    @pl.when(enc)
    def _():
        for c in every(enc_out):
            c.start()
        for i in range(REPEATS):
            for c in self_copies(i) + ffn_copies(i):
                c.wait()
        for c in every(enc_out):
            c.wait()


def first_phase(w):
    saved = dict(
        qkv=twice(TRIPLE), probs=twice(PROBS), att=BOTH, xh1=BOTH, rs1=RSTDS, hlow=BOTH, z=FFN, gd=FFN, xh2=BOTH,
        rs2=RSTDS, h=ROW32, cq=ROW,
    )
    scratch = dict(saved, low=((3, T, D), BF), wqkv=W_QKV, wso=W_SQUARE, fin=W_IN, fout=W_OUT, cross=W_SQUARE, x=ROW32)
    ins = dict(
        lens=w.lens, tok=w.tok, w_qkv=w.w_qkv, w_so=w.w_so, w_fin=w.w_fin, w_fout=w.w_fout, w_cross=w.w_cross,
        b_in=w.b_in, b_out=w.b_out, gain=w.gain, bias=w.bias,
    )
    return phase(first, ins, dict(saved, x1low=ROW, mem=ROW), scratch, 16 * 10**9)


def middle(r):
    @pl.when(jnp.logical_not(is_encoder()))
    def _():
        cp = Copies(r.sems)
        load = cp.table(
            cq=(r.cq, r.v_cq.at[0]),
            h=(r.h, r.v_h),
            cross=(r.w_cross.at[0], r.v_cross),
            fin=(r.w_fin.at[0], r.v_fin),
            fout=(r.w_fout.at[0], r.v_fout),
            qkv=(r.w_qkv.at[0], r.v_wqkv),
            so=(r.w_so.at[0], r.v_wso),
            og=(r.og, r.v_og),
        )
        for c in every(load):
            c.start()
        prepare(r.lens, r.starts)
        gain, bias = gains(r), biases(r)
        cgain, cbias = r.cgain[...].astype(F32), r.cbias[...].astype(F32)
        for ref in (r.v_vec, r.v_gkv, r.v_catt, r.v_att1, r.v_dcq, r.v_dqkv1):
            ref[...] = jnp.zeros(ref.shape, ref.dtype)
        for c in range(2):
            cols = slice(c * D, (c + 1) * D)
            r.v_mkv[:, cols] = nn(r.mem[...], r.w_c0[0, :, cols]).astype(BF)
        load.cq.wait()
        load.h.wait()
        load.cross.wait()
        saved = (
            (r.v_h1low1, r.h1low1), (r.v_x1low, r.x1low), (r.v_att1, r.att1), (r.v_h2low, r.h2low),
            (r.v_catt, r.catt), (r.v_z, r.z), (r.v_declow, r.decoded),
        )
        early = [cp.make(a, b) for a, b in saved]

        @pl.loop(0, REPEATS)
        def _(i):
            @pl.when(i == 1)
            def _():
                load.qkv.wait()
                load.so.wait()
                self_forward(
                    r.v_x, r.v_x1low, r.v_wqkv, r.v_wso, r.v_qkv1, r.v_att1, r.v_probs1, r.v_xh1, r.v_rs1,
                    gain[0], bias[0], r.v_h, r.v_h1low1, r.lens, r.starts, 1, 0,
                )
                r.v_cq[1] = nn(r.v_h1low1[...], r.v_cross[:, :D]).astype(BF)

            attend(
                r.v_cq.at[i], 0, r.v_mkv, 0, r.v_mkv, D, r.v_catt.at[i], r.v_probsc.at[i], r.lens, r.starts, 1, 0,
                None,
            )
            for rows in chunks():
                v = r.v_h[rows, :] + nn(r.v_catt.at[i][rows, :], r.v_cross[:, D:])
                norm_out(v, rows, r.v_xhc.at[i], r.v_rsc.at[i], cgain, cbias, r.v_h2, r.v_h2low.at[i])

            @pl.when(i == 0)
            def _():
                load.fin.wait()
                load.fout.wait()

            ffn_forward(
                r.v_h2, r.v_h2low.at[i], r.v_fin, r.b_in, r.v_fout, r.b_out, r.v_z.at[i], r.v_gdu.at[i],
                r.v_xh2.at[i], r.v_rs2.at[i], gain[1], bias[1], r.v_x, r.v_declow,
            )

            @pl.when(i == 0)
            def _():
                r.v_x1low[...] = r.v_declow[...]

        for c in early:
            c.start()
        load.og.wait()
        r.v_x[...] = r.v_og[...].astype(F32)

        @pl.loop(0, REPEATS)
        def _(j):
            i = 1 - j
            ffn_backward(
                r.v_x, r.v_xh2.at[i], r.v_rs2.at[i], gain[1], r.v_vec, r.v_dz.at[i], r.v_gdu.at[i], r.v_fin, r.v_fout
            )
            norm_backward(r.v_x, r.v_xhc.at[i], r.v_rsc.at[i], cgain, r.v_dc.at[i], r.v_vec, 9, 10)
            r.v_tmp[...] = nt(r.v_dc[i], r.v_cross[:, D:]).astype(BF)
            attend_backward(
                r.v_cq.at[i], 0, r.v_mkv, 0, r.v_mkv, D, r.v_probsc.at[i], r.v_tmp, (r.v_dcq.at[i], 0),
                (r.v_gkv, 0, D), r.lens, r.starts, 1, 0,
            )

            @pl.when(i == 1)
            def _():
                for rows in chunks():
                    r.v_x[rows, :] += nt(r.v_dcq.at[i][rows, :], r.v_cross[:, :D])
                self_backward(
                    r.v_x, r.v_xh1, r.v_rs1, gain[0], r.v_vec, r.v_da1, r.v_wso, r.v_tmp, r.v_qkv1, r.v_probs1,
                    r.v_dqkv1, r.v_wqkv, r.lens, r.starts, 1,
                )

        r.v_gkvlow[:T, :] = r.v_gkv[...].astype(BF)
        r.v_gkvlow[T:, :] = jnp.concatenate(
            [jnp.concatenate([r.v_vec[9:10, :], r.v_vec[10:11, :]], 1), jnp.zeros((15, 2 * D), F32)], 0
        ).astype(BF)
        r.v_gmem[...] = nt(r.v_gkvlow[:T, :], r.w_c0[0]).astype(BF)
        saved = (
            (r.v_gmem, r.gmem), (r.v_gkvlow, r.gkv), (r.v_gdu, r.du), (r.v_dz, r.dz), (r.v_dc, r.dc),
            (r.v_dcq, r.dcq), (r.v_da1, r.da1), (r.v_dqkv1, r.dqkv1), (r.v_x, r.dh), (r.v_vec, r.vec),
        )
        late = [cp.make(a, b) for a, b in saved]
        for c in late:
            c.start()
        for c in early + late:
            c.wait()


def middle_phase(w, one, mem, w_c0):
    outs = dict(
        gmem=ROW, gkv=MEMKV, decoded=ROW, z=FFN, du=FFN, h2low=BOTH, catt=BOTH, h1low1=ROW, dz=BOTH, dc=BOTH, dcq=BOTH,
        att1=ROW, x1low=ROW, da1=ROW, dqkv1=TRIPLE, dh=ROW32, vec=VEC,
    )
    scratch = dict(
        cq=BOTH, h=ROW32, cross=W_CROSS, fin=W_IN, fout=W_OUT, wqkv=W_QKV, wso=W_SQUARE, og=ROW, vec=VEC,
        gkv=((T, 2 * D), F32), catt=BOTH, att1=ROW, dcq=BOTH, dqkv1=TRIPLE, mkv=((T, 2 * D), BF), h1low1=ROW,
        x1low=ROW, h2low=BOTH, z=FFN, declow=ROW, x=ROW32, qkv1=TRIPLE, probs1=PROBS, xh1=ROW, rs1=RSTD,
        probsc=twice(PROBS), xhc=BOTH, rsc=RSTDS, h2=ROW32, gdu=FFN, xh2=BOTH, rs2=RSTDS, dz=BOTH, dc=BOTH, tmp=ROW,
        da1=ROW, gkvlow=MEMKV, gmem=ROW,
    )
    ins = dict(
        lens=w.lens, mem=(mem, VMEM), w_c0=(w_c0, VMEM), cq=(one.cq, HERE), h=(one.h, HERE), og=(w.og[0], HERE),
        w_qkv=w.w_qkv, w_so=w.w_so, w_fin=w.w_fin, w_fout=w.w_fout, w_cross=w.w_cross, b_in=w.b_in, b_out=w.b_out,
        gain=w.gain, bias=w.bias, cgain=w.cgain, cbias=w.cbias,
    )
    return phase(middle, ins, outs, scratch, 30 * 10**9)


PIECES = 16
X_FIRST, Z_FIRST = (0, 1, 2, 3), (0, 2, 3, 1)
SUM_A, SUM_B, SUM_C, SUM_Q = X_FIRST, Z_FIRST, X_FIRST, X_FIRST
OUT_A, OUT_B, OUT_C, OUT_Q = X_FIRST, X_FIRST, Z_FIRST, X_FIRST
ROWS_A = ROWS_B = 512
ROWS_C, ROWS_Q = 32 * 12 + 16, 32 * 12


def place_of(piece, order):
    relative = piece ^ (lax.axis_index("dp") % PIECES)
    place = jnp.int32(0)
    for n, bit in enumerate(order):
        place = place + ((relative >> bit) & 1) * (1 << (3 - n))
    return place


def piece_at(place, order):
    relative = 0
    for n, bit in enumerate(order):
        relative += ((place >> (3 - n)) & 1) << bit
    return relative ^ (lax.axis_index("dp") % PIECES)


def put(dst, order, block, first_row, first_col, high):
    height, width = block.shape
    for j in range(0, height, high):
        place = place_of((first_row + j) // high, order)
        for c in range(0, width, WIN):
            at = ((first_col + c) // WIN) * high
            dst[place, at : at + high, :] = block[j : j + high, c : c + WIN].astype(BF)


def split_out(cp, ref, keep, send):
    made = [cp.make(ref.at[:8], keep), cp.make(ref.at[8:], send)]
    for c in made:
        c.start()
    return made


def third(r):
    enc = is_encoder()
    cp = Copies(r.sems)
    load = cp.table(
        xh2=(r.xh2, r.v_xh2),
        rs2=(r.rs2, r.v_rs2),
        fout=(r.w_fout.at[0], r.v_fout),
        gd=(r.gd, r.v_gdu),
        fin=(r.w_fin.at[0], r.v_fin),
        xh1=(r.xh1.at[1], r.v_xh1),
        rs1=(r.rs1.at[1], r.v_rs1),
        so=(r.w_so.at[0], r.v_wso),
        qkv=(r.qkv.at[1], r.v_qkv1),
        probs=(r.probs.at[1], r.v_probs1),
        wqkv=(r.w_qkv.at[0], r.v_wqkv),
        z=(r.z, r.v_z),
        hlow=(r.hlow, r.v_hlow),
    )
    saved = ((r.v_x, r.dh), (r.v_da1, r.da1), (r.v_dqkv1, r.dqkv1), (r.v_vec, r.vec))
    out = [cp.make(a, b) for a, b in saved]

    @pl.when(enc)
    def _():
        for c in every(load):
            c.start()
        prepare(r.lens, r.starts)
        gain = gains(r)
        r.v_vec[...] = jnp.zeros(r.v_vec.shape, F32)
        r.v_dqkv1[...] = jnp.zeros(r.v_dqkv1.shape, BF)
        r.v_x[...] = r.gmem[...].astype(F32)
        for c in (load.xh2, load.rs2, load.fout, load.gd, load.fin):
            c.wait()

        @pl.loop(0, REPEATS)
        def _(j):
            i = 1 - j
            ffn_backward(
                r.v_x, r.v_xh2.at[i], r.v_rs2.at[i], gain[1], r.v_vec, r.v_dz.at[i], r.v_gdu.at[i], r.v_fin, r.v_fout
            )

            @pl.when(i == 1)
            def _():
                for c in (load.xh1, load.rs1, load.so, load.qkv, load.probs, load.wqkv):
                    c.wait()
                self_backward(
                    r.v_x, r.v_xh1, r.v_rs1, gain[0], r.v_vec, r.v_da1, r.v_wso, r.v_tmp, r.v_qkv1, r.v_probs1,
                    r.v_dqkv1, r.v_wqkv, r.lens, r.starts, 0,
                )

        for c in out:
            c.start()
        load.z.wait()
        load.hlow.wait()

    dec_load = cp.table(z=(r.z_d, r.v_z), du=(r.du_d, r.v_gdu), h=(r.h2low_d, r.v_hlow), dz=(r.dz_d, r.v_dz))

    @pl.when(jnp.logical_not(enc))
    def _():
        for c in every(dec_load):
            c.start()
        for c in every(dec_load):
            c.wait()

    hidden, grad_out = rows_of(r.v_hlow), rows_of(r.v_dz)
    for c in range(4):
        cols = slice(c * D, (c + 1) * D)
        put(r.v_a, SUM_A, tn(hidden, r.v_gdu[:, :, cols].reshape(2 * T, D)), 0, c * D, 32)
    sends = split_out(cp, r.v_a, r.a_keep, r.a_send)
    for c in range(4):
        cols = slice(c * D, (c + 1) * D)
        put(r.v_b, SUM_B, tn(r.v_z[:, :, cols].reshape(2 * T, D), grad_out), c * D, 0, 128)
    sends += split_out(cp, r.v_b, r.b_keep, r.b_send)
    for c in sends:
        c.wait()

    @pl.when(enc)
    def _():
        for c in out:
            c.wait()


def third_phase(w, one, two, gmem):
    half_a, half_b = ((8, ROWS_A, WIN), BF), ((8, ROWS_B, WIN), BF)
    outs = dict(dh=ROW32, da1=ROW, dqkv1=TRIPLE, vec=VEC, a_keep=half_a, a_send=half_a, b_keep=half_b, b_send=half_b)
    scratch = dict(
        xh2=BOTH, rs2=RSTDS, fout=W_OUT, gdu=FFN, fin=W_IN, xh1=ROW, rs1=RSTD, wso=W_SQUARE, qkv1=TRIPLE, probs1=PROBS,
        wqkv=W_QKV, z=FFN, hlow=BOTH, x=ROW32, da1=ROW, dqkv1=TRIPLE, vec=VEC, dz=BOTH, tmp=ROW,
        a=((PIECES, ROWS_A, WIN), BF), b=((PIECES, ROWS_B, WIN), BF),
    )
    ins = dict(lens=w.lens, gmem=(gmem, VMEM), w_qkv=w.w_qkv, w_so=w.w_so, w_fin=w.w_fin, w_fout=w.w_fout, gain=w.gain)
    more = dict(
        xh2=one.xh2, rs2=one.rs2, gd=one.gd, xh1=one.xh1, rs1=one.rs1, qkv=one.qkv, probs=one.probs, z=one.z,
        hlow=one.hlow, z_d=two.z, du_d=two.du, h2low_d=two.h2low, dz_d=two.dz,
    )
    ins.update({n: (a, HERE) for n, a in more.items()})
    return phase(third, ins, outs, scratch, 25 * 10**9)


def fourth(r):
    enc = is_encoder()
    dec = jnp.logical_not(enc)
    cp = Copies(r.sems)
    first_slot = cp.slots(6)

    def own(encoder):
        pairs = (
            (r.dh_e if encoder else r.dh_d, r.v_x),
            (r.vec_e if encoder else r.vec_d, r.v_vec),
            (r.da1_e if encoder else r.da1_d, r.v_da.at[1]),
            (r.att.at[1] if encoder else r.att1_d, r.v_att.at[1]),
        )
        return [cp.make(a, b, first_slot + n) for n, (a, b) in enumerate(pairs)]

    load = cp.table(
        xh1=(r.xh1.at[0], r.v_xh1),
        rs1=(r.rs1.at[0], r.v_rs1),
        att=(r.att.at[0], r.v_att.at[0]),
    )
    enc_cross = cp.table(mem=(r.mem, r.v_one.at[0]))
    dec_cross = cp.table(
        cross=(r.w_cross.at[0, :, :D], r.v_cross),
        h0=(r.hlow.at[0], r.v_one.at[0]),
        h1=(r.h1low1, r.v_one.at[1]),
        att=(r.catt, r.v_two),
        dc=(r.dc, r.v_dc),
        dcq=(r.dcq, r.v_dcq),
        layer=(r.decoded, r.v_layer),
    )
    gain = gains(r)

    @pl.when(enc)
    def _():
        for c in own(True) + every(enc_cross):
            c.start()

    @pl.when(dec)
    def _():
        for c in own(False) + every(dec_cross):
            c.start()

    for c in every(load):
        c.start()
    for c in own(True) + every(load):
        c.wait()

    @pl.when(dec)
    def _():
        dec_cross.cross.wait()
        dec_cross.dcq.wait()
        for rows in chunks():
            r.v_x[rows, :] += nt(r.v_dcq.at[0][rows, :], r.v_cross[...])

    norm_backward(r.v_x, r.v_xh1, r.v_rs1, gain[0], r.v_da.at[0], r.v_vec, 5, 7)
    out = cp.table(x=(r.v_x, r.ds), da=(r.v_da.at[0], r.da0))
    for c in every(out):
        c.start()
    layer_slot = cp.slots()
    enc_layer = cp.make(r.v_one.at[0], r.layer.at[0], layer_slot)
    dec_layer = cp.make(r.v_layer, r.layer.at[0], layer_slot)
    put(r.v_c, SUM_C, tn(rows_of(r.v_att), rows_of(r.v_da)), 0, 0, 32)

    @pl.when(enc)
    def _():
        enc_cross.mem.wait()
        enc_layer.start()
        for c in range(2):
            cols = slice(c * D, (c + 1) * D)
            put(r.v_c, SUM_C, tn(r.v_one[0], r.gkv[:T, cols]), 0, D + c * D, 32)
        tail = r.gkv[T:, :].astype(F32)
        r.v_vec[9:10, :] = tail[0:1, :D]
        r.v_vec[10:11, :] = tail[0:1, D:]

    @pl.when(dec)
    def _():
        dec_cross.layer.wait()
        dec_layer.start()
        for c in (dec_cross.h0, dec_cross.h1, dec_cross.att, dec_cross.dc):
            c.wait()
        put(r.v_c, SUM_C, tn(rows_of(r.v_one), rows_of(r.v_dcq)), 0, D, 32)
        put(r.v_c, SUM_C, tn(rows_of(r.v_two), rows_of(r.v_dc)), 0, 2 * D, 32)

    for p in range(PIECES):
        line = r.v_vec[p : p + 1, :]
        tile = [line[:, j * WIN : (j + 1) * WIN] for j in range(4)] + [jnp.zeros((12, WIN), F32)]
        r.v_c[place_of(p, SUM_C), ROWS_C - 16 :, :] = jnp.concatenate(tile, 0).astype(BF)
    for c in split_out(cp, r.v_c, r.c_keep, r.c_send) + every(out) + [enc_layer]:
        c.wait()


def fourth_phase(w, one, two, three, gkv):
    half_c = ((8, ROWS_C, WIN), BF)
    outs = dict(layer=((1, T, D), BF), ds=ROW32, da0=ROW, c_keep=half_c, c_send=half_c)
    scratch = dict(
        xh1=ROW, rs1=RSTD, att=BOTH, x=ROW32, vec=VEC, da=BOTH, one=BOTH, two=BOTH, dc=BOTH, dcq=BOTH, cross=W_SQUARE,
        layer=ROW, c=((PIECES, ROWS_C, WIN), BF),
    )
    ins = dict(gkv=(gkv, VMEM), gain=w.gain, w_cross=w.w_cross)
    more = dict(
        xh1=one.xh1, rs1=one.rs1, att=one.att, mem=one.mem, hlow=one.hlow, dh_e=three.dh, vec_e=three.vec,
        da1_e=three.da1, dh_d=two.dh, vec_d=two.vec, da1_d=two.da1, att1_d=two.att1, h1low1=two.h1low1, catt=two.catt,
        dc=two.dc, dcq=two.dcq, decoded=two.decoded,
    )
    ins.update({n: (a, HERE) for n, a in more.items()})
    return phase(fourth, ins, outs, scratch, 4 * 10**9)


def fifth(r):
    enc = is_encoder()
    cp = Copies(r.sems)
    first_slot = cp.slots(2)

    def own(encoder):
        pairs = (
            (r.dqkv1_e if encoder else r.dqkv1_d, r.v_dqkv.at[1]),
            (r.x1low_e if encoder else r.x1low_d, r.v_low.at[1]),
        )
        return [cp.make(a, b, first_slot + n) for n, (a, b) in enumerate(pairs)]

    load = cp.table(
        da=(r.da0, r.v_da),
        so=(r.w_so.at[0], r.v_wso),
        qkv=(r.qkv.at[0], r.v_qkv),
        probs=(r.probs.at[0], r.v_probs),
        x=(r.ds, r.v_x),
        wqkv=(r.w_qkv.at[0], r.v_wqkv),
        low=(r.tok.at[0], r.v_low.at[0]),
    )
    for c in every(load):
        c.start()

    @pl.when(enc)
    def _():
        for c in own(True):
            c.start()

    @pl.when(jnp.logical_not(enc))
    def _():
        for c in own(False):
            c.start()

    prepare(r.lens, r.starts)
    r.v_dqkv[0] = jnp.zeros(r.v_dqkv.shape[1:], BF)
    for c in every(load) + own(True):
        c.wait()
    self_tail(
        r.v_x, r.v_da, r.v_wso, r.v_tmp, r.v_qkv, r.v_probs, r.v_dqkv.at[0], r.v_wqkv, r.lens, r.starts,
        lax.axis_index("section"),
    )
    made = [cp.make(r.v_x, r.rows.at[0])]
    made[0].start()
    inputs, grads = rows_of(r.v_low), rows_of(r.v_dqkv)
    for c in range(3):
        cols = slice(c * D, (c + 1) * D)
        put(r.v_q, SUM_Q, tn(inputs, grads[:, cols]), 0, c * D, 32)
    for c in made + split_out(cp, r.v_q, r.q_keep, r.q_send):
        c.wait()


def fifth_phase(w, one, two, three, four, before):
    half_q = ((8, ROWS_Q, WIN), BF)
    outs = dict(rows=((1, T, D), F32), q_keep=half_q, q_send=half_q)
    scratch = dict(
        wso=W_SQUARE, qkv=TRIPLE, probs=PROBS, wqkv=W_QKV, low=BOTH, x=ROW32, da=ROW, dqkv=twice(TRIPLE), tmp=ROW,
        q=((PIECES, ROWS_Q, WIN), BF),
    )
    ins = dict(lens=w.lens, tok=w.tok, w_qkv=w.w_qkv, w_so=w.w_so)
    more = dict(
        qkv=one.qkv, probs=one.probs, x1low_e=one.x1low, x1low_d=two.x1low, dqkv1_e=three.dqkv1, dqkv1_d=two.dqkv1,
        ds=four.ds, da0=four.da0,
    )
    ins.update({n: (a, HERE) for n, a in more.items()})
    ins.update({"before%d" % n: (a, VMEM) for n, a in enumerate(before)})
    return phase(fifth, ins, outs, scratch, 8 * 10**9)


def across(value, bit):
    pairs = [(i, i ^ (1 << bit)) for i in range(lax.axis_size("dp"))]
    return lax.ppermute(value, "dp", pairs)


def added(a, b):
    return (a.astype(F32) + b.astype(F32)).astype(BF)


class Chain:
    def __init__(self, keep, send, scatter, gather):
        self.keep, self.send = keep, send
        self.scatter, self.gather = list(scatter), list(reversed(gather))
        self.result = None
        self.start()

    def start(self):
        if self.scatter:
            self.got = across(self.send, self.scatter[0])
        elif self.gather:
            self.got = across(self.keep, self.gather[0])

    def finish(self):
        keep, got = self.keep, self.got
        if self.scatter:
            self.scatter.pop(0)
            half = keep.shape[0] // 2
            if half:
                self.keep, self.send = added(keep[:half], got[:half]), added(keep[half:], got[half:])
            else:
                self.keep = added(keep, got)
                bit = 4
                while (1 << bit) < lax.axis_size("dp"):
                    self.keep = added(self.keep, across(self.keep, bit))
                    bit += 1
        else:
            self.gather.pop(0)
            if self.gather:
                self.keep = jnp.concatenate([keep, got], 0)
            else:
                self.result = (keep, got)

    def run(self):
        while self.result is None:
            self.finish()
            self.start()


def advance(chains, *others):
    got = lax.optimization_barrier(tuple(c.got for c in chains) + others)
    for c, g in zip(chains, got):
        c.got = g
        c.finish()
        c.start()
    return got[len(chains) :]


def unpack(kernel, ins, scratch, outs):
    return pl.pallas_call(
        kernel,
        name=kernel.__name__,
        in_specs=[pl.BlockSpec(memory_space=VMEM)] * len(ins),
        out_specs=[pl.BlockSpec(memory_space=HERE if big else VMEM) for _, big in outs],
        out_shape=[jax.ShapeDtypeStruct(s, F32) for s, _ in outs],
        scratch_shapes=[VMEM(s, F32) for s in scratch] + [pltpu.SemaphoreType.DMA((len(scratch), PIECES))],
        compiler_params=pltpu.CompilerParams(vmem_limit_bytes=VMEM_LIMIT),
        cost_estimate=pl.CostEstimate(flops=4 * 10**9, bytes_accessed=12 * 10**6, transcendentals=0),
    )(*ins)


def pieces_out(halves, order, high, first, wide, out, whole, sems):
    made = []
    for place in range(PIECES):
        ref, at = halves[place // 8], place % 8
        rows = pl.ds(pl.multiple_of(piece_at(place, order) * high, high), high)
        for c in range(wide // WIN):
            start = first + c * high
            whole[rows, c * WIN : (c + 1) * WIN] = ref[at, start : start + high, :].astype(F32)
        made.append(pltpu.make_async_copy(whole.at[rows, :], out.at[0, rows, :], sems.at[place]))
        made[-1].start()
    return made


def unpack_in(a0, a1, fin, v_fin, sems):
    for c in pieces_out((a0, a1), OUT_A, 32, 0, FF, fin, v_fin, sems.at[0]):
        c.wait()


def unpack_out(b0, b1, fout, v_fout, sems):
    for c in pieces_out((b0, b1), OUT_B, 128, 0, D, fout, v_fout, sems.at[0]):
        c.wait()


def unpack_qkv(q0, q1, qkv, v_qkv, sems):
    for c in pieces_out((q0, q1), OUT_Q, 32, 0, 3 * D, qkv, v_qkv, sems.at[0]):
        c.wait()


def unpack_rest(c0, c1, so, cross, b_in, b_out, gain, bias, cgain, cbias, v_so, v_cross, sems):
    made = pieces_out((c0, c1), OUT_C, 32, 0, D, so, v_so, sems.at[0])
    made += pieces_out((c0, c1), OUT_C, 32, 4 * 32, 2 * D, cross, v_cross, sems.at[1])

    def line(p):
        place = place_of(p, OUT_C)
        at = place % 8
        tail = jnp.where(place < 8, c0[at, ROWS_C - 16 :, :].astype(F32), c1[at, ROWS_C - 16 :, :].astype(F32))
        return jnp.concatenate([tail[j : j + 1, :] for j in range(4)], 1)

    for n in range(4):
        b_in[:, n * D : (n + 1) * D] = line(n)
    b_out[...] = line(4)
    for n in range(2):
        gain[0, n : n + 1, :] = line(5 + n)
        bias[0, n : n + 1, :] = line(7 + n)
    cgain[...] = line(9)
    cbias[...] = line(10)
    for c in made:
        c.wait()


def body(
    token_rows, lengths, self_qkv, self_out, ffn_in, ffn_in_bias, ffn_out, ffn_out_bias, norm_gain, norm_bias,
    cross_weights, cross_gain, cross_bias, output_grad,
):
    to_decoder, to_encoder = [(0, 1)], [(1, 0)]
    w = at_hand(
        types.SimpleNamespace(
            tok=token_rows, lens=lengths, w_qkv=self_qkv, w_so=self_out, w_fin=ffn_in, b_in=ffn_in_bias, w_fout=ffn_out,
            b_out=ffn_out_bias, gain=norm_gain, bias=norm_bias, w_cross=cross_weights, cgain=cross_gain.reshape(1, D),
            cbias=cross_bias.reshape(1, D), og=output_grad,
        )
    )
    w_c0 = lax.ppermute(cross_weights, "section", to_decoder)
    one = first_phase(w)
    mem = lax.ppermute(one.mem, "section", to_decoder)
    two = middle_phase(w, one, mem, w_c0)
    gmem = lax.ppermute(two.gmem, "section", to_encoder)
    gkv = lax.ppermute(two.gkv, "section", to_encoder)
    three = third_phase(w, one, two, gmem)
    four = fourth_phase(w, one, two, three, gkv)
    a = Chain(three.a_keep, three.a_send, SUM_A, OUT_A)
    b = Chain(three.b_keep, three.b_send, SUM_B, OUT_B)
    advance([a, b])
    c = Chain(four.c_keep, four.c_send, SUM_C, OUT_C)
    five = fifth_phase(w, one, two, three, four, (a.send, b.send))
    (q_send,) = advance([a, b, c], five.q_send)
    q = Chain(five.q_keep, q_send, SUM_Q, OUT_Q)
    for chain in (q, c, a, b):
        chain.run()
    (g_qkv,) = unpack(unpack_qkv, q.result, [(D, 3 * D)], [((1, D, 3 * D), True)])
    (g_fin,) = unpack(unpack_in, a.result, [(D, FF)], [((1, D, FF), True)])
    (g_fout,) = unpack(unpack_out, b.result, [(FF, D)], [((1, FF, D), True)])
    small = [(1, FF), (1, D), (1, 2, D), (1, 2, D), (1, D), (1, D)]
    g_so, g_cross, g_bin, g_bout, g_gain, g_bias, g_cgain, g_cbias = unpack(
        unpack_rest,
        c.result,
        [(D, D), (D, 2 * D)],
        [((1, D, D), True), ((1, D, 2 * D), True)] + [(shape, False) for shape in small],
    )
    return (
        four.layer, five.rows, g_qkv, g_so, g_fin, g_bin, g_fout, g_bout, g_gain, g_bias, g_cross, g_cgain.reshape(D),
        g_cbias.reshape(D),
    )


def solution(mesh):
    by_section = P("section")
    in_specs = (
        P("section", "dp"), P("dp"), by_section, by_section, by_section, by_section, by_section, by_section, by_section,
        by_section, by_section, P(), P(), P("dp"),
    )
    out_specs = (P("section", "dp"), P("section", "dp")) + (by_section,) * 9 + (P(), P())
    return jax.shard_map(body, mesh=mesh, in_specs=in_specs, out_specs=out_specs, check_vma=False)
```

```python
import types

import jax
import jax.numpy as jnp
from jax import lax
from jax.experimental import pallas as pl
from jax.experimental.pallas import tpu as pltpu
from jax.sharding import PartitionSpec as P

BF, F32 = jnp.bfloat16, jnp.float32
D, FF, HEAD_DIM, SENTS, REPEATS = 512, 2048, 64, 8, 2
T = 512
WIN = 128
EPSILON = 1e-05
MASKED = -1e9
SCALE = HEAD_DIM**-0.5
LOG2E = 1.4426950408889634
K0 = 0.7978845608028654
K1 = K0 * 0.044715
UNROLL_FORWARD, UNROLL_BACKWARD = 8, 4
VMEM_LIMIT = 60 * 2**20


def nn(a, b):
    return lax.dot_general(a, b, (((1,), (0,)), ((), ())), preferred_element_type=F32)


def nt(a, b):
    return lax.dot_general(a, b, (((1,), (1,)), ((), ())), preferred_element_type=F32)


def tn(a, b):
    return lax.dot_general(a, b, (((0,), (0,)), ((), ())), preferred_element_type=F32)


def iota(axis):
    return lax.broadcasted_iota(jnp.int32, (WIN, WIN), axis)


def halves():
    lane = lax.broadcasted_iota(jnp.int32, (1, WIN), 1)
    even = jnp.where(lane < HEAD_DIM, 1.0, 0.0).astype(BF)
    odd = jnp.where(lane < HEAD_DIM, 0.0, 1.0).astype(BF)
    return even, odd


def wide(ref, rows):
    part = ref[rows, :]
    return jnp.concatenate([part] * (D // WIN), 1)


def chunks(size=256):
    return [slice(i, i + size) for i in range(0, T, size)]


def prepare(lens, starts):
    for side in range(2):
        total = jnp.int32(0)
        for j in range(SENTS):
            starts[side, j] = total
            total = total + lens[0, side, j]


def window(lens, starts, side, s):
    first = starts[side, s]
    base = pl.multiple_of(jnp.minimum((first // 16) * 16, T - WIN), 16)
    return base, first - base, first - base + lens[0, side, s]


def sentences(body, unroll):
    @pl.loop(0, SENTS // unroll)
    def _(j):
        for t in range(unroll):
            body(j * unroll + t)


def attend(q, qc, k, kc, v, vc, out, probs, lens, starts, qside, kside, lim):
    even, odd = halves()
    row, col = iota(0), iota(1)
    line = lax.broadcasted_iota(jnp.int32, (1, WIN), 1)

    def body(s):
        wq, lo, hi = window(lens, starts, qside, s)
        wk, klo, khi = (wq, lo, hi) if kside is qside else window(lens, starts, kside, s)
        valid = (row >= klo) & (row < khi)
        if lim is not None:
            valid = valid & (row - col <= lim)
        mine = (line >= lo) & (line < hi)

        def score(g):
            qs = q[pl.ds(wq, WIN), qc + g * WIN : qc + (g + 1) * WIN]
            ks = k[pl.ds(wk, WIN), kc + g * WIN : kc + (g + 1) * WIN]
            return nt(ks, jnp.concatenate([qs * even, qs * odd], 0))

        def soften(g, scores):
            parts = []
            for h in range(2):
                x = jnp.where(valid, scores[:, h * WIN : (h + 1) * WIN] * (SCALE * LOG2E), MASKED)
                p = jnp.exp2(x - jnp.max(x, 0, keepdims=True))
                inverse = jnp.where(mine, 1.0 / jnp.sum(p, 0, keepdims=True), 0.0)
                parts.append((p * inverse).astype(BF))
            probs[s, :, g * 2 * WIN : (g + 1) * 2 * WIN] = jnp.concatenate(parts, 1)
            return jnp.concatenate(parts, 1)

        def finish(g, turned):
            vs = v[pl.ds(wk, WIN), vc + g * WIN : vc + (g + 1) * WIN]
            place = (pl.ds(wq, WIN), slice(g * WIN, (g + 1) * WIN))
            both = tn(turned, vs)
            out[place] += jnp.where(col < HEAD_DIM, both[:WIN], both[WIN:]).astype(BF)

        for g in range(4):
            finish(g, soften(g, score(g)))

    sentences(body, UNROLL_FORWARD)


def attend_backward(q, qc, k, kc, v, vc, probs, grad, dq, dkv, lens, starts, qside, kside):
    even, odd = halves()
    even_s, odd_s = even * SCALE, odd * SCALE

    def body(s):
        wq, _, _ = window(lens, starts, qside, s)
        wk, _, _ = (wq, 0, 0) if kside is qside else window(lens, starts, kside, s)

        def cut(ref, at, c, g):
            return ref[pl.ds(at, WIN), c + g * WIN : c + (g + 1) * WIN]

        def first_part(g):
            go = cut(grad, wq, 0, g)
            both_g = jnp.concatenate([go * even, go * odd], 0)
            return both_g, nt(cut(v, wk, vc, g), both_g)

        def second_part(g, dp):
            p_low = probs[s, :, g * 2 * WIN : (g + 1) * 2 * WIN]
            p = p_low.astype(F32)
            return p_low, (p * (dp - jnp.sum(p * dp, 0, keepdims=True))).astype(BF)

        def third_part(g, both_g, p_low, ds):
            qs, ks = cut(q, wq, qc, g), cut(k, wk, kc, g)
            dv = nn(p_low, both_g)
            dk = nn(ds, jnp.concatenate([qs * even_s, qs * odd_s], 0))
            turned = jnp.concatenate([ds[:, :WIN].T, ds[:, WIN:].T], 1)
            dqs = nn(turned, jnp.concatenate([ks * even_s, ks * odd_s], 0))
            ref, c = dq
            ref[pl.ds(wq, WIN), c + g * WIN : c + (g + 1) * WIN] += dqs.astype(ref.dtype)
            ref, c_k, c_v = dkv
            for c, value in ((c_k, dk), (c_v, dv)):
                ref[pl.ds(wk, WIN), c + g * WIN : c + (g + 1) * WIN] += value.astype(ref.dtype)

        start = [first_part(g) for g in range(4)]
        middle_part = [second_part(g, start[g][1]) for g in range(4)]
        for g in range(4):
            third_part(g, start[g][0], *middle_part[g])

    sentences(body, UNROLL_BACKWARD)


def normed(v):
    centre = v - jnp.mean(v, -1, keepdims=True)
    rstd = lax.rsqrt(jnp.mean(centre * centre, -1, keepdims=True) + EPSILON)
    return centre * rstd, rstd


def norm_out(v, rows, xh, rs, gain, bias, wide_ref, low_ref):
    xhat, rstd = normed(v)
    xh[rows, :] = xhat.astype(BF)
    rs[rows, :] = jnp.broadcast_to(rstd, (v.shape[0], WIN))
    h = xhat * gain + bias
    wide_ref[rows, :] = h
    low_ref[rows, :] = h.astype(BF)


def norm_backward(dst, xh, rs, gain, low, vec, gain_row, bias_row):
    for rows in chunks():
        dy = dst[rows, :]
        xhat = xh[rows, :].astype(F32)
        rstd = wide(rs, rows)
        prod = dy * xhat
        vec[gain_row : gain_row + 1, :] += jnp.sum(prod, 0, keepdims=True)
        vec[bias_row : bias_row + 1, :] += jnp.sum(dy, 0, keepdims=True)
        scaled = dy * gain
        m1 = jnp.mean(scaled, -1, keepdims=True)
        m2 = jnp.mean(prod * gain, -1, keepdims=True)
        ds = rstd * (scaled - m1 - xhat * m2)
        dst[rows, :] = ds
        low[rows, :] = ds.astype(BF)


def self_forward(x, low, w_qkv, w_out, qkv, att, probs, xh, rs, gain, bias, h, h_low, lens, starts, side, lim):
    for c in range(3):
        cols = slice(c * D, (c + 1) * D)
        qkv[:, cols] = nn(low[...], w_qkv[:, cols]).astype(BF)
    attend(qkv, 0, qkv, D, qkv, 2 * D, att, probs, lens, starts, side, side, lim)
    for rows in chunks():
        norm_out(x[rows, :] + nn(att[rows, :], w_out[...]), rows, xh, rs, gain, bias, h, h_low)


def self_tail(dst, da, w_out, tmp, qkv, probs, dqkv, w_qkv, lens, starts, side):
    tmp[...] = nt(da[...], w_out[...]).astype(BF)
    attend_backward(
        qkv, 0, qkv, D, qkv, 2 * D, probs, tmp, (dqkv, 0), (dqkv, D, 2 * D), lens, starts, side, side
    )
    for rows in chunks():
        dst[rows, :] += nt(dqkv[rows, :], w_qkv[...])


def self_backward(dst, xh, rs, gain, vec, da, w_out, tmp, qkv, probs, dqkv, w_qkv, lens, starts, side):
    norm_backward(dst, xh, rs, gain, da, vec, 5, 7)
    self_tail(dst, da, w_out, tmp, qkv, probs, dqkv, w_qkv, lens, starts, side)


def ffn_forward(h, h_low, w_in, b_in, w_out, b_out, z, gd, xh, rs, gain, bias, out, out_low, between=None):
    for c in range(4):
        cols = slice(c * D, (c + 1) * D)
        u = nn(h_low[...], w_in[:, cols]) + b_in[:, cols].astype(F32)
        square = u * u
        half = 0.5 + 0.5 * jnp.tanh(u * (K0 + K1 * square))
        act = u * half
        z[:, cols] = act.astype(BF)
        gd[:, cols] = (half + act * (1.0 - half) * (2.0 * K0 + 6.0 * K1 * square)).astype(BF)
    if between is not None:
        between()
    for rows in chunks():
        v = h[rows, :] + (nn(z[rows, :], w_out[...]) + b_out[...].astype(F32))
        norm_out(v, rows, xh, rs, gain, bias, out, out_low)


def ffn_backward(dst, xh, rs, gain, vec, dz, gdu, w_in, w_out):
    norm_backward(dst, xh, rs, gain, dz, vec, 6, 8)
    vec[4:5, :] += jnp.sum(dz[...].astype(F32), 0, keepdims=True)
    for c in range(4):
        cols = slice(c * D, (c + 1) * D)
        du = (nt(dz[...], w_out[cols, :]) * gdu[:, cols].astype(F32)).astype(BF)
        gdu[:, cols] = du
        vec[c : c + 1, :] += jnp.sum(du.astype(F32), 0, keepdims=True)
    for rows in chunks():
        dst[rows, :] += nt(gdu[rows, :], w_in[...])


def rows_of(ref):
    return ref[...].reshape(2 * T, ref.shape[-1])


class Copies:
    def __init__(self, sems):
        self.sems, self.used = sems, 0

    def slots(self, count=1):
        first = self.used
        self.used += count
        return first

    def make(self, src, dst, slot=None):
        slot = self.slots() if slot is None else slot
        return pltpu.make_async_copy(src, dst, self.sems.at[slot])

    def table(self, **pairs):
        return types.SimpleNamespace(**{n: self.make(a, b) for n, (a, b) in pairs.items()})


def every(table):
    return list(vars(table).values())


HERE, VMEM, SMEM = pl.ANY, pltpu.VMEM, pltpu.SMEM


def phase(body, ins, outs, scratch, flops, limit=56, n_sems=64):
    in_names, out_names, names = list(ins), list(outs), list(scratch)

    def kernel(*refs):
        labels = in_names + out_names + ["v_" + n for n in names]
        r = types.SimpleNamespace(**dict(zip(labels, refs)))
        r.starts, r.sems = refs[-2:]
        body(r)

    moved = sum(a.size * a.dtype.itemsize for a, _ in ins.values())
    results = pl.pallas_call(
        kernel,
        name=body.__name__,
        in_specs=[pl.BlockSpec(memory_space=s) for _, s in ins.values()],
        out_specs=[pl.BlockSpec(memory_space=HERE)] * len(outs),
        out_shape=[jax.ShapeDtypeStruct(s, d) for s, d in outs.values()],
        scratch_shapes=[VMEM(s, d) for s, d in scratch.values()]
        + [SMEM((2, SENTS), jnp.int32), pltpu.SemaphoreType.DMA((n_sems,))],
        compiler_params=pltpu.CompilerParams(vmem_limit_bytes=limit * 2**20),
        cost_estimate=pl.CostEstimate(flops=flops, bytes_accessed=moved, transcendentals=0),
    )(*[a for a, _ in ins.values()])
    return types.SimpleNamespace(**dict(zip(out_names, results)))


ROW, BOTH, FFN = ((T, D), BF), ((2, T, D), BF), ((2, T, FF), BF)
ROW32, TRIPLE = ((T, D), F32), ((T, 3 * D), BF)
RSTD, RSTDS = ((T, WIN), F32), ((2, T, WIN), F32)
PROBS, VEC, MEMKV = ((SENTS, WIN, 2 * T), BF), ((16, D), F32), ((T + 16, 2 * D), BF)
W_IN, W_OUT, W_QKV, W_CROSS, W_SQUARE = ((D, FF), BF), ((FF, D), BF), ((D, 3 * D), BF), ((D, 2 * D), BF), ((D, D), BF)


def twice(kind):
    return ((2,) + kind[0], kind[1])


def at_hand(w):
    return types.SimpleNamespace(**{n: (a, SMEM if n == "lens" else VMEM if a.ndim < 3 or a.shape[1] < 8 else HERE) for n, a in vars(w).items()})


def is_encoder():
    return lax.axis_index("section") == 0


def gains(r):
    return [r.gain[0, j : j + 1, :].astype(F32) for j in range(2)]


def biases(r):
    return [r.bias[0, j : j + 1, :].astype(F32) for j in range(2)]


def first(r):
    enc = is_encoder()
    dec = jnp.logical_not(enc)
    cp = Copies(r.sems)
    load = cp.table(
        x=(r.tok.at[0], r.v_low.at[0]),
        qkv=(r.w_qkv.at[0], r.v_wqkv),
        so=(r.w_so.at[0], r.v_wso),
        fin=(r.w_fin.at[0], r.v_fin),
        fout=(r.w_fout.at[0], r.v_fout),
        cq=(r.w_cross.at[0, :, :D], r.v_cross),
    )
    load.x.start()
    load.qkv.start()
    load.so.start()

    @pl.when(enc)
    def _():
        load.fin.start()
        load.fout.start()

    @pl.when(dec)
    def _():
        load.cq.start()

    prepare(r.lens, r.starts)
    lim = jnp.where(enc, 4 * T, 0)
    r.v_att[...] = jnp.zeros(r.v_att.shape, BF)
    load.x.wait()
    r.v_x[...] = r.v_low[0].astype(F32)
    gain, bias = gains(r), biases(r)
    self_slots, ffn_slots = cp.slots(12), cp.slots(8)

    def self_copies(i):
        pairs = (
            (r.v_qkv, r.qkv), (r.v_probs, r.probs), (r.v_att, r.att), (r.v_xh1, r.xh1), (r.v_rs1, r.rs1),
            (r.v_hlow, r.hlow),
        )
        return [cp.make(a.at[i], b.at[i], self_slots + 2 * n + i) for n, (a, b) in enumerate(pairs)]

    def ffn_copies(i):
        pairs = ((r.v_z, r.z), (r.v_gd, r.gd), (r.v_xh2, r.xh2), (r.v_rs2, r.rs2))
        return [cp.make(a.at[i], b.at[i], ffn_slots + 2 * n + i) for n, (a, b) in enumerate(pairs)]

    @pl.loop(0, REPEATS)
    def _(i):
        @pl.when(i == 0)
        def _():
            load.qkv.wait()
            load.so.wait()

        @pl.when(jnp.logical_or(enc, i == 0))
        def _():
            self_forward(
                r.v_x, r.v_low.at[i], r.v_wqkv, r.v_wso, r.v_qkv.at[i], r.v_att.at[i], r.v_probs.at[i],
                r.v_xh1.at[i], r.v_rs1.at[i], gain[0], bias[0], r.v_h, r.v_hlow.at[i], r.lens, r.starts,
                lax.axis_index("section"), lim,
            )
            for c in self_copies(i):
                c.start()

        @pl.when(jnp.logical_and(enc, i == 0))
        def _():
            load.fin.wait()
            load.fout.wait()

        @pl.when(enc)
        def _():
            ffn_forward(
                r.v_h, r.v_hlow.at[i], r.v_fin, r.b_in, r.v_fout, r.b_out, r.v_z.at[i], r.v_gd.at[i],
                r.v_xh2.at[i], r.v_rs2.at[i], gain[1], bias[1], r.v_x, r.v_low.at[i + 1],
                lambda: [c.start() for c in ffn_copies(i)[:2]],
            )
            for c in ffn_copies(i)[2:]:
                c.start()

    dec_out = cp.table(h=(r.v_h, r.h), cq=(r.v_cq, r.cq))
    enc_out = cp.table(x1=(r.v_low.at[1], r.x1low), mem=(r.v_low.at[2], r.mem))

    @pl.when(dec)
    def _():
        load.cq.wait()
        r.v_cq[...] = nn(r.v_hlow[0], r.v_cross[...]).astype(BF)
        for c in every(dec_out):
            c.start()
        for c in self_copies(0) + every(dec_out):
            c.wait()

    @pl.when(enc)
    def _():
        for c in every(enc_out):
            c.start()
        for i in range(REPEATS):
            for c in self_copies(i) + ffn_copies(i):
                c.wait()
        for c in every(enc_out):
            c.wait()


def first_phase(w):
    saved = dict(
        qkv=twice(TRIPLE), probs=twice(PROBS), att=BOTH, xh1=BOTH, rs1=RSTDS, hlow=BOTH, z=FFN, gd=FFN, xh2=BOTH,
        rs2=RSTDS, h=ROW32, cq=ROW,
    )
    scratch = dict(saved, low=((3, T, D), BF), wqkv=W_QKV, wso=W_SQUARE, fin=W_IN, fout=W_OUT, cross=W_SQUARE, x=ROW32)
    ins = dict(
        lens=w.lens, tok=w.tok, w_qkv=w.w_qkv, w_so=w.w_so, w_fin=w.w_fin, w_fout=w.w_fout, w_cross=w.w_cross,
        b_in=w.b_in, b_out=w.b_out, gain=w.gain, bias=w.bias,
    )
    return phase(first, ins, dict(saved, x1low=ROW, mem=ROW), scratch, 16 * 10**9)


def middle(r):
    @pl.when(jnp.logical_not(is_encoder()))
    def _():
        cp = Copies(r.sems)
        load = cp.table(
            cq=(r.cq, r.v_cq.at[0]),
            h=(r.h, r.v_h),
            cross=(r.w_cross.at[0], r.v_cross),
            fin=(r.w_fin.at[0], r.v_fin),
            fout=(r.w_fout.at[0], r.v_fout),
            qkv=(r.w_qkv.at[0], r.v_wqkv),
            so=(r.w_so.at[0], r.v_wso),
            og=(r.og, r.v_og),
        )
        for c in every(load):
            c.start()
        prepare(r.lens, r.starts)
        gain, bias = gains(r), biases(r)
        cgain, cbias = r.cgain[...].astype(F32), r.cbias[...].astype(F32)
        for ref in (r.v_vec, r.v_gkv, r.v_catt, r.v_att1, r.v_dcq, r.v_dqkv1):
            ref[...] = jnp.zeros(ref.shape, ref.dtype)
        for c in range(2):
            cols = slice(c * D, (c + 1) * D)
            r.v_mkv[:, cols] = nn(r.mem[...], r.w_c0[0, :, cols]).astype(BF)
        load.cq.wait()
        load.h.wait()
        load.cross.wait()
        saved = (
            (r.v_h1low1, r.h1low1), (r.v_x1low, r.x1low), (r.v_att1, r.att1), (r.v_h2low, r.h2low),
            (r.v_catt, r.catt), (r.v_z, r.z), (r.v_declow, r.decoded),
        )
        early = [cp.make(a, b) for a, b in saved]

        @pl.loop(0, REPEATS)
        def _(i):
            @pl.when(i == 1)
            def _():
                load.qkv.wait()
                load.so.wait()
                self_forward(
                    r.v_x, r.v_x1low, r.v_wqkv, r.v_wso, r.v_qkv1, r.v_att1, r.v_probs1, r.v_xh1, r.v_rs1,
                    gain[0], bias[0], r.v_h, r.v_h1low1, r.lens, r.starts, 1, 0,
                )
                r.v_cq[1] = nn(r.v_h1low1[...], r.v_cross[:, :D]).astype(BF)

            attend(
                r.v_cq.at[i], 0, r.v_mkv, 0, r.v_mkv, D, r.v_catt.at[i], r.v_probsc.at[i], r.lens, r.starts, 1, 0,
                None,
            )
            for rows in chunks():
                v = r.v_h[rows, :] + nn(r.v_catt.at[i][rows, :], r.v_cross[:, D:])
                norm_out(v, rows, r.v_xhc.at[i], r.v_rsc.at[i], cgain, cbias, r.v_h2, r.v_h2low.at[i])

            @pl.when(i == 0)
            def _():
                load.fin.wait()
                load.fout.wait()

            ffn_forward(
                r.v_h2, r.v_h2low.at[i], r.v_fin, r.b_in, r.v_fout, r.b_out, r.v_z.at[i], r.v_gdu.at[i],
                r.v_xh2.at[i], r.v_rs2.at[i], gain[1], bias[1], r.v_x, r.v_declow,
            )

            @pl.when(i == 0)
            def _():
                r.v_x1low[...] = r.v_declow[...]

        for c in early:
            c.start()
        load.og.wait()
        r.v_x[...] = r.v_og[...].astype(F32)

        @pl.loop(0, REPEATS)
        def _(j):
            i = 1 - j
            ffn_backward(
                r.v_x, r.v_xh2.at[i], r.v_rs2.at[i], gain[1], r.v_vec, r.v_dz.at[i], r.v_gdu.at[i], r.v_fin, r.v_fout
            )
            norm_backward(r.v_x, r.v_xhc.at[i], r.v_rsc.at[i], cgain, r.v_dc.at[i], r.v_vec, 9, 10)
            r.v_tmp[...] = nt(r.v_dc[i], r.v_cross[:, D:]).astype(BF)
            attend_backward(
                r.v_cq.at[i], 0, r.v_mkv, 0, r.v_mkv, D, r.v_probsc.at[i], r.v_tmp, (r.v_dcq.at[i], 0),
                (r.v_gkv, 0, D), r.lens, r.starts, 1, 0,
            )

            @pl.when(i == 1)
            def _():
                for rows in chunks():
                    r.v_x[rows, :] += nt(r.v_dcq.at[i][rows, :], r.v_cross[:, :D])
                self_backward(
                    r.v_x, r.v_xh1, r.v_rs1, gain[0], r.v_vec, r.v_da1, r.v_wso, r.v_tmp, r.v_qkv1, r.v_probs1,
                    r.v_dqkv1, r.v_wqkv, r.lens, r.starts, 1,
                )

        r.v_gkvlow[:T, :] = r.v_gkv[...].astype(BF)
        r.v_gkvlow[T:, :] = jnp.concatenate(
            [jnp.concatenate([r.v_vec[9:10, :], r.v_vec[10:11, :]], 1), jnp.zeros((15, 2 * D), F32)], 0
        ).astype(BF)
        r.v_gmem[...] = nt(r.v_gkvlow[:T, :], r.w_c0[0]).astype(BF)
        saved = (
            (r.v_gmem, r.gmem), (r.v_gkvlow, r.gkv), (r.v_gdu, r.du), (r.v_dz, r.dz), (r.v_dc, r.dc),
            (r.v_dcq, r.dcq), (r.v_da1, r.da1), (r.v_dqkv1, r.dqkv1), (r.v_x, r.dh), (r.v_vec, r.vec),
        )
        late = [cp.make(a, b) for a, b in saved]
        for c in late:
            c.start()
        for c in early + late:
            c.wait()


def middle_phase(w, one, mem, w_c0):
    outs = dict(
        gmem=ROW, gkv=MEMKV, decoded=ROW, z=FFN, du=FFN, h2low=BOTH, catt=BOTH, h1low1=ROW, dz=BOTH, dc=BOTH, dcq=BOTH,
        att1=ROW, x1low=ROW, da1=ROW, dqkv1=TRIPLE, dh=ROW32, vec=VEC,
    )
    scratch = dict(
        cq=BOTH, h=ROW32, cross=W_CROSS, fin=W_IN, fout=W_OUT, wqkv=W_QKV, wso=W_SQUARE, og=ROW, vec=VEC,
        gkv=((T, 2 * D), F32), catt=BOTH, att1=ROW, dcq=BOTH, dqkv1=TRIPLE, mkv=((T, 2 * D), BF), h1low1=ROW,
        x1low=ROW, h2low=BOTH, z=FFN, declow=ROW, x=ROW32, qkv1=TRIPLE, probs1=PROBS, xh1=ROW, rs1=RSTD,
        probsc=twice(PROBS), xhc=BOTH, rsc=RSTDS, h2=ROW32, gdu=FFN, xh2=BOTH, rs2=RSTDS, dz=BOTH, dc=BOTH, tmp=ROW,
        da1=ROW, gkvlow=MEMKV, gmem=ROW,
    )
    ins = dict(
        lens=w.lens, mem=(mem, VMEM), w_c0=(w_c0, VMEM), cq=(one.cq, HERE), h=(one.h, HERE), og=(w.og[0], HERE),
        w_qkv=w.w_qkv, w_so=w.w_so, w_fin=w.w_fin, w_fout=w.w_fout, w_cross=w.w_cross, b_in=w.b_in, b_out=w.b_out,
        gain=w.gain, bias=w.bias, cgain=w.cgain, cbias=w.cbias,
    )
    return phase(middle, ins, outs, scratch, 30 * 10**9, 60)


PIECES = 16
X_FIRST, Z_FIRST = (0, 1, 2, 3), (0, 2, 3, 1)
SUM_A, SUM_B, SUM_C, SUM_Q = X_FIRST, Z_FIRST, X_FIRST, X_FIRST
OUT_A, OUT_B, OUT_C, OUT_Q = X_FIRST, X_FIRST, Z_FIRST, X_FIRST
ROWS_A = ROWS_B = 512
ROWS_C, ROWS_Q = 32 * 12 + 16, 32 * 12


def place_of(piece, order):
    relative = piece ^ (lax.axis_index("dp") % PIECES)
    place = jnp.int32(0)
    for n, bit in enumerate(order):
        place = place + ((relative >> bit) & 1) * (1 << (3 - n))
    return place


def piece_at(place, order):
    relative = 0
    for n, bit in enumerate(order):
        relative += ((place >> (3 - n)) & 1) << bit
    return relative ^ (lax.axis_index("dp") % PIECES)


def put(dst, order, block, first_row, first_col, high):
    height, width = block.shape
    for j in range(0, height, high):
        place = place_of((first_row + j) // high, order)
        for c in range(0, width, WIN):
            at = ((first_col + c) // WIN) * high
            dst[place, at : at + high, :] = block[j : j + high, c : c + WIN].astype(BF)


def split_out(cp, ref, keep, send):
    made = [cp.make(ref.at[:8], keep), cp.make(ref.at[8:], send)]
    for c in made:
        c.start()
    return made


def third(r):
    enc = is_encoder()
    cp = Copies(r.sems)
    load = cp.table(
        xh2=(r.xh2, r.v_xh2),
        rs2=(r.rs2, r.v_rs2),
        fout=(r.w_fout.at[0], r.v_fout),
        gd=(r.gd, r.v_gdu),
        fin=(r.w_fin.at[0], r.v_fin),
        xh1=(r.xh1.at[1], r.v_xh1),
        rs1=(r.rs1.at[1], r.v_rs1),
        so=(r.w_so.at[0], r.v_wso),
        qkv=(r.qkv.at[1], r.v_qkv1),
        probs=(r.probs.at[1], r.v_probs1),
        wqkv=(r.w_qkv.at[0], r.v_wqkv),
        z=(r.z, r.v_z),
        hlow=(r.hlow, r.v_hlow),
    )
    saved = ((r.v_x, r.dh), (r.v_da1, r.da1), (r.v_dqkv1, r.dqkv1), (r.v_vec, r.vec))
    out = [cp.make(a, b) for a, b in saved]

    @pl.when(enc)
    def _():
        for c in every(load):
            c.start()
        prepare(r.lens, r.starts)
        gain = gains(r)
        r.v_vec[...] = jnp.zeros(r.v_vec.shape, F32)
        r.v_dqkv1[...] = jnp.zeros(r.v_dqkv1.shape, BF)
        r.v_x[...] = r.gmem[...].astype(F32)
        for c in (load.xh2, load.rs2, load.fout, load.gd, load.fin):
            c.wait()

        @pl.loop(0, REPEATS)
        def _(j):
            i = 1 - j
            ffn_backward(
                r.v_x, r.v_xh2.at[i], r.v_rs2.at[i], gain[1], r.v_vec, r.v_dz.at[i], r.v_gdu.at[i], r.v_fin, r.v_fout
            )

            @pl.when(i == 1)
            def _():
                for c in (load.xh1, load.rs1, load.so, load.qkv, load.probs, load.wqkv):
                    c.wait()
                self_backward(
                    r.v_x, r.v_xh1, r.v_rs1, gain[0], r.v_vec, r.v_da1, r.v_wso, r.v_tmp, r.v_qkv1, r.v_probs1,
                    r.v_dqkv1, r.v_wqkv, r.lens, r.starts, 0,
                )

        for c in out:
            c.start()
        load.z.wait()
        load.hlow.wait()

    dec_load = cp.table(z=(r.z_d, r.v_z), du=(r.du_d, r.v_gdu), h=(r.h2low_d, r.v_hlow), dz=(r.dz_d, r.v_dz))

    @pl.when(jnp.logical_not(enc))
    def _():
        for c in every(dec_load):
            c.start()
        for c in every(dec_load):
            c.wait()

    hidden, grad_out = rows_of(r.v_hlow), rows_of(r.v_dz)
    for c in range(4):
        cols = slice(c * D, (c + 1) * D)
        put(r.v_a, SUM_A, tn(hidden, r.v_gdu[:, :, cols].reshape(2 * T, D)), 0, c * D, 32)
    sends = split_out(cp, r.v_a, r.a_keep, r.a_send)
    for c in range(4):
        cols = slice(c * D, (c + 1) * D)
        put(r.v_b, SUM_B, tn(r.v_z[:, :, cols].reshape(2 * T, D), grad_out), c * D, 0, 128)
    sends += split_out(cp, r.v_b, r.b_keep, r.b_send)
    for c in sends:
        c.wait()

    @pl.when(enc)
    def _():
        for c in out:
            c.wait()


def third_phase(w, one, two, gmem):
    half_a, half_b = ((8, ROWS_A, WIN), BF), ((8, ROWS_B, WIN), BF)
    outs = dict(dh=ROW32, da1=ROW, dqkv1=TRIPLE, vec=VEC, a_keep=half_a, a_send=half_a, b_keep=half_b, b_send=half_b)
    scratch = dict(
        xh2=BOTH, rs2=RSTDS, fout=W_OUT, gdu=FFN, fin=W_IN, xh1=ROW, rs1=RSTD, wso=W_SQUARE, qkv1=TRIPLE, probs1=PROBS,
        wqkv=W_QKV, z=FFN, hlow=BOTH, x=ROW32, da1=ROW, dqkv1=TRIPLE, vec=VEC, dz=BOTH, tmp=ROW,
        a=((PIECES, ROWS_A, WIN), BF), b=((PIECES, ROWS_B, WIN), BF),
    )
    ins = dict(lens=w.lens, gmem=(gmem, VMEM), w_qkv=w.w_qkv, w_so=w.w_so, w_fin=w.w_fin, w_fout=w.w_fout, gain=w.gain)
    more = dict(
        xh2=one.xh2, rs2=one.rs2, gd=one.gd, xh1=one.xh1, rs1=one.rs1, qkv=one.qkv, probs=one.probs, z=one.z,
        hlow=one.hlow, z_d=two.z, du_d=two.du, h2low_d=two.h2low, dz_d=two.dz,
    )
    ins.update({n: (a, HERE) for n, a in more.items()})
    return phase(third, ins, outs, scratch, 25 * 10**9)


def fourth(r):
    enc = is_encoder()
    dec = jnp.logical_not(enc)
    cp = Copies(r.sems)
    first_slot = cp.slots(6)

    def own(encoder):
        pairs = (
            (r.dh_e if encoder else r.dh_d, r.v_x),
            (r.vec_e if encoder else r.vec_d, r.v_vec),
            (r.da1_e if encoder else r.da1_d, r.v_da.at[1]),
            (r.att.at[1] if encoder else r.att1_d, r.v_att.at[1]),
        )
        return [cp.make(a, b, first_slot + n) for n, (a, b) in enumerate(pairs)]

    load = cp.table(
        xh1=(r.xh1.at[0], r.v_xh1),
        rs1=(r.rs1.at[0], r.v_rs1),
        att=(r.att.at[0], r.v_att.at[0]),
    )
    enc_cross = cp.table(mem=(r.mem, r.v_one.at[0]))
    dec_cross = cp.table(
        cross=(r.w_cross.at[0, :, :D], r.v_cross),
        h0=(r.hlow.at[0], r.v_one.at[0]),
        h1=(r.h1low1, r.v_one.at[1]),
        att=(r.catt, r.v_two),
        dc=(r.dc, r.v_dc),
        dcq=(r.dcq, r.v_dcq),
        layer=(r.decoded, r.v_layer),
    )
    gain = gains(r)

    @pl.when(enc)
    def _():
        for c in own(True) + every(enc_cross):
            c.start()

    @pl.when(dec)
    def _():
        for c in own(False) + every(dec_cross):
            c.start()

    for c in every(load):
        c.start()
    for c in own(True) + every(load):
        c.wait()

    @pl.when(dec)
    def _():
        dec_cross.cross.wait()
        dec_cross.dcq.wait()
        for rows in chunks():
            r.v_x[rows, :] += nt(r.v_dcq.at[0][rows, :], r.v_cross[...])

    norm_backward(r.v_x, r.v_xh1, r.v_rs1, gain[0], r.v_da.at[0], r.v_vec, 5, 7)
    out = cp.table(x=(r.v_x, r.ds), da=(r.v_da.at[0], r.da0))
    for c in every(out):
        c.start()
    layer_slot = cp.slots()
    enc_layer = cp.make(r.v_one.at[0], r.layer.at[0], layer_slot)
    dec_layer = cp.make(r.v_layer, r.layer.at[0], layer_slot)
    put(r.v_c, SUM_C, tn(rows_of(r.v_att), rows_of(r.v_da)), 0, 0, 32)

    @pl.when(enc)
    def _():
        enc_cross.mem.wait()
        enc_layer.start()
        for c in range(2):
            cols = slice(c * D, (c + 1) * D)
            put(r.v_c, SUM_C, tn(r.v_one[0], r.gkv[:T, cols]), 0, D + c * D, 32)
        tail = r.gkv[T:, :].astype(F32)
        r.v_vec[9:10, :] = tail[0:1, :D]
        r.v_vec[10:11, :] = tail[0:1, D:]

    @pl.when(dec)
    def _():
        dec_cross.layer.wait()
        dec_layer.start()
        for c in (dec_cross.h0, dec_cross.h1, dec_cross.att, dec_cross.dc):
            c.wait()
        put(r.v_c, SUM_C, tn(rows_of(r.v_one), rows_of(r.v_dcq)), 0, D, 32)
        put(r.v_c, SUM_C, tn(rows_of(r.v_two), rows_of(r.v_dc)), 0, 2 * D, 32)

    for p in range(PIECES):
        line = r.v_vec[p : p + 1, :]
        tile = [line[:, j * WIN : (j + 1) * WIN] for j in range(4)] + [jnp.zeros((12, WIN), F32)]
        r.v_c[place_of(p, SUM_C), ROWS_C - 16 :, :] = jnp.concatenate(tile, 0).astype(BF)
    for c in split_out(cp, r.v_c, r.c_keep, r.c_send) + every(out) + [enc_layer]:
        c.wait()


def fourth_phase(w, one, two, three, gkv):
    half_c = ((8, ROWS_C, WIN), BF)
    outs = dict(layer=((1, T, D), BF), ds=ROW32, da0=ROW, c_keep=half_c, c_send=half_c)
    scratch = dict(
        xh1=ROW, rs1=RSTD, att=BOTH, x=ROW32, vec=VEC, da=BOTH, one=BOTH, two=BOTH, dc=BOTH, dcq=BOTH, cross=W_SQUARE,
        layer=ROW, c=((PIECES, ROWS_C, WIN), BF),
    )
    ins = dict(gkv=(gkv, VMEM), gain=w.gain, w_cross=w.w_cross)
    more = dict(
        xh1=one.xh1, rs1=one.rs1, att=one.att, mem=one.mem, hlow=one.hlow, dh_e=three.dh, vec_e=three.vec,
        da1_e=three.da1, dh_d=two.dh, vec_d=two.vec, da1_d=two.da1, att1_d=two.att1, h1low1=two.h1low1, catt=two.catt,
        dc=two.dc, dcq=two.dcq, decoded=two.decoded,
    )
    ins.update({n: (a, HERE) for n, a in more.items()})
    return phase(fourth, ins, outs, scratch, 4 * 10**9)


def fifth(r):
    enc = is_encoder()
    cp = Copies(r.sems)
    first_slot = cp.slots(2)

    def own(encoder):
        pairs = (
            (r.dqkv1_e if encoder else r.dqkv1_d, r.v_dqkv.at[1]),
            (r.x1low_e if encoder else r.x1low_d, r.v_low.at[1]),
        )
        return [cp.make(a, b, first_slot + n) for n, (a, b) in enumerate(pairs)]

    load = cp.table(
        da=(r.da0, r.v_da),
        so=(r.w_so.at[0], r.v_wso),
        qkv=(r.qkv.at[0], r.v_qkv),
        probs=(r.probs.at[0], r.v_probs),
        x=(r.ds, r.v_x),
        wqkv=(r.w_qkv.at[0], r.v_wqkv),
        low=(r.tok.at[0], r.v_low.at[0]),
    )
    for c in every(load):
        c.start()

    @pl.when(enc)
    def _():
        for c in own(True):
            c.start()

    @pl.when(jnp.logical_not(enc))
    def _():
        for c in own(False):
            c.start()

    prepare(r.lens, r.starts)
    r.v_dqkv[0] = jnp.zeros(r.v_dqkv.shape[1:], BF)
    for c in every(load) + own(True):
        c.wait()
    self_tail(
        r.v_x, r.v_da, r.v_wso, r.v_tmp, r.v_qkv, r.v_probs, r.v_dqkv.at[0], r.v_wqkv, r.lens, r.starts,
        lax.axis_index("section"),
    )
    made = [cp.make(r.v_x, r.rows.at[0])]
    made[0].start()
    inputs, grads = rows_of(r.v_low), rows_of(r.v_dqkv)
    for c in range(3):
        cols = slice(c * D, (c + 1) * D)
        put(r.v_q, SUM_Q, tn(inputs, grads[:, cols]), 0, c * D, 32)
    for c in made + split_out(cp, r.v_q, r.q_keep, r.q_send):
        c.wait()


def fifth_phase(w, one, two, three, four, before):
    half_q = ((8, ROWS_Q, WIN), BF)
    outs = dict(rows=((1, T, D), F32), q_keep=half_q, q_send=half_q)
    scratch = dict(
        wso=W_SQUARE, qkv=TRIPLE, probs=PROBS, wqkv=W_QKV, low=BOTH, x=ROW32, da=ROW, dqkv=twice(TRIPLE), tmp=ROW,
        q=((PIECES, ROWS_Q, WIN), BF),
    )
    ins = dict(lens=w.lens, tok=w.tok, w_qkv=w.w_qkv, w_so=w.w_so)
    more = dict(
        qkv=one.qkv, probs=one.probs, x1low_e=one.x1low, x1low_d=two.x1low, dqkv1_e=three.dqkv1, dqkv1_d=two.dqkv1,
        ds=four.ds, da0=four.da0,
    )
    ins.update({n: (a, HERE) for n, a in more.items()})
    ins.update({"before%d" % n: (a, VMEM) for n, a in enumerate(before)})
    return phase(fifth, ins, outs, scratch, 8 * 10**9)


def across(value, bit):
    pairs = [(i, i ^ (1 << bit)) for i in range(lax.axis_size("dp"))]
    return lax.ppermute(value, "dp", pairs)


def added(a, b):
    return (a.astype(F32) + b.astype(F32)).astype(BF)


class Chain:
    def __init__(self, keep, send, scatter, gather):
        self.keep, self.send = keep, send
        self.scatter, self.gather = list(scatter), list(reversed(gather))
        self.result = None
        self.start()

    def start(self):
        if self.scatter:
            self.got = across(self.send, self.scatter[0])
        elif self.gather:
            self.got = across(self.keep, self.gather[0])

    def finish(self):
        keep, got = self.keep, self.got
        if self.scatter:
            self.scatter.pop(0)
            half = keep.shape[0] // 2
            if half:
                self.keep, self.send = added(keep[:half], got[:half]), added(keep[half:], got[half:])
            else:
                self.keep = added(keep, got)
                bit = 4
                while (1 << bit) < lax.axis_size("dp"):
                    self.keep = added(self.keep, across(self.keep, bit))
                    bit += 1
        else:
            self.gather.pop(0)
            if self.gather:
                self.keep = jnp.concatenate([keep, got], 0)
            else:
                self.result = (keep, got)

    def run(self, left=0):
        while self.result is None and len(self.scatter) + len(self.gather) > left:
            self.finish()
            self.start()


def advance(chains, *others):
    got = lax.optimization_barrier(tuple(c.got for c in chains) + others)
    for c, g in zip(chains, got):
        c.got = g
        c.finish()
        c.start()
    return got[len(chains) :]


def unpack(kernel, ins, scratch, outs):
    return pl.pallas_call(
        kernel,
        name=kernel.__name__,
        in_specs=[pl.BlockSpec(memory_space=VMEM)] * len(ins),
        out_specs=[pl.BlockSpec(memory_space=HERE if big else VMEM) for _, big in outs],
        out_shape=[jax.ShapeDtypeStruct(s, F32) for s, _ in outs],
        scratch_shapes=[VMEM(s, F32) for s in scratch] + [pltpu.SemaphoreType.DMA((len(scratch), PIECES))],
        compiler_params=pltpu.CompilerParams(vmem_limit_bytes=20 * 2**20),
        cost_estimate=pl.CostEstimate(flops=4 * 10**9, bytes_accessed=12 * 10**6, transcendentals=0),
    )(*ins)


def pieces_out(halves, order, high, first, wide, out, whole, sems):
    made = []
    for place in range(PIECES):
        ref, at = halves[place // 8], place % 8
        rows = pl.ds(pl.multiple_of(piece_at(place, order) * high, high), high)
        for c in range(wide // WIN):
            start = first + c * high
            whole[rows, c * WIN : (c + 1) * WIN] = ref[at, start : start + high, :].astype(F32)
        made.append(pltpu.make_async_copy(whole.at[rows, :], out.at[0, rows, :], sems.at[place]))
        made[-1].start()
    return made


def unpack_in(a0, a1, fin, v_fin, sems):
    for c in pieces_out((a0, a1), OUT_A, 32, 0, FF, fin, v_fin, sems.at[0]):
        c.wait()


def unpack_out(b0, b1, fout, v_fout, sems):
    for c in pieces_out((b0, b1), OUT_B, 128, 0, D, fout, v_fout, sems.at[0]):
        c.wait()


def unpack_qkv(q0, q1, qkv, v_qkv, sems):
    for c in pieces_out((q0, q1), OUT_Q, 32, 0, 3 * D, qkv, v_qkv, sems.at[0]):
        c.wait()


def unpack_rest(c0, c1, so, cross, b_in, b_out, gain, bias, cgain, cbias, v_so, v_cross, sems):
    made = pieces_out((c0, c1), OUT_C, 32, 0, D, so, v_so, sems.at[0])
    made += pieces_out((c0, c1), OUT_C, 32, 4 * 32, 2 * D, cross, v_cross, sems.at[1])

    def line(p):
        place = place_of(p, OUT_C)
        at = place % 8
        tail = jnp.where(place < 8, c0[at, ROWS_C - 16 :, :].astype(F32), c1[at, ROWS_C - 16 :, :].astype(F32))
        return jnp.concatenate([tail[j : j + 1, :] for j in range(4)], 1)

    for n in range(4):
        b_in[:, n * D : (n + 1) * D] = line(n)
    b_out[...] = line(4)
    for n in range(2):
        gain[0, n : n + 1, :] = line(5 + n)
        bias[0, n : n + 1, :] = line(7 + n)
    cgain[...] = line(9)
    cbias[...] = line(10)
    for c in made:
        c.wait()


def body(
    token_rows, lengths, self_qkv, self_out, ffn_in, ffn_in_bias, ffn_out, ffn_out_bias, norm_gain, norm_bias,
    cross_weights, cross_gain, cross_bias, output_grad,
):
    to_decoder, to_encoder = [(0, 1)], [(1, 0)]
    w = at_hand(
        types.SimpleNamespace(
            tok=token_rows, lens=lengths, w_qkv=self_qkv, w_so=self_out, w_fin=ffn_in, b_in=ffn_in_bias, w_fout=ffn_out,
            b_out=ffn_out_bias, gain=norm_gain, bias=norm_bias, w_cross=cross_weights, cgain=cross_gain.reshape(1, D),
            cbias=cross_bias.reshape(1, D), og=output_grad,
        )
    )
    w_c0 = lax.ppermute(cross_weights, "section", to_decoder)
    one = first_phase(w)
    mem = lax.ppermute(one.mem, "section", to_decoder)
    two = middle_phase(w, one, mem, w_c0)
    gmem = lax.ppermute(two.gmem, "section", to_encoder)
    gkv = lax.ppermute(two.gkv, "section", to_encoder)
    three = third_phase(w, one, two, gmem)
    four = fourth_phase(w, one, two, three, gkv)
    a = Chain(three.a_keep, three.a_send, SUM_A, OUT_A)
    b = Chain(three.b_keep, three.b_send, SUM_B, OUT_B)
    advance([a, b])
    c = Chain(four.c_keep, four.c_send, SUM_C, OUT_C)
    five = fifth_phase(w, one, two, three, four, (a.send, b.send))
    (q_send,) = advance([a, b, c], five.q_send)
    q = Chain(five.q_keep, q_send, SUM_Q, OUT_Q)
    for chain in (q, c, a, b):
        chain.run()
    (g_qkv,) = unpack(unpack_qkv, q.result, [(D, 3 * D)], [((1, D, 3 * D), True)])
    (g_fin,) = unpack(unpack_in, a.result, [(D, FF)], [((1, D, FF), True)])
    (g_fout,) = unpack(unpack_out, b.result, [(FF, D)], [((1, FF, D), True)])
    small = [(1, FF), (1, D), (1, 2, D), (1, 2, D), (1, D), (1, D)]
    g_so, g_cross, g_bin, g_bout, g_gain, g_bias, g_cgain, g_cbias = unpack(
        unpack_rest,
        c.result,
        [(D, D), (D, 2 * D)],
        [((1, D, D), True), ((1, D, 2 * D), True)] + [(shape, False) for shape in small],
    )
    return (
        four.layer, five.rows, g_qkv, g_so, g_fin, g_bin, g_fout, g_bout, g_gain, g_bias, g_cross, g_cgain.reshape(D),
        g_cbias.reshape(D),
    )


def solution(mesh):
    by_section = P("section")
    in_specs = (
        P("section", "dp"), P("dp"), by_section, by_section, by_section, by_section, by_section, by_section, by_section,
        by_section, by_section, P(), P(), P("dp"),
    )
    out_specs = (P("section", "dp"), P("section", "dp")) + (by_section,) * 9 + (P(), P())
    return jax.shard_map(body, mesh=mesh, in_specs=in_specs, out_specs=out_specs, check_vma=False)
```

```python
import types

import jax
import jax.numpy as jnp
from jax import lax
from jax.experimental import pallas as pl
from jax.experimental.pallas import tpu as pltpu
from jax.sharding import PartitionSpec as P

BF, F32 = jnp.bfloat16, jnp.float32
D, FF, HEAD_DIM, SENTS, REPEATS = 512, 2048, 64, 8, 2
T = 512
WIN = 128
EPSILON = 1e-05
MASKED = -1e9
SCALE = HEAD_DIM**-0.5
LOG2E = 1.4426950408889634
K0 = 0.7978845608028654
K1 = K0 * 0.044715
UNROLL_FORWARD, UNROLL_BACKWARD = 8, 4
VMEM_LIMIT = 60 * 2**20


def nn(a, b):
    return lax.dot_general(a, b, (((1,), (0,)), ((), ())), preferred_element_type=F32)


def nt(a, b):
    return lax.dot_general(a, b, (((1,), (1,)), ((), ())), preferred_element_type=F32)


def tn(a, b):
    return lax.dot_general(a, b, (((0,), (0,)), ((), ())), preferred_element_type=F32)


def iota(axis):
    return lax.broadcasted_iota(jnp.int32, (WIN, WIN), axis)


def halves():
    lane = lax.broadcasted_iota(jnp.int32, (1, WIN), 1)
    even = jnp.where(lane < HEAD_DIM, 1.0, 0.0).astype(BF)
    odd = jnp.where(lane < HEAD_DIM, 0.0, 1.0).astype(BF)
    return even, odd


def wide(ref, rows):
    part = ref[rows, :]
    return jnp.concatenate([part] * (D // WIN), 1)


def chunks(size=256):
    return [slice(i, i + size) for i in range(0, T, size)]


def prepare(lens, starts):
    for side in range(2):
        total = jnp.int32(0)
        for j in range(SENTS):
            starts[side, j] = total
            total = total + lens[0, side, j]


def window(lens, starts, side, s):
    first = starts[side, s]
    base = pl.multiple_of(jnp.minimum((first // 16) * 16, T - WIN), 16)
    return base, first - base, first - base + lens[0, side, s]


def sentences(body, unroll):
    @pl.loop(0, SENTS // unroll)
    def _(j):
        for t in range(unroll):
            body(j * unroll + t)


def attend(q, qc, k, kc, v, vc, out, probs, lens, starts, qside, kside, lim):
    even, odd = halves()
    row, col = iota(0), iota(1)
    line = lax.broadcasted_iota(jnp.int32, (1, WIN), 1)

    def body(s):
        wq, lo, hi = window(lens, starts, qside, s)
        wk, klo, khi = (wq, lo, hi) if kside is qside else window(lens, starts, kside, s)
        valid = (row >= klo) & (row < khi)
        if lim is not None:
            valid = valid & (row - col <= lim)
        mine = (line >= lo) & (line < hi)

        def score(g):
            qs = q[pl.ds(wq, WIN), qc + g * WIN : qc + (g + 1) * WIN]
            ks = k[pl.ds(wk, WIN), kc + g * WIN : kc + (g + 1) * WIN]
            return nt(ks, jnp.concatenate([qs * even, qs * odd], 0))

        def soften(g, scores):
            parts = []
            for h in range(2):
                x = jnp.where(valid, scores[:, h * WIN : (h + 1) * WIN] * (SCALE * LOG2E), MASKED)
                p = jnp.exp2(x - jnp.max(x, 0, keepdims=True))
                inverse = jnp.where(mine, 1.0 / jnp.sum(p, 0, keepdims=True), 0.0)
                parts.append((p * inverse).astype(BF))
            probs[s, :, g * 2 * WIN : (g + 1) * 2 * WIN] = jnp.concatenate(parts, 1)
            return jnp.concatenate(parts, 1)

        def finish(g, turned):
            vs = v[pl.ds(wk, WIN), vc + g * WIN : vc + (g + 1) * WIN]
            place = (pl.ds(wq, WIN), slice(g * WIN, (g + 1) * WIN))
            both = tn(turned, vs)
            out[place] += jnp.where(col < HEAD_DIM, both[:WIN], both[WIN:]).astype(BF)

        for g in range(4):
            finish(g, soften(g, score(g)))

    sentences(body, UNROLL_FORWARD)


def attend_backward(q, qc, k, kc, v, vc, probs, grad, dq, dkv, lens, starts, qside, kside):
    even, odd = halves()
    even_s, odd_s = even * SCALE, odd * SCALE

    def body(s):
        wq, _, _ = window(lens, starts, qside, s)
        wk, _, _ = (wq, 0, 0) if kside is qside else window(lens, starts, kside, s)

        def cut(ref, at, c, g):
            return ref[pl.ds(at, WIN), c + g * WIN : c + (g + 1) * WIN]

        def first_part(g):
            go = cut(grad, wq, 0, g)
            both_g = jnp.concatenate([go * even, go * odd], 0)
            return both_g, nt(cut(v, wk, vc, g), both_g)

        def second_part(g, dp):
            p_low = probs[s, :, g * 2 * WIN : (g + 1) * 2 * WIN]
            p = p_low.astype(F32)
            return p_low, (p * (dp - jnp.sum(p * dp, 0, keepdims=True))).astype(BF)

        def third_part(g, both_g, p_low, ds):
            qs, ks = cut(q, wq, qc, g), cut(k, wk, kc, g)
            dv = nn(p_low, both_g)
            dk = nn(ds, jnp.concatenate([qs * even_s, qs * odd_s], 0))
            turned = jnp.concatenate([ds[:, :WIN].T, ds[:, WIN:].T], 1)
            dqs = nn(turned, jnp.concatenate([ks * even_s, ks * odd_s], 0))
            ref, c = dq
            ref[pl.ds(wq, WIN), c + g * WIN : c + (g + 1) * WIN] += dqs.astype(ref.dtype)
            ref, c_k, c_v = dkv
            for c, value in ((c_k, dk), (c_v, dv)):
                ref[pl.ds(wk, WIN), c + g * WIN : c + (g + 1) * WIN] += value.astype(ref.dtype)

        start = [first_part(g) for g in range(4)]
        middle_part = [second_part(g, start[g][1]) for g in range(4)]
        for g in range(4):
            third_part(g, start[g][0], *middle_part[g])

    sentences(body, UNROLL_BACKWARD)


def normed(v):
    centre = v - jnp.mean(v, -1, keepdims=True)
    rstd = lax.rsqrt(jnp.mean(centre * centre, -1, keepdims=True) + EPSILON)
    return centre * rstd, rstd


def norm_out(v, rows, xh, rs, gain, bias, wide_ref, low_ref):
    xhat, rstd = normed(v)
    xh[rows, :] = xhat.astype(BF)
    rs[rows, :] = jnp.broadcast_to(rstd, (v.shape[0], WIN))
    h = xhat * gain + bias
    wide_ref[rows, :] = h
    low_ref[rows, :] = h.astype(BF)


def norm_backward(dst, xh, rs, gain, low, vec, gain_row, bias_row):
    for rows in chunks():
        dy = dst[rows, :]
        xhat = xh[rows, :].astype(F32)
        rstd = wide(rs, rows)
        prod = dy * xhat
        vec[gain_row : gain_row + 1, :] += jnp.sum(prod, 0, keepdims=True)
        vec[bias_row : bias_row + 1, :] += jnp.sum(dy, 0, keepdims=True)
        scaled = dy * gain
        m1 = jnp.mean(scaled, -1, keepdims=True)
        m2 = jnp.mean(prod * gain, -1, keepdims=True)
        ds = rstd * (scaled - m1 - xhat * m2)
        dst[rows, :] = ds
        low[rows, :] = ds.astype(BF)


def self_forward(x, low, w_qkv, w_out, qkv, att, probs, xh, rs, gain, bias, h, h_low, lens, starts, side, lim):
    for c in range(3):
        cols = slice(c * D, (c + 1) * D)
        qkv[:, cols] = nn(low[...], w_qkv[:, cols]).astype(BF)
    attend(qkv, 0, qkv, D, qkv, 2 * D, att, probs, lens, starts, side, side, lim)
    for rows in chunks():
        norm_out(x[rows, :] + nn(att[rows, :], w_out[...]), rows, xh, rs, gain, bias, h, h_low)


def self_tail(dst, da, w_out, tmp, qkv, probs, dqkv, w_qkv, lens, starts, side):
    tmp[...] = nt(da[...], w_out[...]).astype(BF)
    attend_backward(
        qkv, 0, qkv, D, qkv, 2 * D, probs, tmp, (dqkv, 0), (dqkv, D, 2 * D), lens, starts, side, side
    )
    for rows in chunks():
        dst[rows, :] += nt(dqkv[rows, :], w_qkv[...])


def self_backward(dst, xh, rs, gain, vec, da, w_out, tmp, qkv, probs, dqkv, w_qkv, lens, starts, side):
    norm_backward(dst, xh, rs, gain, da, vec, 5, 7)
    self_tail(dst, da, w_out, tmp, qkv, probs, dqkv, w_qkv, lens, starts, side)


def ffn_forward(h, h_low, w_in, b_in, w_out, b_out, z, gd, xh, rs, gain, bias, out, out_low, between=None):
    for c in range(4):
        cols = slice(c * D, (c + 1) * D)
        u = nn(h_low[...], w_in[:, cols]) + b_in[:, cols].astype(F32)
        square = u * u
        half = 0.5 + 0.5 * jnp.tanh(u * (K0 + K1 * square))
        act = u * half
        z[:, cols] = act.astype(BF)
        gd[:, cols] = (half + act * (1.0 - half) * (2.0 * K0 + 6.0 * K1 * square)).astype(BF)
    if between is not None:
        between()
    for rows in chunks():
        v = h[rows, :] + (nn(z[rows, :], w_out[...]) + b_out[...].astype(F32))
        norm_out(v, rows, xh, rs, gain, bias, out, out_low)


def ffn_backward(dst, xh, rs, gain, vec, dz, gdu, w_in, w_out):
    norm_backward(dst, xh, rs, gain, dz, vec, 6, 8)
    vec[4:5, :] += jnp.sum(dz[...].astype(F32), 0, keepdims=True)
    for c in range(4):
        cols = slice(c * D, (c + 1) * D)
        du = (nt(dz[...], w_out[cols, :]) * gdu[:, cols].astype(F32)).astype(BF)
        gdu[:, cols] = du
        vec[c : c + 1, :] += jnp.sum(du.astype(F32), 0, keepdims=True)
    for rows in chunks():
        dst[rows, :] += nt(gdu[rows, :], w_in[...])


def rows_of(ref):
    return ref[...].reshape(2 * T, ref.shape[-1])


class Copies:
    def __init__(self, sems):
        self.sems, self.used = sems, 0

    def slots(self, count=1):
        first = self.used
        self.used += count
        return first

    def make(self, src, dst, slot=None):
        slot = self.slots() if slot is None else slot
        return pltpu.make_async_copy(src, dst, self.sems.at[slot])

    def table(self, **pairs):
        return types.SimpleNamespace(**{n: self.make(a, b) for n, (a, b) in pairs.items()})


def every(table):
    return list(vars(table).values())


HERE, VMEM, SMEM = pl.ANY, pltpu.VMEM, pltpu.SMEM


def phase(body, ins, outs, scratch, flops, limit=56, n_sems=64):
    in_names, out_names, names = list(ins), list(outs), list(scratch)

    def kernel(*refs):
        labels = in_names + out_names + ["v_" + n for n in names]
        r = types.SimpleNamespace(**dict(zip(labels, refs)))
        r.starts, r.sems = refs[-2:]
        body(r)

    moved = sum(a.size * a.dtype.itemsize for a, _ in ins.values())
    results = pl.pallas_call(
        kernel,
        name=body.__name__,
        in_specs=[pl.BlockSpec(memory_space=s) for _, s in ins.values()],
        out_specs=[pl.BlockSpec(memory_space=HERE)] * len(outs),
        out_shape=[jax.ShapeDtypeStruct(s, d) for s, d in outs.values()],
        scratch_shapes=[VMEM(s, d) for s, d in scratch.values()]
        + [SMEM((2, SENTS), jnp.int32), pltpu.SemaphoreType.DMA((n_sems,))],
        compiler_params=pltpu.CompilerParams(vmem_limit_bytes=limit * 2**20),
        cost_estimate=pl.CostEstimate(flops=flops, bytes_accessed=moved, transcendentals=0),
    )(*[a for a, _ in ins.values()])
    return types.SimpleNamespace(**dict(zip(out_names, results)))


ROW, BOTH, FFN = ((T, D), BF), ((2, T, D), BF), ((2, T, FF), BF)
ROW32, TRIPLE = ((T, D), F32), ((T, 3 * D), BF)
RSTD, RSTDS = ((T, WIN), F32), ((2, T, WIN), F32)
PROBS, VEC, MEMKV = ((SENTS, WIN, 2 * T), BF), ((16, D), F32), ((T + 16, 2 * D), BF)
W_IN, W_OUT, W_QKV, W_CROSS, W_SQUARE = ((D, FF), BF), ((FF, D), BF), ((D, 3 * D), BF), ((D, 2 * D), BF), ((D, D), BF)


def twice(kind):
    return ((2,) + kind[0], kind[1])


def at_hand(w):
    return types.SimpleNamespace(**{n: (a, SMEM if n == "lens" else VMEM if a.ndim < 3 or a.shape[1] < 8 else HERE) for n, a in vars(w).items()})


def is_encoder():
    return lax.axis_index("section") == 0


def gains(r):
    return [r.gain[0, j : j + 1, :].astype(F32) for j in range(2)]


def biases(r):
    return [r.bias[0, j : j + 1, :].astype(F32) for j in range(2)]


def first(r):
    enc = is_encoder()
    dec = jnp.logical_not(enc)
    cp = Copies(r.sems)
    load = cp.table(
        x=(r.tok.at[0], r.v_low.at[0]),
        qkv=(r.w_qkv.at[0], r.v_wqkv),
        so=(r.w_so.at[0], r.v_wso),
        fin=(r.w_fin.at[0], r.v_fin),
        fout=(r.w_fout.at[0], r.v_fout),
        cq=(r.w_cross.at[0, :, :D], r.v_cross),
    )
    load.x.start()
    load.qkv.start()
    load.so.start()

    @pl.when(enc)
    def _():
        load.fin.start()
        load.fout.start()

    @pl.when(dec)
    def _():
        load.cq.start()

    prepare(r.lens, r.starts)
    lim = jnp.where(enc, 4 * T, 0)
    r.v_att[...] = jnp.zeros(r.v_att.shape, BF)
    load.x.wait()
    r.v_x[...] = r.v_low[0].astype(F32)
    gain, bias = gains(r), biases(r)
    self_slots, ffn_slots = cp.slots(12), cp.slots(8)

    def self_copies(i):
        pairs = (
            (r.v_qkv, r.qkv), (r.v_probs, r.probs), (r.v_att, r.att), (r.v_xh1, r.xh1), (r.v_rs1, r.rs1),
            (r.v_hlow, r.hlow),
        )
        return [cp.make(a.at[i], b.at[i], self_slots + 2 * n + i) for n, (a, b) in enumerate(pairs)]

    def ffn_copies(i):
        pairs = ((r.v_z, r.z), (r.v_gd, r.gd), (r.v_xh2, r.xh2), (r.v_rs2, r.rs2))
        return [cp.make(a.at[i], b.at[i], ffn_slots + 2 * n + i) for n, (a, b) in enumerate(pairs)]

    @pl.loop(0, REPEATS)
    def _(i):
        @pl.when(i == 0)
        def _():
            load.qkv.wait()
            load.so.wait()

        @pl.when(jnp.logical_or(enc, i == 0))
        def _():
            self_forward(
                r.v_x, r.v_low.at[i], r.v_wqkv, r.v_wso, r.v_qkv.at[i], r.v_att.at[i], r.v_probs.at[i],
                r.v_xh1.at[i], r.v_rs1.at[i], gain[0], bias[0], r.v_h, r.v_hlow.at[i], r.lens, r.starts,
                lax.axis_index("section"), lim,
            )
            for c in self_copies(i):
                c.start()

        @pl.when(jnp.logical_and(enc, i == 0))
        def _():
            load.fin.wait()
            load.fout.wait()

        @pl.when(enc)
        def _():
            ffn_forward(
                r.v_h, r.v_hlow.at[i], r.v_fin, r.b_in, r.v_fout, r.b_out, r.v_z.at[i], r.v_gd.at[i],
                r.v_xh2.at[i], r.v_rs2.at[i], gain[1], bias[1], r.v_x, r.v_low.at[i + 1],
                lambda: [c.start() for c in ffn_copies(i)[:2]],
            )
            for c in ffn_copies(i)[2:]:
                c.start()

    dec_out = cp.table(h=(r.v_h, r.h), cq=(r.v_cq, r.cq))
    enc_out = cp.table(x1=(r.v_low.at[1], r.x1low), mem=(r.v_low.at[2], r.mem))

    @pl.when(dec)
    def _():
        load.cq.wait()
        r.v_cq[...] = nn(r.v_hlow[0], r.v_cross[...]).astype(BF)
        for c in every(dec_out):
            c.start()
        for c in self_copies(0) + every(dec_out):
            c.wait()

    @pl.when(enc)
    def _():
        for c in every(enc_out):
            c.start()
        for i in range(REPEATS):
            for c in self_copies(i) + ffn_copies(i):
                c.wait()
        for c in every(enc_out):
            c.wait()


def first_phase(w):
    saved = dict(
        qkv=twice(TRIPLE), probs=twice(PROBS), att=BOTH, xh1=BOTH, rs1=RSTDS, hlow=BOTH, z=FFN, gd=FFN, xh2=BOTH,
        rs2=RSTDS, h=ROW32, cq=ROW,
    )
    scratch = dict(saved, low=((3, T, D), BF), wqkv=W_QKV, wso=W_SQUARE, fin=W_IN, fout=W_OUT, cross=W_SQUARE, x=ROW32)
    ins = dict(
        lens=w.lens, tok=w.tok, w_qkv=w.w_qkv, w_so=w.w_so, w_fin=w.w_fin, w_fout=w.w_fout, w_cross=w.w_cross,
        b_in=w.b_in, b_out=w.b_out, gain=w.gain, bias=w.bias,
    )
    return phase(first, ins, dict(saved, x1low=ROW, mem=ROW), scratch, 16 * 10**9)


def middle(r):
    @pl.when(jnp.logical_not(is_encoder()))
    def _():
        cp = Copies(r.sems)
        load = cp.table(
            cq=(r.cq, r.v_cq.at[0]),
            h=(r.h, r.v_h),
            cross=(r.w_cross.at[0], r.v_cross),
            fin=(r.w_fin.at[0], r.v_fin),
            fout=(r.w_fout.at[0], r.v_fout),
            qkv=(r.w_qkv.at[0], r.v_wqkv),
            so=(r.w_so.at[0], r.v_wso),
            og=(r.og, r.v_og),
        )
        for c in every(load):
            c.start()
        prepare(r.lens, r.starts)
        gain, bias = gains(r), biases(r)
        cgain, cbias = r.cgain[...].astype(F32), r.cbias[...].astype(F32)
        for ref in (r.v_vec, r.v_gkv, r.v_catt, r.v_att1, r.v_dcq, r.v_dqkv1):
            ref[...] = jnp.zeros(ref.shape, ref.dtype)
        for c in range(2):
            cols = slice(c * D, (c + 1) * D)
            r.v_mkv[:, cols] = nn(r.mem[...], r.w_c0[0, :, cols]).astype(BF)
        load.cq.wait()
        load.h.wait()
        load.cross.wait()
        saved = (
            (r.v_h1low1, r.h1low1), (r.v_x1low, r.x1low), (r.v_att1, r.att1), (r.v_h2low, r.h2low),
            (r.v_catt, r.catt), (r.v_z, r.z), (r.v_declow, r.decoded),
        )
        early = [cp.make(a, b) for a, b in saved]

        @pl.loop(0, REPEATS)
        def _(i):
            @pl.when(i == 1)
            def _():
                load.qkv.wait()
                load.so.wait()
                self_forward(
                    r.v_x, r.v_x1low, r.v_wqkv, r.v_wso, r.v_qkv1, r.v_att1, r.v_probs1, r.v_xh1, r.v_rs1,
                    gain[0], bias[0], r.v_h, r.v_h1low1, r.lens, r.starts, 1, 0,
                )
                r.v_cq[1] = nn(r.v_h1low1[...], r.v_cross[:, :D]).astype(BF)

            attend(
                r.v_cq.at[i], 0, r.v_mkv, 0, r.v_mkv, D, r.v_catt.at[i], r.v_probsc.at[i], r.lens, r.starts, 1, 0,
                None,
            )
            for rows in chunks():
                v = r.v_h[rows, :] + nn(r.v_catt.at[i][rows, :], r.v_cross[:, D:])
                norm_out(v, rows, r.v_xhc.at[i], r.v_rsc.at[i], cgain, cbias, r.v_h2, r.v_h2low.at[i])

            @pl.when(i == 0)
            def _():
                load.fin.wait()
                load.fout.wait()

            ffn_forward(
                r.v_h2, r.v_h2low.at[i], r.v_fin, r.b_in, r.v_fout, r.b_out, r.v_z.at[i], r.v_gdu.at[i],
                r.v_xh2.at[i], r.v_rs2.at[i], gain[1], bias[1], r.v_x, r.v_declow,
            )

            @pl.when(i == 0)
            def _():
                r.v_x1low[...] = r.v_declow[...]

        for c in early:
            c.start()
        load.og.wait()
        r.v_x[...] = r.v_og[...].astype(F32)

        @pl.loop(0, REPEATS)
        def _(j):
            i = 1 - j
            ffn_backward(
                r.v_x, r.v_xh2.at[i], r.v_rs2.at[i], gain[1], r.v_vec, r.v_dz.at[i], r.v_gdu.at[i], r.v_fin, r.v_fout
            )
            norm_backward(r.v_x, r.v_xhc.at[i], r.v_rsc.at[i], cgain, r.v_dc.at[i], r.v_vec, 9, 10)
            r.v_tmp[...] = nt(r.v_dc[i], r.v_cross[:, D:]).astype(BF)
            attend_backward(
                r.v_cq.at[i], 0, r.v_mkv, 0, r.v_mkv, D, r.v_probsc.at[i], r.v_tmp, (r.v_dcq.at[i], 0),
                (r.v_gkv, 0, D), r.lens, r.starts, 1, 0,
            )

            @pl.when(i == 1)
            def _():
                for rows in chunks():
                    r.v_x[rows, :] += nt(r.v_dcq.at[i][rows, :], r.v_cross[:, :D])
                self_backward(
                    r.v_x, r.v_xh1, r.v_rs1, gain[0], r.v_vec, r.v_da1, r.v_wso, r.v_tmp, r.v_qkv1, r.v_probs1,
                    r.v_dqkv1, r.v_wqkv, r.lens, r.starts, 1,
                )

        r.v_gkvlow[:T, :] = r.v_gkv[...].astype(BF)
        r.v_gkvlow[T:, :] = jnp.concatenate(
            [jnp.concatenate([r.v_vec[9:10, :], r.v_vec[10:11, :]], 1), jnp.zeros((15, 2 * D), F32)], 0
        ).astype(BF)
        r.v_gmem[...] = nt(r.v_gkvlow[:T, :], r.w_c0[0]).astype(BF)
        saved = (
            (r.v_gmem, r.gmem), (r.v_gkvlow, r.gkv), (r.v_gdu, r.du), (r.v_dz, r.dz), (r.v_dc, r.dc),
            (r.v_dcq, r.dcq), (r.v_da1, r.da1), (r.v_dqkv1, r.dqkv1), (r.v_x, r.dh), (r.v_vec, r.vec),
        )
        late = [cp.make(a, b) for a, b in saved]
        for c in late:
            c.start()
        for c in early + late:
            c.wait()


def middle_phase(w, one, mem, w_c0):
    outs = dict(
        gmem=ROW, gkv=MEMKV, decoded=ROW, z=FFN, du=FFN, h2low=BOTH, catt=BOTH, h1low1=ROW, dz=BOTH, dc=BOTH, dcq=BOTH,
        att1=ROW, x1low=ROW, da1=ROW, dqkv1=TRIPLE, dh=ROW32, vec=VEC,
    )
    scratch = dict(
        cq=BOTH, h=ROW32, cross=W_CROSS, fin=W_IN, fout=W_OUT, wqkv=W_QKV, wso=W_SQUARE, og=ROW, vec=VEC,
        gkv=((T, 2 * D), F32), catt=BOTH, att1=ROW, dcq=BOTH, dqkv1=TRIPLE, mkv=((T, 2 * D), BF), h1low1=ROW,
        x1low=ROW, h2low=BOTH, z=FFN, declow=ROW, x=ROW32, qkv1=TRIPLE, probs1=PROBS, xh1=ROW, rs1=RSTD,
        probsc=twice(PROBS), xhc=BOTH, rsc=RSTDS, h2=ROW32, gdu=FFN, xh2=BOTH, rs2=RSTDS, dz=BOTH, dc=BOTH, tmp=ROW,
        da1=ROW, gkvlow=MEMKV, gmem=ROW,
    )
    ins = dict(
        lens=w.lens, mem=(mem, VMEM), w_c0=(w_c0, VMEM), cq=(one.cq, HERE), h=(one.h, HERE), og=(w.og[0], HERE),
        w_qkv=w.w_qkv, w_so=w.w_so, w_fin=w.w_fin, w_fout=w.w_fout, w_cross=w.w_cross, b_in=w.b_in, b_out=w.b_out,
        gain=w.gain, bias=w.bias, cgain=w.cgain, cbias=w.cbias,
    )
    return phase(middle, ins, outs, scratch, 30 * 10**9, 58)


PIECES = 16
X_FIRST, Z_FIRST = (0, 1, 2, 3), (0, 2, 3, 1)
SUM_A, SUM_B, SUM_C, SUM_Q = X_FIRST, Z_FIRST, X_FIRST, X_FIRST
OUT_A, OUT_B, OUT_C, OUT_Q = X_FIRST, X_FIRST, Z_FIRST, X_FIRST
ROWS_A = ROWS_B = 512
ROWS_C, ROWS_Q = 32 * 12 + 16, 32 * 12


def place_of(piece, order):
    relative = piece ^ (lax.axis_index("dp") % PIECES)
    place = jnp.int32(0)
    for n, bit in enumerate(order):
        place = place + ((relative >> bit) & 1) * (1 << (3 - n))
    return place


def piece_at(place, order):
    relative = 0
    for n, bit in enumerate(order):
        relative += ((place >> (3 - n)) & 1) << bit
    return relative ^ (lax.axis_index("dp") % PIECES)


def put(dst, order, block, first_row, first_col, high):
    height, width = block.shape
    for j in range(0, height, high):
        place = place_of((first_row + j) // high, order)
        for c in range(0, width, WIN):
            at = ((first_col + c) // WIN) * high
            dst[place, at : at + high, :] = block[j : j + high, c : c + WIN].astype(BF)


def split_out(cp, ref, keep, send):
    made = [cp.make(ref.at[:8], keep), cp.make(ref.at[8:], send)]
    for c in made:
        c.start()
    return made


def third(r):
    enc = is_encoder()
    cp = Copies(r.sems)
    load = cp.table(
        xh2=(r.xh2, r.v_xh2),
        rs2=(r.rs2, r.v_rs2),
        fout=(r.w_fout.at[0], r.v_fout),
        gd=(r.gd, r.v_gdu),
        fin=(r.w_fin.at[0], r.v_fin),
        xh1=(r.xh1.at[1], r.v_xh1),
        rs1=(r.rs1.at[1], r.v_rs1),
        so=(r.w_so.at[0], r.v_wso),
        qkv=(r.qkv.at[1], r.v_qkv1),
        probs=(r.probs.at[1], r.v_probs1),
        wqkv=(r.w_qkv.at[0], r.v_wqkv),
        z=(r.z, r.v_z),
        hlow=(r.hlow, r.v_hlow),
    )
    saved = ((r.v_x, r.dh), (r.v_da1, r.da1), (r.v_dqkv1, r.dqkv1), (r.v_vec, r.vec))
    out = [cp.make(a, b) for a, b in saved]

    @pl.when(enc)
    def _():
        for c in every(load):
            c.start()
        prepare(r.lens, r.starts)
        gain = gains(r)
        r.v_vec[...] = jnp.zeros(r.v_vec.shape, F32)
        r.v_dqkv1[...] = jnp.zeros(r.v_dqkv1.shape, BF)
        r.v_x[...] = r.gmem[...].astype(F32)
        for c in (load.xh2, load.rs2, load.fout, load.gd, load.fin):
            c.wait()

        @pl.loop(0, REPEATS)
        def _(j):
            i = 1 - j
            ffn_backward(
                r.v_x, r.v_xh2.at[i], r.v_rs2.at[i], gain[1], r.v_vec, r.v_dz.at[i], r.v_gdu.at[i], r.v_fin, r.v_fout
            )

            @pl.when(i == 1)
            def _():
                for c in (load.xh1, load.rs1, load.so, load.qkv, load.probs, load.wqkv):
                    c.wait()
                self_backward(
                    r.v_x, r.v_xh1, r.v_rs1, gain[0], r.v_vec, r.v_da1, r.v_wso, r.v_tmp, r.v_qkv1, r.v_probs1,
                    r.v_dqkv1, r.v_wqkv, r.lens, r.starts, 0,
                )

        for c in out:
            c.start()
        load.z.wait()
        load.hlow.wait()

    dec_load = cp.table(z=(r.z_d, r.v_z), du=(r.du_d, r.v_gdu), h=(r.h2low_d, r.v_hlow), dz=(r.dz_d, r.v_dz))

    @pl.when(jnp.logical_not(enc))
    def _():
        for c in every(dec_load):
            c.start()
        for c in every(dec_load):
            c.wait()

    hidden, grad_out = rows_of(r.v_hlow), rows_of(r.v_dz)
    for c in range(4):
        cols = slice(c * D, (c + 1) * D)
        put(r.v_a, SUM_A, tn(hidden, r.v_gdu[:, :, cols].reshape(2 * T, D)), 0, c * D, 32)
    sends = split_out(cp, r.v_a, r.a_keep, r.a_send)
    for c in range(4):
        cols = slice(c * D, (c + 1) * D)
        put(r.v_b, SUM_B, tn(r.v_z[:, :, cols].reshape(2 * T, D), grad_out), c * D, 0, 128)
    sends += split_out(cp, r.v_b, r.b_keep, r.b_send)
    for c in sends:
        c.wait()

    @pl.when(enc)
    def _():
        for c in out:
            c.wait()


def third_phase(w, one, two, gmem):
    half_a, half_b = ((8, ROWS_A, WIN), BF), ((8, ROWS_B, WIN), BF)
    outs = dict(dh=ROW32, da1=ROW, dqkv1=TRIPLE, vec=VEC, a_keep=half_a, a_send=half_a, b_keep=half_b, b_send=half_b)
    scratch = dict(
        xh2=BOTH, rs2=RSTDS, fout=W_OUT, gdu=FFN, fin=W_IN, xh1=ROW, rs1=RSTD, wso=W_SQUARE, qkv1=TRIPLE, probs1=PROBS,
        wqkv=W_QKV, z=FFN, hlow=BOTH, x=ROW32, da1=ROW, dqkv1=TRIPLE, vec=VEC, dz=BOTH, tmp=ROW,
        a=((PIECES, ROWS_A, WIN), BF), b=((PIECES, ROWS_B, WIN), BF),
    )
    ins = dict(lens=w.lens, gmem=(gmem, VMEM), w_qkv=w.w_qkv, w_so=w.w_so, w_fin=w.w_fin, w_fout=w.w_fout, gain=w.gain)
    more = dict(
        xh2=one.xh2, rs2=one.rs2, gd=one.gd, xh1=one.xh1, rs1=one.rs1, qkv=one.qkv, probs=one.probs, z=one.z,
        hlow=one.hlow, z_d=two.z, du_d=two.du, h2low_d=two.h2low, dz_d=two.dz,
    )
    ins.update({n: (a, HERE) for n, a in more.items()})
    return phase(third, ins, outs, scratch, 25 * 10**9, 52)


def fourth(r):
    enc = is_encoder()
    dec = jnp.logical_not(enc)
    cp = Copies(r.sems)
    first_slot = cp.slots(6)

    def own(encoder):
        pairs = (
            (r.dh_e if encoder else r.dh_d, r.v_x),
            (r.vec_e if encoder else r.vec_d, r.v_vec),
            (r.da1_e if encoder else r.da1_d, r.v_da.at[1]),
            (r.att.at[1] if encoder else r.att1_d, r.v_att.at[1]),
        )
        return [cp.make(a, b, first_slot + n) for n, (a, b) in enumerate(pairs)]

    load = cp.table(
        xh1=(r.xh1.at[0], r.v_xh1),
        rs1=(r.rs1.at[0], r.v_rs1),
        att=(r.att.at[0], r.v_att.at[0]),
    )
    enc_cross = cp.table(mem=(r.mem, r.v_one.at[0]))
    dec_cross = cp.table(
        cross=(r.w_cross.at[0, :, :D], r.v_cross),
        h0=(r.hlow.at[0], r.v_one.at[0]),
        h1=(r.h1low1, r.v_one.at[1]),
        att=(r.catt, r.v_two),
        dc=(r.dc, r.v_dc),
        dcq=(r.dcq, r.v_dcq),
        layer=(r.decoded, r.v_layer),
    )
    gain = gains(r)

    @pl.when(enc)
    def _():
        for c in own(True) + every(enc_cross):
            c.start()

    @pl.when(dec)
    def _():
        for c in own(False) + every(dec_cross):
            c.start()

    for c in every(load):
        c.start()
    for c in own(True) + every(load):
        c.wait()

    @pl.when(dec)
    def _():
        dec_cross.cross.wait()
        dec_cross.dcq.wait()
        for rows in chunks():
            r.v_x[rows, :] += nt(r.v_dcq.at[0][rows, :], r.v_cross[...])

    norm_backward(r.v_x, r.v_xh1, r.v_rs1, gain[0], r.v_da.at[0], r.v_vec, 5, 7)
    out = cp.table(x=(r.v_x, r.ds), da=(r.v_da.at[0], r.da0))
    for c in every(out):
        c.start()
    layer_slot = cp.slots()
    enc_layer = cp.make(r.v_one.at[0], r.layer.at[0], layer_slot)
    dec_layer = cp.make(r.v_layer, r.layer.at[0], layer_slot)
    put(r.v_c, SUM_C, tn(rows_of(r.v_att), rows_of(r.v_da)), 0, 0, 32)

    @pl.when(enc)
    def _():
        enc_cross.mem.wait()
        enc_layer.start()
        for c in range(2):
            cols = slice(c * D, (c + 1) * D)
            put(r.v_c, SUM_C, tn(r.v_one[0], r.gkv[:T, cols]), 0, D + c * D, 32)
        tail = r.gkv[T:, :].astype(F32)
        r.v_vec[9:10, :] = tail[0:1, :D]
        r.v_vec[10:11, :] = tail[0:1, D:]

    @pl.when(dec)
    def _():
        dec_cross.layer.wait()
        dec_layer.start()
        for c in (dec_cross.h0, dec_cross.h1, dec_cross.att, dec_cross.dc):
            c.wait()
        put(r.v_c, SUM_C, tn(rows_of(r.v_one), rows_of(r.v_dcq)), 0, D, 32)
        put(r.v_c, SUM_C, tn(rows_of(r.v_two), rows_of(r.v_dc)), 0, 2 * D, 32)

    for p in range(PIECES):
        line = r.v_vec[p : p + 1, :]
        tile = [line[:, j * WIN : (j + 1) * WIN] for j in range(4)] + [jnp.zeros((12, WIN), F32)]
        r.v_c[place_of(p, SUM_C), ROWS_C - 16 :, :] = jnp.concatenate(tile, 0).astype(BF)
    for c in split_out(cp, r.v_c, r.c_keep, r.c_send) + every(out) + [enc_layer]:
        c.wait()


def fourth_phase(w, one, two, three, gkv):
    half_c = ((8, ROWS_C, WIN), BF)
    outs = dict(layer=((1, T, D), BF), ds=ROW32, da0=ROW, c_keep=half_c, c_send=half_c)
    scratch = dict(
        xh1=ROW, rs1=RSTD, att=BOTH, x=ROW32, vec=VEC, da=BOTH, one=BOTH, two=BOTH, dc=BOTH, dcq=BOTH, cross=W_SQUARE,
        layer=ROW, c=((PIECES, ROWS_C, WIN), BF),
    )
    ins = dict(gkv=(gkv, VMEM), gain=w.gain, w_cross=w.w_cross)
    more = dict(
        xh1=one.xh1, rs1=one.rs1, att=one.att, mem=one.mem, hlow=one.hlow, dh_e=three.dh, vec_e=three.vec,
        da1_e=three.da1, dh_d=two.dh, vec_d=two.vec, da1_d=two.da1, att1_d=two.att1, h1low1=two.h1low1, catt=two.catt,
        dc=two.dc, dcq=two.dcq, decoded=two.decoded,
    )
    ins.update({n: (a, HERE) for n, a in more.items()})
    return phase(fourth, ins, outs, scratch, 4 * 10**9, 50)


def fifth(r):
    enc = is_encoder()
    cp = Copies(r.sems)
    first_slot = cp.slots(2)

    def own(encoder):
        pairs = (
            (r.dqkv1_e if encoder else r.dqkv1_d, r.v_dqkv.at[1]),
            (r.x1low_e if encoder else r.x1low_d, r.v_low.at[1]),
        )
        return [cp.make(a, b, first_slot + n) for n, (a, b) in enumerate(pairs)]

    load = cp.table(
        da=(r.da0, r.v_da),
        so=(r.w_so.at[0], r.v_wso),
        qkv=(r.qkv.at[0], r.v_qkv),
        probs=(r.probs.at[0], r.v_probs),
        x=(r.ds, r.v_x),
        wqkv=(r.w_qkv.at[0], r.v_wqkv),
        low=(r.tok.at[0], r.v_low.at[0]),
    )
    for c in every(load):
        c.start()

    @pl.when(enc)
    def _():
        for c in own(True):
            c.start()

    @pl.when(jnp.logical_not(enc))
    def _():
        for c in own(False):
            c.start()

    prepare(r.lens, r.starts)
    r.v_dqkv[0] = jnp.zeros(r.v_dqkv.shape[1:], BF)
    for c in every(load) + own(True):
        c.wait()
    self_tail(
        r.v_x, r.v_da, r.v_wso, r.v_tmp, r.v_qkv, r.v_probs, r.v_dqkv.at[0], r.v_wqkv, r.lens, r.starts,
        lax.axis_index("section"),
    )
    made = [cp.make(r.v_x, r.rows.at[0])]
    made[0].start()
    inputs, grads = rows_of(r.v_low), rows_of(r.v_dqkv)
    for c in range(3):
        cols = slice(c * D, (c + 1) * D)
        put(r.v_q, SUM_Q, tn(inputs, grads[:, cols]), 0, c * D, 32)
    for c in made + split_out(cp, r.v_q, r.q_keep, r.q_send):
        c.wait()


def fifth_phase(w, one, two, three, four, before):
    half_q = ((8, ROWS_Q, WIN), BF)
    outs = dict(rows=((1, T, D), F32), q_keep=half_q, q_send=half_q)
    scratch = dict(
        wso=W_SQUARE, qkv=TRIPLE, probs=PROBS, wqkv=W_QKV, low=BOTH, x=ROW32, da=ROW, dqkv=twice(TRIPLE), tmp=ROW,
        q=((PIECES, ROWS_Q, WIN), BF),
    )
    ins = dict(lens=w.lens, tok=w.tok, w_qkv=w.w_qkv, w_so=w.w_so)
    more = dict(
        qkv=one.qkv, probs=one.probs, x1low_e=one.x1low, x1low_d=two.x1low, dqkv1_e=three.dqkv1, dqkv1_d=two.dqkv1,
        ds=four.ds, da0=four.da0,
    )
    ins.update({n: (a, HERE) for n, a in more.items()})
    ins.update({"before%d" % n: (a, VMEM) for n, a in enumerate(before)})
    return phase(fifth, ins, outs, scratch, 8 * 10**9, 50)


def across(value, bit):
    pairs = [(i, i ^ (1 << bit)) for i in range(lax.axis_size("dp"))]
    return lax.ppermute(value, "dp", pairs)


def added(a, b):
    return (a.astype(F32) + b.astype(F32)).astype(BF)


class Chain:
    def __init__(self, keep, send, scatter, gather):
        self.keep, self.send = keep, send
        self.scatter, self.gather = list(scatter), list(reversed(gather))
        self.result = None
        self.start()

    def start(self):
        if self.scatter:
            self.got = across(self.send, self.scatter[0])
        elif self.gather:
            self.got = across(self.keep, self.gather[0])

    def finish(self):
        keep, got = self.keep, self.got
        if self.scatter:
            self.scatter.pop(0)
            half = keep.shape[0] // 2
            if half:
                self.keep, self.send = added(keep[:half], got[:half]), added(keep[half:], got[half:])
            else:
                self.keep = added(keep, got)
                bit = 4
                while (1 << bit) < lax.axis_size("dp"):
                    self.keep = added(self.keep, across(self.keep, bit))
                    bit += 1
        else:
            self.gather.pop(0)
            if self.gather:
                self.keep = jnp.concatenate([keep, got], 0)
            else:
                self.result = (keep, got)

    def run(self, left=0):
        while self.result is None and len(self.scatter) + len(self.gather) > left:
            self.finish()
            self.start()


def advance(chains, *others):
    got = lax.optimization_barrier(tuple(c.got for c in chains) + others)
    for c, g in zip(chains, got):
        c.got = g
        c.finish()
        c.start()
    return got[len(chains) :]


def unpack(kernel, ins, scratch, outs):
    return pl.pallas_call(
        kernel,
        name=kernel.__name__,
        in_specs=[pl.BlockSpec(memory_space=VMEM)] * len(ins),
        out_specs=[pl.BlockSpec(memory_space=HERE if big else VMEM) for _, big in outs],
        out_shape=[jax.ShapeDtypeStruct(s, F32) for s, _ in outs],
        scratch_shapes=[VMEM(s, F32) for s in scratch] + [pltpu.SemaphoreType.DMA((len(scratch), PIECES))],
        compiler_params=pltpu.CompilerParams(vmem_limit_bytes=20 * 2**20),
        cost_estimate=pl.CostEstimate(flops=4 * 10**9, bytes_accessed=12 * 10**6, transcendentals=0),
    )(*ins)


def pieces_out(halves, order, high, first, wide, out, whole, sems):
    made = []
    for place in range(PIECES):
        ref, at = halves[place // 8], place % 8
        rows = pl.ds(pl.multiple_of(piece_at(place, order) * high, high), high)
        for c in range(wide // WIN):
            start = first + c * high
            whole[rows, c * WIN : (c + 1) * WIN] = ref[at, start : start + high, :].astype(F32)
        made.append(pltpu.make_async_copy(whole.at[rows, :], out.at[0, rows, :], sems.at[place]))
        made[-1].start()
    return made


def unpack_in(a0, a1, fin, v_fin, sems):
    for c in pieces_out((a0, a1), OUT_A, 32, 0, FF, fin, v_fin, sems.at[0]):
        c.wait()


def unpack_out(b0, b1, fout, v_fout, sems):
    for c in pieces_out((b0, b1), OUT_B, 128, 0, D, fout, v_fout, sems.at[0]):
        c.wait()


def unpack_qkv(q0, q1, qkv, v_qkv, sems):
    for c in pieces_out((q0, q1), OUT_Q, 32, 0, 3 * D, qkv, v_qkv, sems.at[0]):
        c.wait()


def unpack_rest(c0, c1, so, cross, b_in, b_out, gain, bias, cgain, cbias, v_so, v_cross, sems):
    made = pieces_out((c0, c1), OUT_C, 32, 0, D, so, v_so, sems.at[0])
    made += pieces_out((c0, c1), OUT_C, 32, 4 * 32, 2 * D, cross, v_cross, sems.at[1])

    def line(p):
        place = place_of(p, OUT_C)
        at = place % 8
        tail = jnp.where(place < 8, c0[at, ROWS_C - 16 :, :].astype(F32), c1[at, ROWS_C - 16 :, :].astype(F32))
        return jnp.concatenate([tail[j : j + 1, :] for j in range(4)], 1)

    for n in range(4):
        b_in[:, n * D : (n + 1) * D] = line(n)
    b_out[...] = line(4)
    for n in range(2):
        gain[0, n : n + 1, :] = line(5 + n)
        bias[0, n : n + 1, :] = line(7 + n)
    cgain[...] = line(9)
    cbias[...] = line(10)
    for c in made:
        c.wait()


def body(
    token_rows, lengths, self_qkv, self_out, ffn_in, ffn_in_bias, ffn_out, ffn_out_bias, norm_gain, norm_bias,
    cross_weights, cross_gain, cross_bias, output_grad,
):
    to_decoder, to_encoder = [(0, 1)], [(1, 0)]
    w = at_hand(
        types.SimpleNamespace(
            tok=token_rows, lens=lengths, w_qkv=self_qkv, w_so=self_out, w_fin=ffn_in, b_in=ffn_in_bias, w_fout=ffn_out,
            b_out=ffn_out_bias, gain=norm_gain, bias=norm_bias, w_cross=cross_weights, cgain=cross_gain.reshape(1, D),
            cbias=cross_bias.reshape(1, D), og=output_grad,
        )
    )
    w_c0 = lax.ppermute(cross_weights, "section", to_decoder)
    one = first_phase(w)
    mem = lax.ppermute(one.mem, "section", to_decoder)
    two = middle_phase(w, one, mem, w_c0)
    gmem = lax.ppermute(two.gmem, "section", to_encoder)
    gkv = lax.ppermute(two.gkv, "section", to_encoder)
    three = third_phase(w, one, two, gmem)
    four = fourth_phase(w, one, two, three, gkv)
    a = Chain(three.a_keep, three.a_send, SUM_A, OUT_A)
    b = Chain(three.b_keep, three.b_send, SUM_B, OUT_B)
    advance([a, b])
    c = Chain(four.c_keep, four.c_send, SUM_C, OUT_C)
    five = fifth_phase(w, one, two, three, four, (a.send, b.send))
    (q_send,) = advance([a, b, c], five.q_send)
    q = Chain(five.q_keep, q_send, SUM_Q, OUT_Q)
    for chain in (q, c, a, b):
        chain.run()
    (g_qkv,) = unpack(unpack_qkv, q.result, [(D, 3 * D)], [((1, D, 3 * D), True)])
    (g_fin,) = unpack(unpack_in, a.result, [(D, FF)], [((1, D, FF), True)])
    (g_fout,) = unpack(unpack_out, b.result, [(FF, D)], [((1, FF, D), True)])
    small = [(1, FF), (1, D), (1, 2, D), (1, 2, D), (1, D), (1, D)]
    g_so, g_cross, g_bin, g_bout, g_gain, g_bias, g_cgain, g_cbias = unpack(
        unpack_rest,
        c.result,
        [(D, D), (D, 2 * D)],
        [((1, D, D), True), ((1, D, 2 * D), True)] + [(shape, False) for shape in small],
    )
    return (
        four.layer, five.rows, g_qkv, g_so, g_fin, g_bin, g_fout, g_bout, g_gain, g_bias, g_cross, g_cgain.reshape(D),
        g_cbias.reshape(D),
    )


def solution(mesh):
    by_section = P("section")
    in_specs = (
        P("section", "dp"), P("dp"), by_section, by_section, by_section, by_section, by_section, by_section, by_section,
        by_section, by_section, P(), P(), P("dp"),
    )
    out_specs = (P("section", "dp"), P("section", "dp")) + (by_section,) * 9 + (P(), P())
    return jax.shard_map(body, mesh=mesh, in_specs=in_specs, out_specs=out_specs, check_vma=False)
```
